256 devices in a mesh: dp: 16 (over z, core), tensor: 16 (over y, x).
Axes of the slice: x: 4, y: 4, z: 8, core: 2. Of those that a mesh axis runs over, the one named last changes fastest.
Arguments:
- hidden_in: bfloat16 [16384, 896], P('dp', 'tensor'), may hold values from -6 to 6
- out_grad: bfloat16 [16384, 896], P('dp', 'tensor'), may hold values from -6 to 6
- w_gate: bfloat16 [4096, 896], P('tensor'), may hold values from -0.1875 to 0.1875
- w_up: bfloat16 [4096, 896], P('tensor'), may hold values from -0.1875 to 0.1875
- w_down: bfloat16 [4096, 896], P('tensor'), may hold values from -0.1875 to 0.1875
- error_in: bfloat16 [16, 3, 4096, 896], P('dp', None, 'tensor'), may hold values from -96 to 96
- q_init: float32 [3, 32, 896], P(None, None, 'tensor'), may hold values from -6 to 6
Outputs:
- input_grad: bfloat16 [16384, 896], P('dp', 'tensor')
- error_out: bfloat16 [16, 3, 4096, 896], P('dp', None, 'tensor')
- q_out: float32 [3, 32, 896], P(None, None, 'tensor')
The draws below stay inside these ranges and needn't reach their ends.
All inputs are finite; a program needn't handle non-finite values.
Results may differ from the reference program's by a relative error of at most 0.017.
Values may be sent and summed in bfloat16 or wider, within the bound.
No kernel may reach another device: no remote copies, remote signals or barrier semaphores. Data moves between devices by JAX's collectives and lax.ppermute only.
A program may use at most 128 MiB of HBM per device.

```python
import jax
import jax.numpy as jnp
from jax import lax

D = 896
FF = 4096
TOK_DEV = 1024
R = 32
HID_DEV = 256
TOKENS = 16384
WORKERS = 16
N_DP = 16
N_TENSOR = 16


def block_scale(own_key, extent, shards, least, largest):
    loudness = 1.0
    for position, blocks in shards:
        steps = jax.random.uniform(jax.random.fold_in(jax.random.fold_in(own_key, 6), position), (blocks,), jnp.float32, least / len(shards), largest / len(shards))
        loudness = loudness * jnp.repeat(jnp.exp(steps), extent[position] // blocks).reshape((-1,) + (1,) * (len(extent) - 1 - position))
    return loudness


def normal_values(key, extent, scale, limit, pieces=(), kind=jnp.bfloat16):
    array = jax.random.normal(key, extent, jnp.float32) * scale
    if len(pieces) > 0:
        array = block_scale(key, extent, pieces, -0.22, 0.18) * array
    return jnp.clip(array, min=-limit, max=limit).astype(kind)


def setup_inputs(seed: int = 0) -> dict:
    streams_of = jax.random.split(jax.random.key(seed), 8)
    hidden_in = normal_values(streams_of[0], (TOKENS, D), 1.0, 6.0, ((0, 16), (1, 16)))
    out_grad = normal_values(streams_of[1], (TOKENS, D), 1.0, 6.0, ((0, 16), (1, 16)))
    w_gate = normal_values(streams_of[2], (FF, D), D ** -0.5, 0.1875, ((0, 16),))
    w_up = normal_values(streams_of[3], (FF, D), D ** -0.5, 0.1875, ((0, 16),))
    w_down = normal_values(streams_of[4], (FF, D), D ** -0.5, 0.1875, ((0, 16),))
    error_in = normal_values(streams_of[5], (WORKERS, 3, FF, D), 16.0, 96.0, ((0, 16), (2, 16)))
    q_init = normal_values(streams_of[6], (3, R, D), 1.0, 6.0, ((2, 16),), jnp.float32)
    return {"hidden_in": hidden_in, "out_grad": out_grad, "w_gate": w_gate, "w_up": w_up, "w_down": w_down, "error_in": error_in, "q_init": q_init}


def worker_grads(inputs):
    x_rows, dy_rows, w_gate, w_up, w_down, err_rows = inputs
    gate_pre = jnp.dot(x_rows.astype(jnp.float32), w_gate.T.astype(jnp.float32), preferred_element_type=jnp.float32)
    up_pre = jnp.dot(x_rows.astype(jnp.float32), w_up.T.astype(jnp.float32), preferred_element_type=jnp.float32)
    gate_sig = jax.nn.sigmoid(gate_pre)
    gate_act = gate_pre * gate_sig
    hidden = (gate_act * up_pre).astype(jnp.bfloat16)
    hidden_grad = jnp.dot(dy_rows.astype(jnp.float32), w_down.T.astype(jnp.float32), preferred_element_type=jnp.float32)
    gate_grad = (hidden_grad * up_pre * gate_sig * (1.0 + gate_pre * (1.0 - gate_sig))).astype(jnp.bfloat16)
    up_grad = (hidden_grad * gate_act).astype(jnp.bfloat16)
    rows = x_rows.shape[0]
    blocks = jnp.einsum('tnh,nhd->ntd', gate_grad.reshape(rows, N_TENSOR, HID_DEV).astype(jnp.float32), w_gate.reshape(N_TENSOR, HID_DEV, D).astype(jnp.float32))
    blocks = blocks + jnp.einsum('tnh,nhd->ntd', up_grad.reshape(rows, N_TENSOR, HID_DEV).astype(jnp.float32), w_up.reshape(N_TENSOR, HID_DEV, D).astype(jnp.float32))
    rounded = lax.optimization_barrier(blocks.astype(jnp.bfloat16))
    input_grad = jnp.sum(rounded.astype(jnp.float32), axis=0).astype(jnp.bfloat16)
    grad_gate = jnp.dot(gate_grad.T.astype(jnp.float32), x_rows.astype(jnp.float32), preferred_element_type=jnp.float32)
    grad_up = jnp.dot(up_grad.T.astype(jnp.float32), x_rows.astype(jnp.float32), preferred_element_type=jnp.float32)
    grad_down = jnp.dot(hidden.T.astype(jnp.float32), dy_rows.astype(jnp.float32), preferred_element_type=jnp.float32)
    matrices = jnp.stack([grad_gate, grad_up, grad_down]) + err_rows.astype(jnp.float32)
    return (input_grad, matrices)

def ortho_one(chol_factor, p_trans):
    return lax.linalg.triangular_solve(chol_factor, p_trans, left_side=True, lower=True)

def reference(hidden_in, out_grad, w_gate, w_up, w_down, error_in, q_init):
    x_all = hidden_in.reshape(N_DP, TOK_DEV, D)
    dy_all = out_grad.reshape(N_DP, TOK_DEV, D)

    def one_worker(inputs):
        return worker_grads((inputs[0], inputs[1], w_gate, w_up, w_down, inputs[2]))
    input_grad, matrices = lax.map(one_worker, (x_all, dy_all, error_in))
    highest = lax.Precision.HIGHEST
    p_factor = jnp.einsum('wkfd,krd->kfr', matrices, q_init, precision=highest) / N_DP
    gram_matrix = jnp.einsum('kfr,kfs->krs', p_factor, p_factor, precision=highest)
    chol_factor = jnp.linalg.cholesky(gram_matrix)
    p_ortho = jax.vmap(ortho_one)(chol_factor, jnp.swapaxes(p_factor, 1, 2))
    q_out = jnp.einsum('krf,wkfd->krd', p_ortho, matrices, precision=highest) / N_DP
    approx = jnp.einsum('krf,krd->kfd', p_ortho, q_out, precision=highest)
    error_out = (matrices - approx[None]).astype(jnp.bfloat16)
    return (input_grad.reshape(TOKENS, D), error_out, q_out)
```

```python
import jax
import jax.numpy as jnp
from jax import lax
from jax.experimental import pallas as pl
from jax.experimental.pallas import tpu as pltpu
from jax.sharding import PartitionSpec as P

BF = jnp.bfloat16
F32 = jnp.float32
HIGHEST = lax.Precision.HIGHEST
SIDE = 4
DEPTH = 8


def x_ring(k):
    return [(y * SIDE + x, y * SIDE + (x + k) % SIDE) for y in range(SIDE) for x in range(SIDE)]


def y_ring(k):
    return [(y * SIDE + x, ((y + k) % SIDE) * SIDE + x) for y in range(SIDE) for x in range(SIDE)]


CORE_PAIR = [(i, i ^ 1) for i in range(2 * DEPTH)]
Z_GROUPS = [[z * 2 + c for z in range(DEPTH)] for c in range(2)]


def gather_pair(a, b, x, y):
    a_near = [a] + [None] * 3
    b_near = [b] + [None] * 3
    for k in (1, 3, 2):
        a_near[k] = lax.ppermute(a, "tensor", x_ring(k))
        b_near[k] = lax.ppermute(b, "tensor", y_ring(k))
    a_row = jnp.stack([lax.dynamic_index_in_dim(jnp.stack(a_near), (x - i) % SIDE, 0, False) for i in range(SIDE)])
    b_row = jnp.stack([lax.dynamic_index_in_dim(jnp.stack(b_near), (y - i) % SIDE, 0, False) for i in range(SIDE)])
    a_far = [a_row] + [None] * 3
    b_far = [b_row] + [None] * 3
    for k in (1, 3, 2):
        a_far[k] = lax.ppermute(a_row, "tensor", y_ring(k))
        b_far[k] = lax.ppermute(b_row, "tensor", x_ring(k))
    a_all = jnp.stack([lax.dynamic_index_in_dim(jnp.stack(a_far), (y - i) % SIDE, 0, False) for i in range(SIDE)])
    b_all = jnp.stack(
        [lax.dynamic_index_in_dim(jnp.stack(b_far), (x - i) % SIDE, 0, False) for i in range(SIDE)], axis=1
    )
    rows = a.shape[0] * SIDE * SIDE
    return a_all.reshape(rows, -1), b_all.reshape(rows, -1)


def chol_inverse_kernel(gram_ref, out_ref):
    n = gram_ref.shape[-1]
    gram = gram_ref[...]
    rows = lax.broadcasted_iota(jnp.int32, (1, n, n), 1)
    cols = lax.broadcasted_iota(jnp.int32, (1, n, n), 2)
    eye = jnp.broadcast_to(jnp.where(rows == cols, 1.0, 0.0), gram.shape)
    work = jnp.concatenate([gram, eye], axis=2)
    below = lax.broadcasted_iota(jnp.int32, (1, n, 1), 1)
    for k in range(n):
        pivot = work[:, k : k + 1, :]
        scale = 1.0 / pivot[:, :, k : k + 1]
        factor = jnp.where(below > k, work[:, :, k : k + 1] * scale, 0.0)
        work = work - factor * pivot
    diag = jnp.sum(jnp.where(rows == cols, work[:, :, :n], 0.0), axis=2, keepdims=True)
    out_ref[...] = work[:, :, n:] * lax.rsqrt(diag)


def chol_inverse(gram):
    return pl.pallas_call(
        chol_inverse_kernel,
        out_shape=jax.ShapeDtypeStruct(gram.shape, F32),
        in_specs=[pl.BlockSpec(memory_space=pltpu.VMEM)],
        out_specs=pl.BlockSpec(memory_space=pltpu.VMEM),
    )(gram)


def dot(a, b, ca, cb, precision=None):
    return lax.dot_general(a, b, (((ca,), (cb,)), ((), ())), precision=precision, preferred_element_type=F32)


def sum_pair(value):
    return value + lax.ppermute(value, "dp", CORE_PAIR)


def join_halves(half, core):
    other = lax.ppermute(half, "dp", CORE_PAIR)
    return jnp.where(core == 0, jnp.concatenate([half, other]), jnp.concatenate([other, half]))


def sum_z(value):
    spread = jnp.broadcast_to(value[None], (DEPTH,) + value.shape)
    return jnp.sum(
        lax.all_to_all(spread, "dp", 0, 0, tiled=True, axis_index_groups=Z_GROUPS).astype(F32), axis=0
    )


def per_device(hidden_in, out_grad, w_gate, w_up, w_down, error_in, q_init):
    n_workers = lax.axis_size("dp")
    n_tensor = lax.axis_size("tensor")
    me = lax.axis_index("tensor")
    y, x = me // SIDE, me % SIDE
    core = lax.axis_index("dp") % 2
    rank = q_init.shape[1]
    shard = hidden_in.shape[1]
    width = shard * n_tensor
    n_rows = 3 * rank
    half_rows = n_rows // 2

    x_all, dy_all = gather_pair(hidden_in.T, out_grad.T, x, y)
    q_cols = q_init.reshape(n_rows, shard).T
    q_all = lax.all_to_all(
        jnp.broadcast_to(q_cols[None], (n_tensor,) + q_cols.shape), "tensor", 0, 0, tiled=True
    ).reshape(width, n_rows)

    gate_pre = dot(w_gate, x_all, 1, 0)
    up_pre = dot(w_up, x_all, 1, 0)
    gate_sig = jax.nn.sigmoid(gate_pre)
    gate_act = gate_pre * gate_sig
    hidden = (gate_act * up_pre).astype(BF)
    hidden_grad = dot(w_down, dy_all, 1, 0)
    gate_grad = (hidden_grad * up_pre * gate_sig * (1.0 + gate_pre * (1.0 - gate_sig))).astype(BF)
    up_grad = (hidden_grad * gate_act).astype(BF)
    term = (dot(w_gate, gate_grad, 0, 0) + dot(w_up, up_grad, 0, 0)).astype(BF)
    input_grad = lax.psum_scatter(term, "tensor", scatter_dimension=0, tiled=True).T

    matrices = [dot(gate_grad, x_all, 1, 1), dot(up_grad, x_all, 1, 1), dot(hidden, dy_all, 1, 1)]
    matrices = [m + error_in[0, k].astype(F32) for k, m in enumerate(matrices)]

    p_local = jnp.concatenate(
        [dot(q_all[:, k * rank : (k + 1) * rank], m, 0, 1, HIGHEST) for k, m in enumerate(matrices)]
    )
    p_pair = sum_pair(p_local.astype(BF).astype(F32))
    p_half = lax.dynamic_slice_in_dim(p_pair, core * half_rows, half_rows, 0)
    p_trans = join_halves(sum_z(p_half.astype(BF)), core) / n_workers

    s_rows = []
    for k, m in enumerate(matrices):
        p_k = p_trans[k * rank : (k + 1) * rank]
        s_rows.append(
            jnp.concatenate(
                [dot(p_k, m, 1, 0, HIGHEST), dot(p_k, p_k, 1, 1, HIGHEST), jnp.zeros((rank, 96), F32)], axis=1
            )
        )
    s_local = jnp.concatenate(s_rows)
    s_pair = lax.dynamic_slice_in_dim(s_local, core * half_rows, half_rows, 0) + lax.ppermute(
        lax.dynamic_slice_in_dim(s_local, (1 - core) * half_rows, half_rows, 0), "dp", CORE_PAIR
    )
    s_split = s_pair.reshape(n_tensor, -1, 128)
    s_mine = jnp.sum(lax.all_to_all(s_split, "tensor", 0, 0, tiled=True), axis=0)
    s_mine = sum_z(s_mine)
    s_half = lax.all_to_all(
        jnp.broadcast_to(s_mine[None], (n_tensor,) + s_mine.shape), "tensor", 0, 0, tiled=True
    ).reshape(s_pair.shape)
    s_all = join_halves(s_half, core).reshape(3, rank, -1) / n_workers

    inverse = chol_inverse(s_all[:, :, width : width + rank])
    q_new = jnp.einsum("krs,ksd->krd", inverse, s_all[:, :, :width], precision=HIGHEST)
    p_ortho = jnp.einsum("krs,ksh->krh", inverse, p_trans.reshape(3, rank, -1), precision=HIGHEST)
    error_out = jnp.stack([m - dot(p_ortho[k], q_new[k], 0, 0, HIGHEST) for k, m in enumerate(matrices)])
    q_out = lax.dynamic_slice_in_dim(q_new, me * shard, shard, 2)
    return (input_grad, error_out[None].astype(BF), q_out)


def solution(mesh):
    in_specs = (
        P("dp", "tensor"),
        P("dp", "tensor"),
        P("tensor", None),
        P("tensor", None),
        P("tensor", None),
        P("dp", None, "tensor", None),
        P(None, None, "tensor"),
    )
    out_specs = (P("dp", "tensor"), P("dp", None, "tensor", None), P(None, None, "tensor"))
    return jax.shard_map(
        per_device, mesh=mesh, in_specs=in_specs, out_specs=out_specs, check_vma=False
    )
```

```python
import jax
import jax.numpy as jnp
from jax import lax
from jax.experimental import pallas as pl
from jax.experimental.pallas import tpu as pltpu
from jax.sharding import PartitionSpec as P

BF = jnp.bfloat16
F32 = jnp.float32
HIGHEST = lax.Precision.HIGHEST
SIDE = 4
DEPTH = 8


def x_ring(k):
    return [(y * SIDE + x, y * SIDE + (x + k) % SIDE) for y in range(SIDE) for x in range(SIDE)]


def y_ring(k):
    return [(y * SIDE + x, ((y + k) % SIDE) * SIDE + x) for y in range(SIDE) for x in range(SIDE)]


CORE_PAIR = [(i, i ^ 1) for i in range(2 * DEPTH)]
Z_GROUPS = [[z * 2 + c for z in range(DEPTH)] for c in range(2)]


def gather_pair(a, b, x, y):
    a_near = [a] + [None] * 3
    b_near = [b] + [None] * 3
    for k in (1, 3, 2):
        a_near[k] = lax.ppermute(a, "tensor", x_ring(k))
        b_near[k] = lax.ppermute(b, "tensor", y_ring(k))
    a_near, b_near = lax.optimization_barrier((a_near, b_near))
    a_row = jnp.stack([lax.dynamic_index_in_dim(jnp.stack(a_near), (x - i) % SIDE, 0, False) for i in range(SIDE)])
    b_row = jnp.stack([lax.dynamic_index_in_dim(jnp.stack(b_near), (y - i) % SIDE, 0, False) for i in range(SIDE)])
    a_row, b_row = lax.optimization_barrier((a_row, b_row))
    a_far = [a_row] + [None] * 3
    b_far = [b_row] + [None] * 3
    for k in (1, 3, 2):
        a_far[k] = lax.ppermute(a_row, "tensor", y_ring(k))
        b_far[k] = lax.ppermute(b_row, "tensor", x_ring(k))
    a_all = jnp.stack([lax.dynamic_index_in_dim(jnp.stack(a_far), (y - i) % SIDE, 0, False) for i in range(SIDE)])
    b_all = jnp.stack(
        [lax.dynamic_index_in_dim(jnp.stack(b_far), (x - i) % SIDE, 0, False) for i in range(SIDE)], axis=1
    )
    rows = a.shape[0] * SIDE * SIDE
    return a_all.reshape(rows, -1), b_all.reshape(rows, -1)


def scatter_sum(value, x, y):
    rows, cols = value.shape
    blocks = value.reshape(SIDE, SIDE, rows // (SIDE * SIDE), cols)
    a, b = blocks[..., : cols // 2], blocks[..., cols // 2 :]

    def part(array, index, axis):
        return lax.dynamic_index_in_dim(array, index % SIDE, axis, False)

    a_got = [part(a, y, 0)] + [lax.ppermute(part(a, y + k, 0), "tensor", y_ring(k)) for k in (1, 3, 2)]
    b_got = [part(b, x, 1)] + [lax.ppermute(part(b, x + k, 1), "tensor", x_ring(k)) for k in (1, 3, 2)]
    a_got, b_got = lax.optimization_barrier((a_got, b_got))
    a_sum = sum(v.astype(F32) for v in a_got).astype(value.dtype)
    b_sum = sum(v.astype(F32) for v in b_got).astype(value.dtype)
    a_sum, b_sum = lax.optimization_barrier((a_sum, b_sum))
    a_got = [part(a_sum, x, 0)] + [lax.ppermute(part(a_sum, x + k, 0), "tensor", x_ring(k)) for k in (1, 3, 2)]
    b_got = [part(b_sum, y, 0)] + [lax.ppermute(part(b_sum, y + k, 0), "tensor", y_ring(k)) for k in (1, 3, 2)]
    a_out = sum(v.astype(F32) for v in a_got)
    b_out = sum(v.astype(F32) for v in b_got)
    return jnp.concatenate([a_out, b_out], axis=1).astype(value.dtype)


def chol_inverse_kernel(gram_ref, out_ref):
    n = gram_ref.shape[-1]
    gram = gram_ref[...]
    rows = lax.broadcasted_iota(jnp.int32, (1, n, n), 1)
    cols = lax.broadcasted_iota(jnp.int32, (1, n, n), 2)
    eye = jnp.broadcast_to(jnp.where(rows == cols, 1.0, 0.0), gram.shape)
    work = jnp.concatenate([gram, eye], axis=2)
    below = lax.broadcasted_iota(jnp.int32, (1, n, 1), 1)
    for k in range(n):
        pivot = work[:, k : k + 1, :]
        scale = 1.0 / pivot[:, :, k : k + 1]
        factor = jnp.where(below > k, work[:, :, k : k + 1] * scale, 0.0)
        work = work - factor * pivot
    diag = jnp.sum(jnp.where(rows == cols, work[:, :, :n], 0.0), axis=2, keepdims=True)
    out_ref[...] = work[:, :, n:] * lax.rsqrt(diag)


def chol_inverse(gram):
    return pl.pallas_call(
        chol_inverse_kernel,
        out_shape=jax.ShapeDtypeStruct(gram.shape, F32),
        in_specs=[pl.BlockSpec(memory_space=pltpu.VMEM)],
        out_specs=pl.BlockSpec(memory_space=pltpu.VMEM),
    )(gram)


def dot(a, b, ca, cb, precision=None):
    return lax.dot_general(a, b, (((ca,), (cb,)), ((), ())), precision=precision, preferred_element_type=F32)


def sum_pair(value):
    return value + lax.ppermute(value, "dp", CORE_PAIR)


def join_halves(half, core):
    other = lax.ppermute(half, "dp", CORE_PAIR)
    return jnp.where(core == 0, jnp.concatenate([half, other]), jnp.concatenate([other, half]))


def sum_z(value):
    spread = jnp.broadcast_to(value[None], (DEPTH,) + value.shape)
    return jnp.sum(
        lax.all_to_all(spread, "dp", 0, 0, tiled=True, axis_index_groups=Z_GROUPS).astype(F32), axis=0
    )


def per_device(hidden_in, out_grad, w_gate, w_up, w_down, error_in, q_init):
    n_workers = lax.axis_size("dp")
    n_tensor = lax.axis_size("tensor")
    me = lax.axis_index("tensor")
    y, x = me // SIDE, me % SIDE
    core = lax.axis_index("dp") % 2
    rank = q_init.shape[1]
    shard = hidden_in.shape[1]
    width = shard * n_tensor
    n_rows = 3 * rank
    half_rows = n_rows // 2

    x_all, dy_all = gather_pair(hidden_in.T, out_grad.T, x, y)
    q_cols = q_init.reshape(n_rows, shard).T
    q_all = lax.all_to_all(
        jnp.broadcast_to(q_cols[None], (n_tensor,) + q_cols.shape), "tensor", 0, 0, tiled=True
    ).reshape(width, n_rows)

    gate_pre = dot(w_gate, x_all, 1, 0)
    up_pre = dot(w_up, x_all, 1, 0)
    gate_sig = jax.nn.sigmoid(gate_pre)
    gate_act = gate_pre * gate_sig
    hidden = (gate_act * up_pre).astype(BF)
    hidden_grad = dot(w_down, dy_all, 1, 0)
    gate_grad = (hidden_grad * up_pre * gate_sig * (1.0 + gate_pre * (1.0 - gate_sig))).astype(BF)
    up_grad = (hidden_grad * gate_act).astype(BF)
    term = (dot(w_gate, gate_grad, 0, 0) + dot(w_up, up_grad, 0, 0)).astype(BF)
    input_grad = scatter_sum(term, x, y).T

    matrices = [dot(gate_grad, x_all, 1, 1), dot(up_grad, x_all, 1, 1), dot(hidden, dy_all, 1, 1)]
    matrices = [m + error_in[0, k].astype(F32) for k, m in enumerate(matrices)]

    p_local = jnp.concatenate(
        [dot(q_all[:, k * rank : (k + 1) * rank], m, 0, 1, HIGHEST) for k, m in enumerate(matrices)]
    )
    p_pair = sum_pair(p_local.astype(BF).astype(F32))
    p_half = lax.dynamic_slice_in_dim(p_pair, core * half_rows, half_rows, 0)
    p_trans = join_halves(sum_z(p_half.astype(BF)), core) / n_workers

    s_rows = []
    for k, m in enumerate(matrices):
        p_k = p_trans[k * rank : (k + 1) * rank]
        s_rows.append(
            jnp.concatenate(
                [dot(p_k, m, 1, 0, HIGHEST), dot(p_k, p_k, 1, 1, HIGHEST), jnp.zeros((rank, 96), F32)], axis=1
            )
        )
    s_local = jnp.concatenate(s_rows)
    s_pair = lax.dynamic_slice_in_dim(s_local, core * half_rows, half_rows, 0) + lax.ppermute(
        lax.dynamic_slice_in_dim(s_local, (1 - core) * half_rows, half_rows, 0), "dp", CORE_PAIR
    )
    s_split = s_pair.reshape(n_tensor, -1, 128)
    s_mine = jnp.sum(lax.all_to_all(s_split, "tensor", 0, 0, tiled=True), axis=0)
    s_mine = sum_z(s_mine)
    s_half = lax.all_to_all(
        jnp.broadcast_to(s_mine[None], (n_tensor,) + s_mine.shape), "tensor", 0, 0, tiled=True
    ).reshape(s_pair.shape)
    s_all = join_halves(s_half, core).reshape(3, rank, -1) / n_workers

    inverse = chol_inverse(s_all[:, :, width : width + rank])
    q_new = jnp.einsum("krs,ksd->krd", inverse, s_all[:, :, :width], precision=HIGHEST)
    p_ortho = jnp.einsum("krs,ksh->krh", inverse, p_trans.reshape(3, rank, -1), precision=HIGHEST)
    error_out = jnp.stack([m - dot(p_ortho[k], q_new[k], 0, 0, HIGHEST) for k, m in enumerate(matrices)])
    q_out = lax.dynamic_slice_in_dim(q_new, me * shard, shard, 2)
    return (input_grad, error_out[None].astype(BF), q_out)


def solution(mesh):
    in_specs = (
        P("dp", "tensor"),
        P("dp", "tensor"),
        P("tensor", None),
        P("tensor", None),
        P("tensor", None),
        P("dp", None, "tensor", None),
        P(None, None, "tensor"),
    )
    out_specs = (P("dp", "tensor"), P("dp", None, "tensor", None), P(None, None, "tensor"))
    return jax.shard_map(
        per_device, mesh=mesh, in_specs=in_specs, out_specs=out_specs, check_vma=False
    )
```

```python
import jax
import jax.numpy as jnp
from jax import lax
from jax.experimental import pallas as pl
from jax.experimental.pallas import tpu as pltpu
from jax.sharding import PartitionSpec as P

BF = jnp.bfloat16
F32 = jnp.float32
SIDE = 4
DEPTH = 8
RANK = 32
ROWS = 3 * RANK
HALF = ROWS // 2
LANES = 128
TILES = HALF * 1024 // (8 * LANES)
MIB = 1 << 20

X_GROUPS = [[y * SIDE + x for x in range(SIDE)] for y in range(SIDE)]
Y_GROUPS = [[y * SIDE + x for y in range(SIDE)] for x in range(SIDE)]
CORE_PAIR = [(i, i ^ 1) for i in range(2 * DEPTH)]
Z_GROUPS = [[z * 2 + c for z in range(DEPTH)] for c in range(2)]


def x_ring(k):
    return [(y * SIDE + x, y * SIDE + (x + k) % SIDE) for y in range(SIDE) for x in range(SIDE)]


def y_ring(k):
    return [(y * SIDE + x, ((y + k) % SIDE) * SIDE + x) for y in range(SIDE) for x in range(SIDE)]


def spread(value, axis, groups, size):
    return lax.all_to_all(
        jnp.broadcast_to(value[None], (size,) + value.shape), axis, 0, 0, tiled=True, axis_index_groups=groups
    )


def ring_pieces(value, ring):
    near = [value] + [None] * 3
    for k in (1, 3, 2):
        near[k] = lax.ppermute(value, "tensor", ring(k))
    return near


def order_kernel(place_ref, *refs):
    for pieces, out_ref in ((refs[:SIDE], refs[-2]), (refs[SIDE:-2], refs[-1])):
        for i, ref in enumerate(pieces):
            out_ref[lax.rem(place_ref[0] - i + SIDE, SIDE)] = ref[...]


def order(position, a_pieces, b_pieces):
    vmem = pl.BlockSpec(memory_space=pltpu.VMEM)
    out_shape = tuple(jax.ShapeDtypeStruct((SIDE,) + p[0].shape, p[0].dtype) for p in (a_pieces, b_pieces))
    return pl.pallas_call(
        order_kernel,
        out_shape=out_shape,
        in_specs=[pl.BlockSpec(memory_space=pltpu.SMEM)] + [vmem] * (2 * SIDE),
        out_specs=(vmem, vmem),
    )(position.reshape(1), *a_pieces, *b_pieces)


def gather_all(x_part, dy_part, q_part, me):
    rows = SIDE * x_part.shape[0]
    dy_col = spread(dy_part, "tensor", Y_GROUPS, SIDE)
    near, q_near, dy_col = lax.optimization_barrier(
        (ring_pieces(x_part, x_ring), ring_pieces(q_part, x_ring), dy_col)
    )
    x_row, q_row = order(me % SIDE, near, q_near)
    x_row, q_row, dy_col = lax.optimization_barrier((x_row, q_row, dy_col))
    dy_all = spread(dy_col, "tensor", X_GROUPS, SIDE)
    far, q_far = lax.optimization_barrier((ring_pieces(x_row, y_ring), ring_pieces(q_row, y_ring)))
    return [p.reshape(rows, -1) for p in far], [p.reshape(rows, -1) for p in q_far], dy_all


def swap_order(value):
    blocks = value.reshape((SIDE, SIDE, -1) + value.shape[1:])
    return jnp.swapaxes(blocks, 0, 1).reshape(value.shape)


def scatter_sum(blocks, x):
    got = [blocks[0]] + [lax.ppermute(blocks[k], "tensor", y_ring(k)) for k in (1, 3, 2)]
    got = lax.optimization_barrier(got)
    total = sum(v.astype(F32) for v in got).astype(blocks[0].dtype)
    total = lax.optimization_barrier(total).reshape(SIDE, -1, total.shape[1])

    def part(k):
        return lax.dynamic_index_in_dim(total, (x + k) % SIDE, 0, False)

    got = [part(0)] + [lax.ppermute(part(k), "tensor", x_ring(k)) for k in (1, 3, 2)]
    return sum(v.astype(F32) for v in got).astype(total.dtype)


def split(value):
    high = value.astype(BF)
    return high, (value - high.astype(F32)).astype(BF)


def dot(a, b, ca, cb):
    return lax.dot_general(a, b, (((ca,), (cb,)), ((), ())), preferred_element_type=F32)


def dot3(a, b, ca, cb):
    a_high, a_low = split(a)
    b_high, b_low = split(b)
    return dot(
        jnp.concatenate([a_high, a_high, a_low], axis=ca), jnp.concatenate([b_high, b_low, b_high], axis=cb), ca, cb
    )


def own_half(core, value):
    low, high = value[:HALF], value[HALF:]
    first = core == 0
    return jnp.where(first, low, high), jnp.where(first, high, low)


def whole(core, mine, other):
    first = core == 0
    return jnp.concatenate([jnp.where(first, mine, other), jnp.where(first, other, mine)])


def factors_kernel(place_ref, q0_ref, q1_ref, q2_ref, q3_ref, err_ref, q_both_ref, p_ref, q_ref):
    rows = q0_ref.shape[0]
    for i, ref in enumerate((q0_ref, q1_ref, q2_ref, q3_ref)):
        at = pl.multiple_of(lax.rem(place_ref[0] - i + SIDE, SIDE) * rows, 8)
        q_ref[pl.ds(at, rows), :] = ref[...]
    block = rows // SIDE
    swapped = [
        q_ref[(y * SIDE + x) * block : (y * SIDE + x + 1) * block, 2 * RANK :]
        for x in range(SIDE)
        for y in range(SIDE)
    ]
    q_rows = q_ref[...].T
    for k in range(3):
        q_both = jnp.concatenate(split(q_rows[k * RANK : (k + 1) * RANK]))
        both = dot(q_both, err_ref[0, k], 1, 1)
        p_ref[pl.ds(k * RANK, RANK), :] = both[:RANK] + both[RANK:]
        q_both_ref[k] = q_both if k < 2 else jnp.concatenate(split(jnp.concatenate(swapped).T))


def factors(place, pieces, error_in):
    vmem = pl.BlockSpec(memory_space=pltpu.VMEM)
    hid, width = error_in.shape[2:]
    return pl.pallas_call(
        factors_kernel,
        out_shape=(jax.ShapeDtypeStruct((3, 2 * RANK, width), BF), jax.ShapeDtypeStruct((ROWS, hid), F32)),
        in_specs=[pl.BlockSpec(memory_space=pltpu.SMEM)] + [vmem] * 5,
        out_specs=(vmem, vmem),
        scratch_shapes=[pltpu.VMEM((width, ROWS), F32)],
    )(place, *pieces, error_in)


def backward_kernel(place_ref, p0_ref, p1_ref, p2_ref, p3_ref, dy_hbm, gate_hbm, up_hbm, down_hbm, q_ref, p_err_ref,
                    gate_grad_ref, up_grad_ref, hidden_ref, mine_ref, theirs_ref, x_ref,
                    dy_ref, gate_ref, up_ref, down_ref, sems):
    rows = p0_ref.shape[0]
    copies = [pltpu.make_async_copy(gate_hbm, gate_ref, sems.at[0])]
    for i, ref in enumerate((p0_ref, p1_ref, p2_ref, p3_ref)):
        at = pl.multiple_of(lax.rem(place_ref[0] - i + SIDE, SIDE) * rows, 16)
        copies.append(pltpu.make_async_copy(ref, x_ref.at[pl.ds(at, rows), :], sems.at[1 + i]))
    late = [
        pltpu.make_async_copy(up_hbm, up_ref, sems.at[5]),
        pltpu.make_async_copy(down_hbm, down_ref, sems.at[6]),
        pltpu.make_async_copy(dy_hbm, dy_ref, sems.at[7]),
    ]
    for copy in copies + late:
        copy.start()
    for copy in copies:
        copy.wait()
    tokens = x_ref.shape[1]
    chunk = 256
    spans = [slice(i, i + chunk) for i in range(0, tokens, chunk)]
    gate_pres = [dot(gate_ref[...], x_ref[:, spans[0]], 1, 0)]
    for copy in late:
        copy.wait()
    sums = [jnp.zeros((2 * RANK, mine_ref.shape[1]), F32)] * 3
    for i, span in enumerate(spans):
        x, dy = x_ref[:, span], dy_ref[:, span]
        gate_pre = gate_pres[0] if i == 0 else dot(gate_ref[...], x, 1, 0)
        up_pre = dot(up_ref[...], x, 1, 0)
        hidden_grad = dot(down_ref[...], dy, 1, 0)
        gate_sig = jax.nn.sigmoid(gate_pre)
        gate_act = gate_pre * gate_sig
        hidden = (gate_act * up_pre).astype(BF)
        gate_grad = (hidden_grad * up_pre * gate_sig * (1.0 + gate_pre * (1.0 - gate_sig))).astype(BF)
        up_grad = (hidden_grad * gate_act).astype(BF)
        gate_grad_ref[:, span] = gate_grad
        up_grad_ref[:, span] = up_grad
        hidden_ref[:, span] = hidden
        for k, (left, right) in enumerate(((gate_grad, x), (up_grad, x), (hidden, dy))):
            both = dot(q_ref[k], right, 1, 0)
            halves = jnp.concatenate(split(both[:RANK] + both[RANK:]))
            sums[k] = sums[k] + dot(halves, left, 1, 1)
    p = jnp.concatenate([both[:RANK] + both[RANK:] for both in sums]) + p_err_ref[...]
    mine, theirs = own_half(place_ref[1], p)
    mine_ref[...] = mine
    theirs_ref[...] = theirs.astype(BF)


def backward(place, pieces, dy_all, q_both, p_err, w_gate, w_up, w_down):
    hid, width = w_gate.shape
    tokens = dy_all.shape[1]
    vmem = pl.BlockSpec(memory_space=pltpu.VMEM)
    anywhere = pl.BlockSpec(memory_space=pl.ANY)
    grads = jax.ShapeDtypeStruct((hid, tokens), BF)
    weights = pltpu.VMEM((hid, width), BF)
    return pl.pallas_call(
        backward_kernel,
        out_shape=(
            grads,
            grads,
            grads,
            jax.ShapeDtypeStruct((HALF, hid), F32),
            jax.ShapeDtypeStruct((HALF, hid), BF),
            jax.ShapeDtypeStruct((width, tokens), BF),
        ),
        in_specs=[pl.BlockSpec(memory_space=pltpu.SMEM)] + [anywhere] * 8 + [vmem] * 2,
        out_specs=(vmem,) * 6,
        scratch_shapes=[
            pltpu.VMEM((width, tokens), BF),
            weights,
            weights,
            weights,
            pltpu.SemaphoreType.DMA((8,)),
        ],
        compiler_params=pltpu.CompilerParams(vmem_limit_bytes=58 * MIB),
        cost_estimate=pl.CostEstimate(flops=6 * hid * width * tokens, bytes_accessed=8 * MIB, transcendentals=0),
    )(place, *pieces, dy_all, w_gate, w_up, w_down, q_both, p_err)


def term_kernel(place_ref, w_ref, gate_grad_ref, up_grad_ref, t0_ref, t1_ref, t2_ref, t3_ref):
    grads = jnp.concatenate([gate_grad_ref[...], up_grad_ref[...]])
    rows = t0_ref.shape[0]
    for i, ref in enumerate((t0_ref, t1_ref, t2_ref, t3_ref)):
        at = pl.multiple_of(lax.rem(place_ref[0] + i, SIDE) * rows, 16)
        ref[...] = dot(w_ref[pl.ds(at, rows), :], grads, 1, 0).astype(BF)


def terms(place, w_both, gate_grad, up_grad):
    vmem = pl.BlockSpec(memory_space=pltpu.VMEM)
    width, both = w_both.shape
    tokens = gate_grad.shape[1]
    out = jax.ShapeDtypeStruct((width // SIDE, tokens), BF)
    return pl.pallas_call(
        term_kernel,
        out_shape=(out,) * SIDE,
        in_specs=[pl.BlockSpec(memory_space=pltpu.SMEM)] + [vmem] * 3,
        out_specs=(vmem,) * SIDE,
        compiler_params=pltpu.CompilerParams(vmem_limit_bytes=24 * MIB),
        cost_estimate=pl.CostEstimate(flops=2 * width * both * tokens, bytes_accessed=4 * MIB, transcendentals=0),
    )(place, w_both, gate_grad, up_grad)


def matrices_kernel(gate_grad_ref, up_grad_ref, hidden_ref, x_ref, dy_ref, err_ref, m0_ref, m1_ref, m2_ref):
    m0_ref[...] = dot(gate_grad_ref[...], x_ref[...], 1, 1) + err_ref[0, 0].astype(F32)
    m1_ref[...] = dot(up_grad_ref[...], x_ref[...], 1, 1) + err_ref[0, 1].astype(F32)
    swapped = dot(hidden_ref[...], dy_ref[...], 1, 1)
    block = swapped.shape[1] // (SIDE * SIDE)
    parts = [
        swapped[:, (x * SIDE + y) * block : (x * SIDE + y + 1) * block] for y in range(SIDE) for x in range(SIDE)
    ]
    m2_ref[...] = jnp.concatenate(parts, axis=1) + err_ref[0, 2].astype(F32)


def grad_matrices(gate_grad, up_grad, hidden, x_all, dy_all, error_in):
    vmem = pl.BlockSpec(memory_space=pltpu.VMEM)
    hid, tokens = hidden.shape
    width = x_all.shape[0]
    return pl.pallas_call(
        matrices_kernel,
        out_shape=(jax.ShapeDtypeStruct((hid, width), F32),) * 3,
        in_specs=[vmem] * 6,
        out_specs=(vmem,) * 3,
        compiler_params=pltpu.CompilerParams(vmem_limit_bytes=32 * MIB),
        cost_estimate=pl.CostEstimate(flops=6 * hid * width * tokens, bytes_accessed=9 * MIB, transcendentals=0),
    )(gate_grad, up_grad, hidden, x_all, dy_all, error_in)


def sketch_kernel(core_ref, p_mine_ref, p_other_ref, m0_ref, m1_ref, m2_ref, mine_ref, theirs_ref):
    core = core_ref[0]
    p = whole(core, p_mine_ref[...], p_other_ref[...])
    rows = []
    for k, m_ref in enumerate((m0_ref, m1_ref, m2_ref)):
        p_k = p[k * RANK : (k + 1) * RANK]
        p_high, p_low = split(p_k)
        m_high, m_low = split(m_ref[...])
        both = dot(jnp.concatenate([p_high, p_low]), m_high, 1, 0)
        term = both[:RANK] + both[RANK:] + dot(p_high, m_low, 1, 0)
        gram = dot3(p_k, p_k, 1, 1)
        rows.append(jnp.concatenate([term, gram, jnp.zeros((RANK, LANES - RANK), F32)], axis=1))
    mine, theirs = own_half(core, jnp.concatenate(rows))
    for i in range(HALF // 8):
        for j in range(8):
            tile = (i * 8 + j) * 8
            rows, cols = slice(i * 8, i * 8 + 8), slice(j * LANES, (j + 1) * LANES)
            mine_ref[tile : tile + 8, :] = mine[rows, cols]
            theirs_ref[tile : tile + 8, :] = theirs[rows, cols]


def sketch(core, p_mine, p_other, matrices):
    vmem = pl.BlockSpec(memory_space=pltpu.VMEM)
    out = jax.ShapeDtypeStruct((TILES * 8, LANES), F32)
    return pl.pallas_call(
        sketch_kernel,
        out_shape=(out, out),
        in_specs=[pl.BlockSpec(memory_space=pltpu.SMEM)] + [vmem] * 5,
        out_specs=(vmem, vmem),
        compiler_params=pltpu.CompilerParams(vmem_limit_bytes=40 * MIB),
    )(core, p_mine, p_other, *matrices)


def finish_kernel(core_ref, s_mine_ref, s_other_ref, p_mine_ref, p_other_ref, m0_ref, m1_ref, m2_ref,
                  error_ref, q_ref):
    core = core_ref[0]

    def rows_of(ref):
        return jnp.concatenate(
            [
                jnp.concatenate([ref[(i * 8 + j) * 8 : (i * 8 + j) * 8 + 8, :] for j in range(8)], axis=1)
                for i in range(HALF // 8)
            ]
        )

    s = whole(core, rows_of(s_mine_ref), rows_of(s_other_ref))
    p = whole(core, p_mine_ref[...], p_other_ref[...])
    width = m0_ref.shape[1]
    gram = jnp.stack([s[k * RANK : (k + 1) * RANK, width : width + RANK] for k in range(3)])
    rows = lax.broadcasted_iota(jnp.int32, (1, RANK, RANK), 1)
    cols = lax.broadcasted_iota(jnp.int32, (1, RANK, RANK), 2)
    eye = jnp.broadcast_to(jnp.where(rows == cols, 1.0, 0.0), gram.shape)
    work = jnp.concatenate([gram, eye], axis=2)
    below = lax.broadcasted_iota(jnp.int32, (1, RANK, 1), 1)
    for k in range(RANK):
        pivot = work[:, k : k + 1, :]
        scale = 1.0 / pivot[:, :, k : k + 1]
        factor = jnp.where(below > k, work[:, :, k : k + 1] * scale, 0.0)
        work = work - factor * pivot
    diag = jnp.sum(jnp.where(rows == cols, work[:, :, :RANK], 0.0), axis=2, keepdims=True)
    inverse = work[:, :, RANK:] * lax.rsqrt(diag)
    for k, m_ref in enumerate((m0_ref, m1_ref, m2_ref)):
        part = slice(k * RANK, (k + 1) * RANK)
        q_new = dot3(inverse[k], s[part, :width], 1, 0)
        p_ortho = dot3(inverse[k], p[part], 1, 0)
        q_ref[part, :] = q_new
        error_ref[0, k] = (m_ref[...] - dot3(p_ortho, q_new, 0, 0)).astype(BF)


def finish(core, s_mine, s_other, p_mine, p_other, matrices):
    vmem = pl.BlockSpec(memory_space=pltpu.VMEM)
    hid, width = matrices[0].shape
    return pl.pallas_call(
        finish_kernel,
        out_shape=(jax.ShapeDtypeStruct((1, 3, hid, width), BF), jax.ShapeDtypeStruct((ROWS, width), F32)),
        in_specs=[pl.BlockSpec(memory_space=pltpu.SMEM)] + [vmem] * 7,
        out_specs=(vmem, vmem),
        compiler_params=pltpu.CompilerParams(vmem_limit_bytes=40 * MIB),
    )(core, s_mine, s_other, p_mine, p_other, *matrices)


def swap_core(value):
    return lax.ppermute(value, "dp", CORE_PAIR)


def per_device(hidden_in, out_grad, w_gate, w_up, w_down, error_in, q_init):
    n_workers = lax.axis_size("dp")
    n_tensor = lax.axis_size("tensor")
    me = lax.axis_index("tensor")
    y, x = me // SIDE, me % SIDE
    core = lax.axis_index("dp") % 2
    shard = hidden_in.shape[1]

    q_cols = q_init.reshape(ROWS, shard).T
    pieces, q_pieces, dy_all = gather_all(hidden_in.T, out_grad.T, q_cols, me)
    dy_all = dy_all.reshape(shard * n_tensor, -1)
    spot = jnp.stack([y, core])
    q_both, p_err = factors(spot, q_pieces, error_in)
    w_down_swapped = swap_order(w_down.T).T
    w_both = jnp.concatenate([w_gate, w_up]).T
    gate_grad, up_grad, hidden, p_mine, p_theirs, x_all = backward(
        spot, pieces, dy_all, q_both, p_err, w_gate, w_up, w_down_swapped
    )
    core = core.reshape(1)
    input_grad = scatter_sum(terms(spot, w_both, gate_grad, up_grad), x).T
    p_pair = (p_mine + swap_core(p_theirs).astype(F32)).astype(BF)
    p_half = jnp.sum(spread(p_pair, "dp", Z_GROUPS, DEPTH).astype(F32), axis=0) / n_workers

    matrices = grad_matrices(gate_grad, up_grad, hidden, x_all, dy_all, error_in)

    p_other = swap_core(p_half)
    s_mine, s_theirs = sketch(core, p_half, p_other, matrices)
    s_pair = (s_mine + swap_core(s_theirs)).reshape(n_tensor, -1, LANES)
    s_part = jnp.sum(lax.all_to_all(s_pair, "tensor", 0, 0, tiled=True), axis=0)
    s_part = jnp.sum(spread(s_part, "dp", Z_GROUPS, DEPTH), axis=0) / n_workers
    s_half = spread(s_part, "tensor", None, n_tensor).reshape(-1, LANES)
    error_out, q_new = finish(core, s_half, swap_core(s_half), p_half, p_other, matrices)
    q_out = lax.dynamic_slice_in_dim(q_new, me * shard, shard, 1).reshape(q_init.shape)
    return (input_grad, error_out, q_out)


def solution(mesh):
    in_specs = (
        P("dp", "tensor"),
        P("dp", "tensor"),
        P("tensor", None),
        P("tensor", None),
        P("tensor", None),
        P("dp", None, "tensor", None),
        P(None, None, "tensor"),
    )
    out_specs = (P("dp", "tensor"), P("dp", None, "tensor", None), P(None, None, "tensor"))
    return jax.shard_map(
        per_device, mesh=mesh, in_specs=in_specs, out_specs=out_specs, check_vma=False
    )
```

```python
import jax
import jax.numpy as jnp
from jax import lax
from jax.experimental import pallas as pl
from jax.experimental.pallas import tpu as pltpu
from jax.sharding import PartitionSpec as P

BF = jnp.bfloat16
F32 = jnp.float32
SIDE = 4
DEPTH = 8
RANK = 32
ROWS = 3 * RANK
HALF = ROWS // 2
LANES = 128
TILES = HALF * 1024 // (8 * LANES)
MIB = 1 << 20

X_GROUPS = [[y * SIDE + x for x in range(SIDE)] for y in range(SIDE)]
Y_GROUPS = [[y * SIDE + x for y in range(SIDE)] for x in range(SIDE)]
CORE_PAIR = [(i, i ^ 1) for i in range(2 * DEPTH)]
Z_GROUPS = [[z * 2 + c for z in range(DEPTH)] for c in range(2)]


def x_ring(k):
    return [(y * SIDE + x, y * SIDE + (x + k) % SIDE) for y in range(SIDE) for x in range(SIDE)]


def y_ring(k):
    return [(y * SIDE + x, ((y + k) % SIDE) * SIDE + x) for y in range(SIDE) for x in range(SIDE)]


def spread(value, axis, groups, size):
    return lax.all_to_all(
        jnp.broadcast_to(value[None], (size,) + value.shape), axis, 0, 0, tiled=True, axis_index_groups=groups
    )


def ring_pieces(value, ring):
    near = [value] + [None] * 3
    for k in (1, 3, 2):
        near[k] = lax.ppermute(value, "tensor", ring(SIDE - k))
    return near


def pack_kernel(x_hbm, dy_hbm, q_ref, x_ref, dy_ref, sems):
    tokens = x_hbm.shape[1]
    copies = [pltpu.make_async_copy(x_hbm, x_ref.at[:, pl.ds(0, tokens)], sems.at[0])]
    for i in range(SIDE):
        copies.append(pltpu.make_async_copy(dy_hbm, dy_ref.at[i, :, pl.ds(0, tokens)], sems.at[1 + i]))
    for copy in copies:
        copy.start()
    high, low = split(q_ref[...].T)
    both = [[half[:, k * RANK : (k + 1) * RANK] for half in (high, low)] for k in range(3)]
    x_ref[:, tokens:] = jnp.concatenate(both[0] + both[1], axis=1)
    tail = jnp.concatenate(both[2] + [jnp.zeros((high.shape[0], LANES - 2 * RANK), BF)], axis=1)
    for i in range(SIDE):
        dy_ref[i, :, tokens:] = tail
    for copy in copies:
        copy.wait()


def pack(x_part, dy_part, q_rows):
    vmem = pl.BlockSpec(memory_space=pltpu.VMEM)
    anywhere = pl.BlockSpec(memory_space=pl.ANY)
    rows, tokens = x_part.shape
    return pl.pallas_call(
        pack_kernel,
        out_shape=(
            jax.ShapeDtypeStruct((rows, tokens + LANES), BF),
            jax.ShapeDtypeStruct((SIDE, rows, tokens + LANES), BF),
        ),
        in_specs=[anywhere, anywhere, vmem],
        out_specs=(vmem, vmem),
        scratch_shapes=[pltpu.SemaphoreType.DMA((1 + SIDE,))],
        compiler_params=pltpu.CompilerParams(vmem_limit_bytes=58 * MIB),
    )(x_part, dy_part, q_rows)


def order_kernel(place_ref, p0_ref, p1_ref, p2_ref, p3_ref, out_ref, sems):
    copies = [
        pltpu.make_async_copy(ref, out_ref.at[lax.rem(place_ref[0] + i, SIDE)], sems.at[i])
        for i, ref in enumerate((p0_ref, p1_ref, p2_ref, p3_ref))
    ]
    for copy in copies:
        copy.start()
    for copy in copies:
        copy.wait()


def order(position, pieces):
    anywhere = pl.BlockSpec(memory_space=pl.ANY)
    return pl.pallas_call(
        order_kernel,
        out_shape=jax.ShapeDtypeStruct((SIDE,) + pieces[0].shape, pieces[0].dtype),
        in_specs=[pl.BlockSpec(memory_space=pltpu.SMEM)] + [anywhere] * SIDE,
        out_specs=pl.BlockSpec(memory_space=pltpu.VMEM),
        scratch_shapes=[pltpu.SemaphoreType.DMA((SIDE,))],
        compiler_params=pltpu.CompilerParams(vmem_limit_bytes=20 * MIB),
    )(position.reshape(1), *pieces)


def gather_all(x_part, dy_parts, me):
    rows = SIDE * x_part.shape[0]
    dy_col = lax.all_to_all(dy_parts, "tensor", 0, 0, tiled=True, axis_index_groups=Y_GROUPS)
    near, dy_col = lax.optimization_barrier((ring_pieces(x_part, x_ring), dy_col))
    x_row, dy_col = lax.optimization_barrier((order(me % SIDE, near), dy_col))
    dy_all = spread(dy_col, "tensor", X_GROUPS, SIDE)
    far, dy_all = lax.optimization_barrier((ring_pieces(x_row, y_ring), dy_all))
    return [p.reshape(rows, -1) for p in far], dy_all.reshape(SIDE * rows, -1)


def swap_order(value):
    blocks = value.reshape((SIDE, SIDE, -1) + value.shape[1:])
    return jnp.swapaxes(blocks, 0, 1).reshape(value.shape)


def send_blocks(blocks):
    return [blocks[0]] + [lax.ppermute(blocks[k], "tensor", y_ring(k)) for k in (1, 3, 2)]


def parts_kernel(place_ref, g0_ref, g1_ref, g2_ref, g3_ref, _, o0_ref, o1_ref, o2_ref, o3_ref):
    for k, out_ref in enumerate((o0_ref, o1_ref, o2_ref, o3_ref)):
        at = lax.rem(place_ref[0] + k, SIDE)
        total = sum(ref[at].astype(F32) for ref in (g0_ref, g1_ref, g2_ref, g3_ref))
        out_ref[...] = total.astype(out_ref.dtype)


def send_parts(got, position, token):
    vmem = pl.BlockSpec(memory_space=pltpu.VMEM)
    rows, tokens = got[0].shape
    parts = pl.pallas_call(
        parts_kernel,
        out_shape=(jax.ShapeDtypeStruct((rows // SIDE, tokens), BF),) * SIDE,
        in_specs=[pl.BlockSpec(memory_space=pltpu.SMEM)] + [vmem] * (SIDE + 1),
        out_specs=(vmem,) * SIDE,
        compiler_params=pltpu.CompilerParams(vmem_limit_bytes=20 * MIB),
    )(position.reshape(1), *[v.reshape(SIDE, -1, tokens) for v in got], token)
    return [parts[0]] + [lax.ppermute(parts[k], "tensor", x_ring(k)) for k in (1, 3, 2)]


def split(value):
    high = value.astype(BF)
    return high, (value - high.astype(F32)).astype(BF)


def dot(a, b, ca, cb):
    return lax.dot_general(a, b, (((ca,), (cb,)), ((), ())), preferred_element_type=F32)


def dot3(a, b, ca, cb):
    a_high, a_low = split(a)
    b_high, b_low = split(b)
    return dot(
        jnp.concatenate([a_high, a_high, a_low], axis=ca), jnp.concatenate([b_high, b_low, b_high], axis=cb), ca, cb
    )


def own_half(core, value):
    low, high = value[:HALF], value[HALF:]
    first = core == 0
    return jnp.where(first, low, high), jnp.where(first, high, low)


def whole(core, mine, other):
    first = core == 0
    return jnp.concatenate([jnp.where(first, mine, other), jnp.where(first, other, mine)])


def prepare_kernel(gate_ref, up_ref, down_ref, err_ref, left_ref, both_ref, token_ref):
    hid, width = gate_ref.shape
    gate, up, down = gate_ref[...], up_ref[...], down_ref[...].astype(F32)
    block = width // (SIDE * SIDE)
    left_ref[0] = gate
    left_ref[1] = up
    left_ref[2] = jnp.concatenate(
        [down[:, (y * SIDE + x) * block : (y * SIDE + x + 1) * block] for x in range(SIDE) for y in range(SIDE)],
        axis=1,
    ).astype(BF)
    for k in range(3):
        left_ref[3 + k] = err_ref[0, k]
    both_ref[:, :hid] = gate.astype(F32).T.astype(BF)
    both_ref[:, hid:] = up.astype(F32).T.astype(BF)
    token_ref[...] = jnp.zeros_like(token_ref)


def prepare(w_gate, w_up, w_down, error_in):
    vmem = pl.BlockSpec(memory_space=pltpu.VMEM)
    hid, width = w_gate.shape
    return pl.pallas_call(
        prepare_kernel,
        out_shape=(
            jax.ShapeDtypeStruct((6, hid, width), BF),
            jax.ShapeDtypeStruct((width, 2 * hid), BF),
            jax.ShapeDtypeStruct((8, LANES), F32),
        ),
        in_specs=[vmem] * 4,
        out_specs=(vmem,) * 3,
        compiler_params=pltpu.CompilerParams(vmem_limit_bytes=20 * MIB),
    )(w_gate, w_up, w_down, error_in)


def backward_kernel(place_ref, p0_ref, p1_ref, p2_ref, p3_ref, dy_ref, w_ref,
                    gate_grad_ref, up_grad_ref, hidden_ref, mine_ref, theirs_ref, x_ref):
    rows = p0_ref.shape[0]
    hid, tokens = hidden_ref.shape
    for i, ref in enumerate((p0_ref, p1_ref, p2_ref, p3_ref)):
        at = pl.multiple_of(lax.rem(place_ref[0] + i, SIDE) * rows, 16)
        x_ref[pl.ds(at, rows), :] = ref[...]
    q_x = x_ref[:, tokens:]
    q_dy = dy_ref[:, tokens : tokens + 2 * RANK]
    q_rows = q_x.astype(F32).T.astype(BF)
    q_both = [q_rows[: 2 * RANK], q_rows[2 * RANK :], q_dy.astype(F32).T.astype(BF)]
    sums = [jnp.zeros((2 * RANK, hid), F32)] * 3
    chunk = 256
    for start in range(0, tokens, chunk):
        span = slice(start, start + chunk)
        x, dy = x_ref[:, span], dy_ref[:, span]
        gate_pre = dot(w_ref[0], x, 1, 0)
        up_pre = dot(w_ref[1], x, 1, 0)
        hidden_grad = dot(w_ref[2], dy, 1, 0)
        gate_sig = jax.nn.sigmoid(gate_pre)
        gate_act = gate_pre * gate_sig
        hidden = (gate_act * up_pre).astype(BF)
        gate_grad = (hidden_grad * up_pre * gate_sig * (1.0 + gate_pre * (1.0 - gate_sig))).astype(BF)
        up_grad = (hidden_grad * gate_act).astype(BF)
        gate_grad_ref[:, span] = gate_grad
        up_grad_ref[:, span] = up_grad
        hidden_ref[:, span] = hidden
        for k, (left, right) in enumerate(((gate_grad, x), (up_grad, x), (hidden, dy))):
            both = dot(q_both[k], right, 1, 0)
            halves = jnp.concatenate(split(both[:RANK] + both[RANK:]))
            sums[k] = sums[k] + dot(halves, left, 1, 1)
    block = rows // SIDE
    q_plain = q_dy.astype(F32)
    q_plain = jnp.concatenate(
        [q_plain[(x * SIDE + y) * block : (x * SIDE + y + 1) * block] for y in range(SIDE) for x in range(SIDE)]
    ).astype(BF)
    errors = [
        dot(w_ref[3 + k], q, 1, 0) for k, q in enumerate((q_x[:, : 2 * RANK], q_x[:, 2 * RANK :], q_plain))
    ]
    error_p = jnp.concatenate([both[:, :RANK] + both[:, RANK:] for both in errors], axis=1).T
    p = jnp.concatenate([both[:RANK] + both[RANK:] for both in sums]) + error_p
    mine, theirs = own_half(place_ref[1], p)
    mine_ref[...] = mine
    theirs_ref[...] = theirs.astype(BF)


def backward(place, pieces, dy_all, weights):
    hid, width = weights.shape[1:]
    wide = dy_all.shape[1]
    tokens = wide - LANES
    vmem = pl.BlockSpec(memory_space=pltpu.VMEM)
    grads = jax.ShapeDtypeStruct((hid, tokens), BF)
    return pl.pallas_call(
        backward_kernel,
        out_shape=(
            grads,
            grads,
            grads,
            jax.ShapeDtypeStruct((HALF, hid), F32),
            jax.ShapeDtypeStruct((HALF, hid), BF),
            jax.ShapeDtypeStruct((width, wide), BF),
        ),
        in_specs=[pl.BlockSpec(memory_space=pltpu.SMEM)] + [vmem] * 6,
        out_specs=(vmem,) * 6,
        compiler_params=pltpu.CompilerParams(vmem_limit_bytes=20 * MIB),
        cost_estimate=pl.CostEstimate(flops=6 * hid * width * tokens, bytes_accessed=8 * MIB, transcendentals=0),
    )(place, *pieces, dy_all, weights)


def products_kernel(place_ref, w_ref, gate_grad_ref, up_grad_ref, hidden_ref, x_ref, dy_ref, left_ref, _,
                    t0_ref, t1_ref, t2_ref, t3_ref, m0_ref, m1_ref, m2_ref, token_ref):
    tokens = hidden_ref.shape[1]
    gate_grad, up_grad = gate_grad_ref[...], up_grad_ref[...]
    grads = jnp.concatenate([gate_grad, up_grad])
    rows = t0_ref.shape[0]
    for i, ref in enumerate((t0_ref, t1_ref, t2_ref, t3_ref)):
        at = pl.multiple_of(lax.rem(place_ref[0] + i, SIDE) * rows, 16)
        ref[...] = dot(w_ref[pl.ds(at, rows), :], grads, 1, 0).astype(BF)
    x = x_ref[:, :tokens]
    m0_ref[...] = dot(gate_grad, x, 1, 1) + left_ref[3].astype(F32)
    m1_ref[...] = dot(up_grad, x, 1, 1) + left_ref[4].astype(F32)
    swapped = dot(hidden_ref[...], dy_ref[:, :tokens], 1, 1)
    block = rows // SIDE
    parts = [
        swapped[:, (x * SIDE + y) * block : (x * SIDE + y + 1) * block] for y in range(SIDE) for x in range(SIDE)
    ]
    m2_ref[...] = jnp.concatenate(parts, axis=1) + left_ref[5].astype(F32)
    token_ref[...] = jnp.zeros_like(token_ref)


def products(place, w_both, grads, x_all, dy_all, weights, other):
    vmem = pl.BlockSpec(memory_space=pltpu.VMEM)
    hid, tokens = grads[0].shape
    width = w_both.shape[0]
    out = pl.pallas_call(
        products_kernel,
        out_shape=(jax.ShapeDtypeStruct((width // SIDE, tokens), BF),) * SIDE
        + (jax.ShapeDtypeStruct((hid, width), F32),) * 3
        + (jax.ShapeDtypeStruct((8, LANES), F32),),
        in_specs=[pl.BlockSpec(memory_space=pltpu.SMEM)] + [vmem] * 8,
        out_specs=(vmem,) * (SIDE + 4),
        compiler_params=pltpu.CompilerParams(vmem_limit_bytes=20 * MIB),
        cost_estimate=pl.CostEstimate(flops=10 * hid * width * tokens, bytes_accessed=12 * MIB, transcendentals=0),
    )(place, w_both, *grads, x_all, dy_all, weights, other)
    return out[:SIDE], out[SIDE : SIDE + 3], out[-1]


def mean_kernel(value_ref, _, out_ref):
    total = value_ref[0].astype(F32)
    for i in range(1, value_ref.shape[0]):
        total = total + value_ref[i].astype(F32)
    out_ref[...] = total * (0.5 / value_ref.shape[0])


def mean(value, token):
    vmem = pl.BlockSpec(memory_space=pltpu.VMEM)
    return pl.pallas_call(
        mean_kernel,
        out_shape=jax.ShapeDtypeStruct(value.shape[1:], F32),
        in_specs=[vmem, vmem],
        out_specs=vmem,
        compiler_params=pltpu.CompilerParams(vmem_limit_bytes=20 * MIB),
    )(value, token)


def sketch_kernel(core_ref, p_mine_ref, p_other_ref, m0_ref, m1_ref, m2_ref, mine_ref, theirs_ref, gram_ref):
    core = core_ref[0]
    p = whole(core, p_mine_ref[...], p_other_ref[...])
    rows, grams = [], []
    for k, m_ref in enumerate((m0_ref, m1_ref, m2_ref)):
        p_k = p[k * RANK : (k + 1) * RANK]
        p_high, p_low = split(p_k)
        m_high, m_low = split(m_ref[...])
        both = dot(jnp.concatenate([p_high, p_low]), m_high, 1, 0)
        term = both[:RANK] + both[RANK:] + dot(p_high, m_low, 1, 0)
        grams.append(dot3(p_k, p_k, 1, 1))
        rows.append(jnp.concatenate([term, jnp.zeros((RANK, LANES), F32)], axis=1))
    gram = jnp.concatenate(grams)
    gram_ref[...] = jnp.concatenate([gram[i * 24 : (i + 1) * 24] for i in range(4)], axis=1)
    mine, theirs = own_half(core, jnp.concatenate(rows))
    for i in range(HALF // 8):
        for j in range(8):
            tile = (i * 8 + j) * 8
            rows, cols = slice(i * 8, i * 8 + 8), slice(j * LANES, (j + 1) * LANES)
            mine_ref[tile : tile + 8, :] = mine[rows, cols]
            theirs_ref[tile : tile + 8, :] = theirs[rows, cols]


def sketch(core, p_mine, p_other, matrices):
    vmem = pl.BlockSpec(memory_space=pltpu.VMEM)
    out = jax.ShapeDtypeStruct((TILES * 8, LANES), F32)
    return pl.pallas_call(
        sketch_kernel,
        out_shape=(out, out, jax.ShapeDtypeStruct((24, LANES), F32)),
        in_specs=[pl.BlockSpec(memory_space=pltpu.SMEM)] + [vmem] * 5,
        out_specs=(vmem,) * 3,
        compiler_params=pltpu.CompilerParams(vmem_limit_bytes=20 * MIB),
    )(core, p_mine, p_other, *matrices)


def ortho_kernel(core_ref, gram_ref, p_mine_ref, p_other_ref, _, inverse_ref, p_ortho_ref):
    gram = gram_ref[...]
    gram = jnp.concatenate([gram[:, i * RANK : (i + 1) * RANK] for i in range(4)])
    gram = jnp.stack([gram[k * RANK : (k + 1) * RANK] for k in range(3)])
    rows = lax.broadcasted_iota(jnp.int32, (1, RANK, RANK), 1)
    cols = lax.broadcasted_iota(jnp.int32, (1, RANK, RANK), 2)
    eye = jnp.broadcast_to(jnp.where(rows == cols, 1.0, 0.0), gram.shape)
    work = jnp.concatenate([gram, eye], axis=2)
    below = lax.broadcasted_iota(jnp.int32, (1, RANK, 1), 1)
    for k in range(RANK):
        pivot = work[:, k : k + 1, :]
        scale = 1.0 / pivot[:, :, k : k + 1]
        factor = jnp.where(below > k, work[:, :, k : k + 1] * scale, 0.0)
        work = work - factor * pivot
    diag = jnp.sum(jnp.where(rows == cols, work[:, :, :RANK], 0.0), axis=2, keepdims=True)
    inverse = work[:, :, RANK:] * lax.rsqrt(diag)
    inverse_ref[...] = inverse
    p = whole(core_ref[0], p_mine_ref[...], p_other_ref[...])
    for k in range(3):
        part = slice(k * RANK, (k + 1) * RANK)
        p_ortho_ref[part, :] = dot3(inverse[k], p[part], 1, 0)


def ortho(core, gram, p_mine, p_other, token):
    vmem = pl.BlockSpec(memory_space=pltpu.VMEM)
    return pl.pallas_call(
        ortho_kernel,
        out_shape=(
            jax.ShapeDtypeStruct((3, RANK, RANK), F32),
            jax.ShapeDtypeStruct((ROWS, p_mine.shape[1]), F32),
        ),
        in_specs=[pl.BlockSpec(memory_space=pltpu.SMEM)] + [vmem] * 4,
        out_specs=(vmem, vmem),
        cost_estimate=pl.CostEstimate(flops=MIB * 4096, bytes_accessed=MIB, transcendentals=0),
    )(core, gram, p_mine, p_other, token)


def finish_kernel(place_ref, s_mine_ref, s_other_ref, inverse_ref, p_ortho_ref, m0_hbm, m1_hbm, m2_hbm,
                  error_hbm, q_ref, m_ref, error_ref, sems):
    copies = [pltpu.make_async_copy(m, m_ref.at[k], sems.at[k]) for k, m in enumerate((m0_hbm, m1_hbm, m2_hbm))]
    for copy in copies:
        copy.start()
    width = m_ref.shape[2]

    def rows_of(ref):
        return jnp.concatenate(
            [
                jnp.concatenate([ref[(i * 8 + j) * 8 : (i * 8 + j) * 8 + 8, :] for j in range(7)], axis=1)
                for i in range(HALF // 8)
            ]
        )

    s = whole(place_ref[0], rows_of(s_mine_ref), rows_of(s_other_ref))
    stores, q_rows = [], []
    for k in range(3):
        part = slice(k * RANK, (k + 1) * RANK)
        q_new = dot3(inverse_ref[k], s[part], 1, 0)
        q_rows.append(q_new)
        copies[k].wait()
        error_ref[k] = (m_ref[k] - dot3(p_ortho_ref[part, :], q_new, 0, 0)).astype(BF)
        stores.append(pltpu.make_async_copy(error_ref.at[k], error_hbm.at[0, k], sems.at[3 + k]))
        stores[k].start()
    shard = q_ref.shape[1]
    at = place_ref[1] * shard
    q_ref[...] = pltpu.roll(jnp.concatenate(q_rows), lax.rem(width - at, width), 1)[:, :shard]
    for copy in stores:
        copy.wait()


def finish(place, s_mine, s_other, inverse, p_ortho, matrices, shard):
    vmem = pl.BlockSpec(memory_space=pltpu.VMEM)
    hbm = pl.BlockSpec(memory_space=pltpu.HBM)
    hid, width = matrices[0].shape
    return pl.pallas_call(
        finish_kernel,
        out_shape=(jax.ShapeDtypeStruct((1, 3, hid, width), BF), jax.ShapeDtypeStruct((ROWS, shard), F32)),
        in_specs=[pl.BlockSpec(memory_space=pltpu.SMEM)] + [vmem] * 4 + [hbm] * 3,
        out_specs=(hbm, vmem),
        scratch_shapes=[
            pltpu.VMEM((3, hid, width), F32),
            pltpu.VMEM((3, hid, width), BF),
            pltpu.SemaphoreType.DMA((6,)),
        ],
        compiler_params=pltpu.CompilerParams(vmem_limit_bytes=20 * MIB),
    )(place, s_mine, s_other, inverse, p_ortho, *matrices)


def after(values, other):
    return lax.optimization_barrier((values, other))[0]


def swap_core(value):
    return lax.ppermute(value, "dp", CORE_PAIR)


def z_ring(k):
    return [(z * 2 + c, (z + k) % DEPTH * 2 + c) for z in range(DEPTH) for c in range(2)]


def z_ring_swap():
    return [(z * 2 + c, (z ^ 1) * 2 + c) for z in range(DEPTH) for c in range(2)]


def take_kernel(value_ref, _, out_ref):
    out_ref[...] = value_ref[...]


def take(value, token):
    vmem = pl.BlockSpec(memory_space=pltpu.VMEM)
    return pl.pallas_call(
        take_kernel,
        out_shape=jax.ShapeDtypeStruct(value.shape, value.dtype),
        in_specs=[vmem, vmem],
        out_specs=vmem,
        compiler_params=pltpu.CompilerParams(vmem_limit_bytes=20 * MIB),
    )(value, token)


def add(values, token, scale, kind=F32):
    vmem = pl.BlockSpec(memory_space=pltpu.VMEM)

    def kernel(*refs):
        refs[-1][...] = (sum(ref[...].astype(F32) for ref in refs[:-2]) * scale).astype(kind)

    return pl.pallas_call(
        kernel,
        out_shape=jax.ShapeDtypeStruct(values[0].shape, kind),
        in_specs=[vmem] * (len(values) + 1),
        out_specs=vmem,
        compiler_params=pltpu.CompilerParams(vmem_limit_bytes=20 * MIB),
    )(*values, token)


def close_kernel(*refs):
    refs[-2][...] = sum(ref[...].astype(F32) for ref in refs[:-2]).astype(BF)
    refs[-1][...] = jnp.zeros_like(refs[-1])


def close(values):
    vmem = pl.BlockSpec(memory_space=pltpu.VMEM)
    return pl.pallas_call(
        close_kernel,
        out_shape=(jax.ShapeDtypeStruct(values[0].shape, BF), jax.ShapeDtypeStruct((8, LANES), F32)),
        in_specs=[vmem] * len(values),
        out_specs=(vmem, vmem),
        compiler_params=pltpu.CompilerParams(vmem_limit_bytes=20 * MIB),
    )(*values)


def per_device(hidden_in, out_grad, w_gate, w_up, w_down, error_in, q_init):
    n_workers = lax.axis_size("dp")
    n_tensor = lax.axis_size("tensor")
    me = lax.axis_index("tensor")
    y, x = me // SIDE, me % SIDE
    core = lax.axis_index("dp") % 2
    shard = hidden_in.shape[1]

    weights, w_both, _ = prepare(w_gate, w_up, w_down, error_in)
    x_part, dy_parts = pack(hidden_in.T, out_grad.T, q_init.reshape(ROWS, shard))
    pieces, dy_all = gather_all(x_part, dy_parts, me)
    spot = jnp.stack([y, core])
    gate_grad, up_grad, hidden, p_mine, p_theirs, x_all = backward(spot, pieces, dy_all, weights)
    core = core.reshape(1)
    p_pair = (p_mine + swap_core(p_theirs).astype(F32)).astype(BF)
    p_next = lax.ppermute(p_pair, "dp", z_ring_swap())
    blocks, matrices, token = products(
        spot, w_both, (gate_grad, up_grad, hidden), x_all, dy_all, weights, p_pair
    )
    p_two = add((p_pair, p_next), token, 1.0)
    p_half = add([p_two] + [lax.ppermute(p_two, "dp", z_ring(k)) for k in (4, 2, 6)], token, 1.0 / n_workers)
    p_other = swap_core(p_half)
    got = send_blocks(blocks)
    s_mine, s_theirs, gram = sketch(core, p_half, p_other, matrices)
    s_pair = (s_mine + swap_core(s_theirs)).reshape(n_tensor, -1, LANES)
    gram = jnp.broadcast_to(gram[None], (n_tensor,) + gram.shape)
    sums = jnp.sum(lax.all_to_all(jnp.concatenate([s_pair, gram], axis=1), "tensor", 0, 0, tiled=True), axis=0)
    s_part, gram = sums[: s_pair.shape[1]], sums[s_pair.shape[1] :]
    s_all = spread(s_part, "dp", Z_GROUPS, DEPTH)
    inverse, p_ortho = ortho(core, gram, p_half, p_other, gram)
    s_part = mean(s_all, inverse)
    got = send_parts(got, x, gram)
    input_grad, token = close(got)
    input_grad = input_grad.T
    s_half = take(spread(s_part, "tensor", None, n_tensor).reshape(-1, LANES), token)
    error_out, q_out = finish(
        jnp.stack([core[0], me]), s_half, swap_core(s_half), inverse, p_ortho, matrices, shard
    )
    return (input_grad, error_out, q_out.reshape(q_init.shape))


def solution(mesh):
    in_specs = (
        P("dp", "tensor"),
        P("dp", "tensor"),
        P("tensor", None),
        P("tensor", None),
        P("tensor", None),
        P("dp", None, "tensor", None),
        P(None, None, "tensor"),
    )
    out_specs = (P("dp", "tensor"), P("dp", None, "tensor", None), P(None, None, "tensor"))
    return jax.shard_map(
        per_device, mesh=mesh, in_specs=in_specs, out_specs=out_specs, check_vma=False
    )
```

```python
import jax
import jax.numpy as jnp
from jax import lax
from jax.experimental import pallas as pl
from jax.experimental.pallas import tpu as pltpu
from jax.sharding import PartitionSpec as P

BF = jnp.bfloat16
F32 = jnp.float32
SIDE = 4
DEPTH = 8
RANK = 32
ROWS = 3 * RANK
HALF = ROWS // 2
LANES = 128
TILES = HALF * 1024 // (8 * LANES)
MIB = 1 << 20
STORE = 112

X_GROUPS = [[y * SIDE + x for x in range(SIDE)] for y in range(SIDE)]
Y_GROUPS = [[y * SIDE + x for y in range(SIDE)] for x in range(SIDE)]
CORE_PAIR = [(i, i ^ 1) for i in range(2 * DEPTH)]
Z_GROUPS = [[z * 2 + c for z in range(DEPTH)] for c in range(2)]


def x_ring(k):
    return [(y * SIDE + x, y * SIDE + (x + k) % SIDE) for y in range(SIDE) for x in range(SIDE)]


def y_ring(k):
    return [(y * SIDE + x, ((y + k) % SIDE) * SIDE + x) for y in range(SIDE) for x in range(SIDE)]


def spread(value, axis, groups, size):
    return lax.all_to_all(
        jnp.broadcast_to(value[None], (size,) + value.shape), axis, 0, 0, tiled=True, axis_index_groups=groups
    )


def ring_pieces(value, ring):
    near = [value] + [None] * 3
    for k in (1, 3, 2):
        near[k] = lax.ppermute(value, "tensor", ring(SIDE - k))
    return near


def pack_kernel(x_hbm, dy_hbm, q_ref, x_ref, dy_ref, sems):
    tokens = x_hbm.shape[1]
    copies = [pltpu.make_async_copy(x_hbm, x_ref.at[:, pl.ds(0, tokens)], sems.at[0])]
    for i in range(SIDE):
        copies.append(pltpu.make_async_copy(dy_hbm, dy_ref.at[i, :, pl.ds(0, tokens)], sems.at[1 + i]))
    for copy in copies:
        copy.start()
    high, low = split(q_ref[...].T)
    both = [[half[:, k * RANK : (k + 1) * RANK] for half in (high, low)] for k in range(3)]
    x_ref[:, tokens:] = jnp.concatenate(both[0] + both[1], axis=1)
    tail = jnp.concatenate(both[2] + [jnp.zeros((high.shape[0], LANES - 2 * RANK), BF)], axis=1)
    for i in range(SIDE):
        dy_ref[i, :, tokens:] = tail
    for copy in copies:
        copy.wait()


def pack(x_part, dy_part, q_rows):
    vmem = pl.BlockSpec(memory_space=pltpu.VMEM)
    anywhere = pl.BlockSpec(memory_space=pl.ANY)
    rows, tokens = x_part.shape
    return pl.pallas_call(
        pack_kernel,
        out_shape=(
            jax.ShapeDtypeStruct((rows, tokens + LANES), BF),
            jax.ShapeDtypeStruct((SIDE, rows, tokens + LANES), BF),
        ),
        in_specs=[anywhere, anywhere, vmem],
        out_specs=(vmem, vmem),
        scratch_shapes=[pltpu.SemaphoreType.DMA((1 + SIDE,))],
        compiler_params=pltpu.CompilerParams(vmem_limit_bytes=58 * MIB),
    )(x_part, dy_part, q_rows)


def order_kernel(place_ref, p0_ref, p1_ref, p2_ref, p3_ref, out_ref, sems):
    copies = [
        pltpu.make_async_copy(ref, out_ref.at[lax.rem(place_ref[0] + i, SIDE)], sems.at[i])
        for i, ref in enumerate((p0_ref, p1_ref, p2_ref, p3_ref))
    ]
    for copy in copies:
        copy.start()
    for copy in copies:
        copy.wait()


def order(position, pieces):
    anywhere = pl.BlockSpec(memory_space=pl.ANY)
    return pl.pallas_call(
        order_kernel,
        out_shape=jax.ShapeDtypeStruct((SIDE,) + pieces[0].shape, pieces[0].dtype),
        in_specs=[pl.BlockSpec(memory_space=pltpu.SMEM)] + [anywhere] * SIDE,
        out_specs=pl.BlockSpec(memory_space=pltpu.VMEM),
        scratch_shapes=[pltpu.SemaphoreType.DMA((SIDE,))],
        compiler_params=pltpu.CompilerParams(vmem_limit_bytes=20 * MIB),
    )(position.reshape(1), *pieces)


def gather_all(x_part, dy_parts, me):
    rows = SIDE * x_part.shape[0]
    dy_col = lax.all_to_all(dy_parts, "tensor", 0, 0, tiled=True, axis_index_groups=Y_GROUPS)
    near, dy_col = lax.optimization_barrier((ring_pieces(x_part, x_ring), dy_col))
    x_row, dy_col = lax.optimization_barrier((order(me % SIDE, near), dy_col))
    dy_all = spread(dy_col, "tensor", X_GROUPS, SIDE)
    far, dy_all = lax.optimization_barrier((ring_pieces(x_row, y_ring), dy_all))
    return [p.reshape(rows, -1) for p in far], dy_all.reshape(SIDE * rows, -1)


def swap_order(value):
    blocks = value.reshape((SIDE, SIDE, -1) + value.shape[1:])
    return jnp.swapaxes(blocks, 0, 1).reshape(value.shape)


def send_blocks(blocks):
    return [blocks[0]] + [lax.ppermute(blocks[k], "tensor", y_ring(k)) for k in (1, 3, 2)]


def parts_kernel(place_ref, g0_ref, g1_ref, g2_ref, g3_ref, _, o0_ref, o1_ref, o2_ref, o3_ref):
    for k, out_ref in enumerate((o0_ref, o1_ref, o2_ref, o3_ref)):
        at = lax.rem(place_ref[0] + k, SIDE)
        total = sum(ref[at].astype(F32) for ref in (g0_ref, g1_ref, g2_ref, g3_ref))
        out_ref[...] = total.astype(out_ref.dtype)


def send_parts(got, position, token):
    vmem = pl.BlockSpec(memory_space=pltpu.VMEM)
    rows, tokens = got[0].shape
    parts = pl.pallas_call(
        parts_kernel,
        out_shape=(jax.ShapeDtypeStruct((rows // SIDE, tokens), BF),) * SIDE,
        in_specs=[pl.BlockSpec(memory_space=pltpu.SMEM)] + [vmem] * (SIDE + 1),
        out_specs=(vmem,) * SIDE,
        compiler_params=pltpu.CompilerParams(vmem_limit_bytes=20 * MIB),
    )(position.reshape(1), *[v.reshape(SIDE, -1, tokens) for v in got], token)
    return [parts[0]] + [lax.ppermute(parts[k], "tensor", x_ring(k)) for k in (1, 3, 2)]


def split(value):
    high = value.astype(BF)
    return high, (value - high.astype(F32)).astype(BF)


def dot(a, b, ca, cb):
    return lax.dot_general(a, b, (((ca,), (cb,)), ((), ())), preferred_element_type=F32)


def dot3(a, b, ca, cb):
    a_high, a_low = split(a)
    b_high, b_low = split(b)
    return dot(
        jnp.concatenate([a_high, a_high, a_low], axis=ca), jnp.concatenate([b_high, b_low, b_high], axis=cb), ca, cb
    )


def own_half(core, value):
    low, high = value[:HALF], value[HALF:]
    first = core == 0
    return jnp.where(first, low, high), jnp.where(first, high, low)


def whole(core, mine, other):
    first = core == 0
    return jnp.concatenate([jnp.where(first, mine, other), jnp.where(first, other, mine)])


def prepare_kernel(gate_ref, up_ref, down_ref, err_ref, left_hbm, both_ref, token_ref, left_ref, sem):
    hid, width = gate_ref.shape
    gate, up, down = gate_ref[...], up_ref[...], down_ref[...].astype(F32)
    block = width // (SIDE * SIDE)
    left_ref[0] = gate
    left_ref[1] = up
    left_ref[2] = jnp.concatenate(
        [down[:, (y * SIDE + x) * block : (y * SIDE + x + 1) * block] for x in range(SIDE) for y in range(SIDE)],
        axis=1,
    ).astype(BF)
    for k in range(3):
        left_ref[3 + k] = err_ref[0, k]
    copy = pltpu.make_async_copy(left_ref, left_hbm.at[pl.ds(0, 6)], sem)
    copy.start()
    both_ref[:, :hid] = gate.astype(F32).T.astype(BF)
    both_ref[:, hid:] = up.astype(F32).T.astype(BF)
    token_ref[...] = jnp.zeros_like(token_ref)
    copy.wait()


def prepare(w_gate, w_up, w_down, error_in):
    vmem = pl.BlockSpec(memory_space=pltpu.VMEM)
    hid, width = w_gate.shape
    return pl.pallas_call(
        prepare_kernel,
        out_shape=(
            jax.ShapeDtypeStruct((STORE, hid, width), BF),
            jax.ShapeDtypeStruct((width, 2 * hid), BF),
            jax.ShapeDtypeStruct((8, LANES), F32),
        ),
        in_specs=[vmem] * 4,
        out_specs=(pl.BlockSpec(memory_space=pltpu.HBM), vmem, vmem),
        scratch_shapes=[pltpu.VMEM((6, hid, width), BF), pltpu.SemaphoreType.DMA],
        compiler_params=pltpu.CompilerParams(vmem_limit_bytes=20 * MIB),
    )(w_gate, w_up, w_down, error_in)


def backward_kernel(place_ref, p0_ref, p1_ref, p2_ref, p3_ref, dy_ref, w_hbm,
                    gate_grad_ref, up_grad_ref, hidden_ref, p_out_ref, x_ref, w_ref, hidden_grad_ref, sems):
    rows = p0_ref.shape[0]
    hid, tokens = hidden_ref.shape
    chunk = 256
    loads = [pltpu.make_async_copy(w_hbm.at[k], w_ref.at[k], sems.at[k]) for k in range(6)]
    pieces = []
    for i, ref in enumerate((p0_ref, p1_ref, p2_ref, p3_ref)):
        at = pl.multiple_of(lax.rem(place_ref[0] + i, SIDE) * rows, 16)
        pieces.append(pltpu.make_async_copy(ref, x_ref.at[pl.ds(at, rows), :], sems.at[6 + i]))
    for copy in [loads[2]] + pieces + loads[:2] + loads[3:]:
        copy.start()
    q_dy = dy_ref[:, tokens : tokens + 2 * RANK]
    q_dy_rows = q_dy.astype(F32).T.astype(BF)
    loads[2].wait()
    for start in range(0, tokens, chunk):
        span = slice(start, start + chunk)
        hidden_grad_ref[:, span] = dot(w_ref[2], dy_ref[:, span], 1, 0)
    for copy in pieces + loads[:2]:
        copy.wait()
    q_x = x_ref[:, tokens:]
    q_rows = q_x.astype(F32).T.astype(BF)
    q_both = [q_rows[: 2 * RANK], q_rows[2 * RANK :], q_dy_rows]
    sums = [jnp.zeros((2 * RANK, hid), F32)] * 3
    for start in range(0, tokens, chunk):
        span = slice(start, start + chunk)
        x, dy = x_ref[:, span], dy_ref[:, span]
        gate_pre = dot(w_ref[0], x, 1, 0)
        up_pre = dot(w_ref[1], x, 1, 0)
        hidden_grad = hidden_grad_ref[:, span]
        gate_sig = jax.nn.sigmoid(gate_pre)
        gate_act = gate_pre * gate_sig
        hidden = (gate_act * up_pre).astype(BF)
        gate_grad = (hidden_grad * up_pre * gate_sig * (1.0 + gate_pre * (1.0 - gate_sig))).astype(BF)
        up_grad = (hidden_grad * gate_act).astype(BF)
        gate_grad_ref[:, span] = gate_grad
        up_grad_ref[:, span] = up_grad
        hidden_ref[:, span] = hidden
        for k, (left, right) in enumerate(((gate_grad, x), (up_grad, x), (hidden, dy))):
            both = dot(q_both[k], right, 1, 0)
            halves = jnp.concatenate(split(both[:RANK] + both[RANK:]))
            sums[k] = sums[k] + dot(halves, left, 1, 1)
    block = rows // SIDE
    q_plain = q_dy.astype(F32)
    q_plain = jnp.concatenate(
        [q_plain[(x * SIDE + y) * block : (x * SIDE + y + 1) * block] for y in range(SIDE) for x in range(SIDE)]
    ).astype(BF)
    for copy in loads[3:]:
        copy.wait()
    errors = [
        dot(w_ref[3 + k], q, 1, 0) for k, q in enumerate((q_x[:, : 2 * RANK], q_x[:, 2 * RANK :], q_plain))
    ]
    error_p = jnp.concatenate([both[:, :RANK] + both[:, RANK:] for both in errors], axis=1).T
    p = jnp.concatenate([both[:RANK] + both[RANK:] for both in sums]) + error_p
    p_out_ref[...] = p.astype(BF)


def backward(place, pieces, dy_all, weights):
    hid, width = weights.shape[1:]
    wide = dy_all.shape[1]
    tokens = wide - LANES
    vmem = pl.BlockSpec(memory_space=pltpu.VMEM)
    hbm = pl.BlockSpec(memory_space=pltpu.HBM)
    grads = jax.ShapeDtypeStruct((hid, tokens), BF)
    return pl.pallas_call(
        backward_kernel,
        out_shape=(
            grads,
            grads,
            grads,
            jax.ShapeDtypeStruct((ROWS, hid), BF),
            jax.ShapeDtypeStruct((width, wide), BF),
        ),
        in_specs=[pl.BlockSpec(memory_space=pltpu.SMEM)] + [hbm] * SIDE + [vmem, hbm],
        out_specs=(vmem,) * 5,
        scratch_shapes=[
            pltpu.VMEM((6, hid, width), BF),
            pltpu.VMEM((hid, tokens), F32),
            pltpu.SemaphoreType.DMA((6 + SIDE,)),
        ],
        compiler_params=pltpu.CompilerParams(vmem_limit_bytes=20 * MIB),
        cost_estimate=pl.CostEstimate(flops=6 * hid * width * tokens, bytes_accessed=8 * MIB, transcendentals=0),
    )(place, *pieces, dy_all, weights)


def term_kernel(place_ref, w_ref, gate_grad_ref, up_grad_ref, _, t0_ref, t1_ref, t2_ref, t3_ref, token_ref):
    grads = jnp.concatenate([gate_grad_ref[...], up_grad_ref[...]])
    rows = t0_ref.shape[0]
    for i, ref in enumerate((t0_ref, t1_ref, t2_ref, t3_ref)):
        at = pl.multiple_of(lax.rem(place_ref[0] + i, SIDE) * rows, 16)
        ref[...] = dot(w_ref[pl.ds(at, rows), :], grads, 1, 0).astype(BF)
    token_ref[...] = jnp.zeros_like(token_ref)


def terms(place, w_both, gate_grad, up_grad, other):
    vmem = pl.BlockSpec(memory_space=pltpu.VMEM)
    tokens = gate_grad.shape[1]
    width, both = w_both.shape
    out = pl.pallas_call(
        term_kernel,
        out_shape=(jax.ShapeDtypeStruct((width // SIDE, tokens), BF),) * SIDE
        + (jax.ShapeDtypeStruct((8, LANES), F32),),
        in_specs=[pl.BlockSpec(memory_space=pltpu.SMEM)] + [vmem] * 4,
        out_specs=(vmem,) * (SIDE + 1),
        compiler_params=pltpu.CompilerParams(vmem_limit_bytes=20 * MIB),
        cost_estimate=pl.CostEstimate(flops=2 * width * both * tokens, bytes_accessed=4 * MIB, transcendentals=0),
    )(place, w_both, gate_grad, up_grad, other)
    return out[:SIDE], out[SIDE]


def matrices_kernel(gate_grad_ref, up_grad_ref, hidden_ref, x_ref, dy_ref, left_hbm, _,
                    m0_ref, m1_ref, m2_ref, token_ref, left_ref, sems):
    loads = [pltpu.make_async_copy(left_hbm.at[3 + k], left_ref.at[k], sems.at[k]) for k in range(3)]
    for copy in loads:
        copy.start()
    tokens = hidden_ref.shape[1]
    x = x_ref[:, :tokens]
    m0_ref[...] = dot(gate_grad_ref[...], x, 1, 1)
    m1_ref[...] = dot(up_grad_ref[...], x, 1, 1)
    swapped = dot(hidden_ref[...], dy_ref[:, :tokens], 1, 1)
    block = swapped.shape[1] // (SIDE * SIDE)
    parts = [
        swapped[:, (x * SIDE + y) * block : (x * SIDE + y + 1) * block] for y in range(SIDE) for x in range(SIDE)
    ]
    m2_ref[...] = jnp.concatenate(parts, axis=1)
    for k, m_ref in enumerate((m0_ref, m1_ref, m2_ref)):
        loads[k].wait()
        m_ref[...] += left_ref[k].astype(F32)
    token_ref[...] = jnp.zeros_like(token_ref)


def grad_matrices(grads, x_all, dy_all, weights, other):
    vmem = pl.BlockSpec(memory_space=pltpu.VMEM)
    hid, tokens = grads[0].shape
    width = dy_all.shape[0]
    out = pl.pallas_call(
        matrices_kernel,
        out_shape=(jax.ShapeDtypeStruct((hid, width), F32),) * 3 + (jax.ShapeDtypeStruct((8, LANES), F32),),
        in_specs=[vmem] * 5 + [pl.BlockSpec(memory_space=pltpu.HBM), vmem],
        out_specs=(vmem,) * 4,
        scratch_shapes=[pltpu.VMEM((3, hid, width), BF), pltpu.SemaphoreType.DMA((3,))],
        compiler_params=pltpu.CompilerParams(vmem_limit_bytes=20 * MIB),
        cost_estimate=pl.CostEstimate(flops=6 * hid * width * tokens, bytes_accessed=9 * MIB, transcendentals=0),
    )(*grads, x_all, dy_all, weights, other)
    return out[:3], out[3]


def mean_kernel(value_ref, _, out_ref):
    total = value_ref[0].astype(F32)
    for i in range(1, value_ref.shape[0]):
        total = total + value_ref[i].astype(F32)
    out_ref[...] = total * (0.5 / value_ref.shape[0])


def mean(value, token):
    vmem = pl.BlockSpec(memory_space=pltpu.VMEM)
    return pl.pallas_call(
        mean_kernel,
        out_shape=jax.ShapeDtypeStruct(value.shape[1:], F32),
        in_specs=[vmem, pl.BlockSpec(memory_space=pl.ANY)],
        out_specs=vmem,
        compiler_params=pltpu.CompilerParams(vmem_limit_bytes=20 * MIB),
    )(value, token)


def sketch_kernel(core_ref, p_ref, m0_ref, m1_ref, m2_ref, mine_ref, theirs_ref, gram_ref):
    core = core_ref[0]
    p = p_ref[...]
    rows, grams = [], []
    for k, m_ref in enumerate((m0_ref, m1_ref, m2_ref)):
        p_k = p[k * RANK : (k + 1) * RANK]
        p_high, p_low = split(p_k)
        m_high, m_low = split(m_ref[...])
        both = dot(jnp.concatenate([p_high, p_low]), m_high, 1, 0)
        term = both[:RANK] + both[RANK:] + dot(p_high, m_low, 1, 0)
        grams.append(dot3(p_k, p_k, 1, 1))
        rows.append(jnp.concatenate([term, jnp.zeros((RANK, LANES), F32)], axis=1))
    gram = jnp.concatenate(grams)
    gram_ref[...] = jnp.concatenate([gram[i * 24 : (i + 1) * 24] for i in range(4)], axis=1)
    mine, theirs = own_half(core, jnp.concatenate(rows))
    for i in range(HALF // 8):
        for j in range(8):
            tile = (i * 8 + j) * 8
            rows, cols = slice(i * 8, i * 8 + 8), slice(j * LANES, (j + 1) * LANES)
            mine_ref[tile : tile + 8, :] = mine[rows, cols]
            theirs_ref[tile : tile + 8, :] = theirs[rows, cols]


def sketch(core, p_trans, matrices):
    vmem = pl.BlockSpec(memory_space=pltpu.VMEM)
    out = jax.ShapeDtypeStruct((TILES * 8, LANES), F32)
    return pl.pallas_call(
        sketch_kernel,
        out_shape=(out, out, jax.ShapeDtypeStruct((24, LANES), F32)),
        in_specs=[pl.BlockSpec(memory_space=pltpu.SMEM)] + [vmem] * 4,
        out_specs=(vmem,) * 3,
        compiler_params=pltpu.CompilerParams(vmem_limit_bytes=20 * MIB),
    )(core, p_trans, *matrices)


def ortho_kernel(gram_ref, inverse_ref, token_ref):
    gram = gram_ref[...]
    gram = jnp.concatenate([gram[:, i * RANK : (i + 1) * RANK] for i in range(4)])
    gram = jnp.stack([gram[k * RANK : (k + 1) * RANK] for k in range(3)])
    rows = lax.broadcasted_iota(jnp.int32, (1, RANK, RANK), 1)
    cols = lax.broadcasted_iota(jnp.int32, (1, RANK, RANK), 2)
    eye = jnp.broadcast_to(jnp.where(rows == cols, 1.0, 0.0), gram.shape)
    work = jnp.concatenate([gram, eye], axis=2)
    below = lax.broadcasted_iota(jnp.int32, (1, RANK, 1), 1)
    for k in range(RANK):
        pivot = work[:, k : k + 1, :]
        scale = 1.0 / pivot[:, :, k : k + 1]
        factor = jnp.where(below > k, work[:, :, k : k + 1] * scale, 0.0)
        work = work - factor * pivot
    diag = jnp.sum(jnp.where(rows == cols, work[:, :, :RANK], 0.0), axis=2, keepdims=True)
    inverse = work[:, :, RANK:] * lax.rsqrt(diag)
    inverse_ref[...] = inverse
    token_ref[...] = jnp.zeros_like(token_ref)


def ortho(gram):
    vmem = pl.BlockSpec(memory_space=pltpu.VMEM)
    return pl.pallas_call(
        ortho_kernel,
        out_shape=(
            jax.ShapeDtypeStruct((3, RANK, RANK), F32),
            jax.ShapeDtypeStruct((8, LANES), F32),
        ),
        in_specs=[vmem],
        out_specs=(vmem, vmem),
        cost_estimate=pl.CostEstimate(flops=MIB * 4096, bytes_accessed=MIB, transcendentals=0),
    )(gram)


def finish_kernel(place_ref, s_mine_ref, s_other_ref, inverse_ref, p_ref, m0_hbm, m1_hbm, m2_hbm,
                  error_hbm, q_ref, m_ref, error_ref, sems):
    copies = [pltpu.make_async_copy(m, m_ref.at[k], sems.at[k]) for k, m in enumerate((m0_hbm, m1_hbm, m2_hbm))]
    for copy in copies:
        copy.start()
    width = m_ref.shape[2]

    def rows_of(ref):
        return jnp.concatenate(
            [
                jnp.concatenate([ref[(i * 8 + j) * 8 : (i * 8 + j) * 8 + 8, :] for j in range(7)], axis=1)
                for i in range(HALF // 8)
            ]
        )

    s = whole(place_ref[0], rows_of(s_mine_ref), rows_of(s_other_ref))
    stores, q_rows = [], []
    for k in range(3):
        part = slice(k * RANK, (k + 1) * RANK)
        q_new = dot3(inverse_ref[k], s[part], 1, 0)
        q_rows.append(q_new)
        p_ortho = dot3(inverse_ref[k], p_ref[part, :], 1, 0)
        copies[k].wait()
        error_ref[k] = (m_ref[k] - dot3(p_ortho, q_new, 0, 0)).astype(BF)
        stores.append(pltpu.make_async_copy(error_ref.at[k], error_hbm.at[0, k], sems.at[3 + k]))
        stores[k].start()
    shard = q_ref.shape[1]
    at = place_ref[1] * shard
    q_ref[...] = pltpu.roll(jnp.concatenate(q_rows), lax.rem(width - at, width), 1)[:, :shard]
    for copy in stores:
        copy.wait()


def finish(place, s_mine, s_other, inverse, p_trans, matrices, shard):
    vmem = pl.BlockSpec(memory_space=pltpu.VMEM)
    hbm = pl.BlockSpec(memory_space=pltpu.HBM)
    hid, width = matrices[0].shape
    return pl.pallas_call(
        finish_kernel,
        out_shape=(jax.ShapeDtypeStruct((1, 3, hid, width), BF), jax.ShapeDtypeStruct((ROWS, shard), F32)),
        in_specs=[pl.BlockSpec(memory_space=pltpu.SMEM)] + [vmem] * 4 + [hbm] * 3,
        out_specs=(hbm, vmem),
        scratch_shapes=[
            pltpu.VMEM((3, hid, width), F32),
            pltpu.VMEM((3, hid, width), BF),
            pltpu.SemaphoreType.DMA((6,)),
        ],
        compiler_params=pltpu.CompilerParams(vmem_limit_bytes=20 * MIB),
    )(place, s_mine, s_other, inverse, p_trans, *matrices)


def after(values, other):
    return lax.optimization_barrier((values, other))[0]


def swap_core(value):
    return lax.ppermute(value, "dp", CORE_PAIR)


def z_swap(bit):
    return [(z * 2 + c, (z ^ bit) * 2 + c) for z in range(DEPTH) for c in range(2)]


def take_kernel(value_ref, _, out_ref):
    out_ref[...] = value_ref[...]


def take(value, token):
    vmem = pl.BlockSpec(memory_space=pltpu.VMEM)
    return pl.pallas_call(
        take_kernel,
        out_shape=jax.ShapeDtypeStruct(value.shape, value.dtype),
        in_specs=[vmem, vmem],
        out_specs=vmem,
        compiler_params=pltpu.CompilerParams(vmem_limit_bytes=20 * MIB),
    )(value, token)


def add(values, token, scale, kind=F32):
    vmem = pl.BlockSpec(memory_space=pltpu.VMEM)

    def kernel(*refs):
        refs[-1][...] = (sum(ref[...].astype(F32) for ref in refs[:-2]) * scale).astype(kind)

    return pl.pallas_call(
        kernel,
        out_shape=jax.ShapeDtypeStruct(values[0].shape, kind),
        in_specs=[vmem] * (len(values) + 1),
        out_specs=vmem,
        compiler_params=pltpu.CompilerParams(vmem_limit_bytes=20 * MIB),
    )(*values, token)


def close_kernel(*refs):
    refs[-2][...] = sum(ref[...].astype(F32) for ref in refs[:-2]).astype(BF)
    refs[-1][...] = jnp.zeros_like(refs[-1])


def close(values):
    vmem = pl.BlockSpec(memory_space=pltpu.VMEM)
    return pl.pallas_call(
        close_kernel,
        out_shape=(jax.ShapeDtypeStruct(values[0].shape, BF), jax.ShapeDtypeStruct((8, LANES), F32)),
        in_specs=[vmem] * len(values),
        out_specs=(vmem, vmem),
        compiler_params=pltpu.CompilerParams(vmem_limit_bytes=20 * MIB),
    )(*values)


def per_device(hidden_in, out_grad, w_gate, w_up, w_down, error_in, q_init):
    n_workers = lax.axis_size("dp")
    n_tensor = lax.axis_size("tensor")
    me = lax.axis_index("tensor")
    y, x = me // SIDE, me % SIDE
    core = lax.axis_index("dp") % 2
    shard = hidden_in.shape[1]

    weights, w_both, _ = prepare(w_gate, w_up, w_down, error_in)
    x_part, dy_parts = pack(hidden_in.T, out_grad.T, q_init.reshape(ROWS, shard))
    pieces, dy_all = gather_all(x_part, dy_parts, me)
    spot = jnp.stack([y, core])
    gate_grad, up_grad, hidden, p_part, x_all = backward(spot, pieces, dy_all, weights)
    core = core.reshape(1)
    p_pair = add((p_part, swap_core(p_part)), p_part, 1.0, BF)
    p_next = lax.ppermute(p_pair, "dp", z_swap(1))
    matrices, token = grad_matrices((gate_grad, up_grad, hidden), x_all, dy_all, weights, p_pair)
    p_pair = add((p_pair, p_next), token, 1.0, BF)
    p_pair = add((p_pair, lax.ppermute(p_pair, "dp", z_swap(2))), token, 1.0, BF)
    blocks, token = terms(spot, w_both, gate_grad, up_grad, p_pair)
    p_trans = add((p_pair, lax.ppermute(p_pair, "dp", z_swap(4))), token, 1.0 / n_workers)
    got = send_blocks(blocks)
    s_mine, s_theirs, gram = sketch(core, p_trans, matrices)
    s_pair = (s_mine + swap_core(s_theirs)).reshape(n_tensor, -1, LANES)
    gram = jnp.broadcast_to(gram[None], (n_tensor,) + gram.shape)
    sums = jnp.sum(lax.all_to_all(jnp.concatenate([s_pair, gram], axis=1), "tensor", 0, 0, tiled=True), axis=0)
    s_part, gram = sums[: s_pair.shape[1]], sums[s_pair.shape[1] :]
    s_all = spread(s_part, "dp", Z_GROUPS, DEPTH)
    inverse, token = ortho(gram)
    s_part = mean(s_all, token)
    got = send_parts(got, x, gram)
    input_grad, token = close(got)
    input_grad = input_grad.T
    s_half = take(spread(s_part, "tensor", None, n_tensor).reshape(-1, LANES), token)
    error_out, q_out = finish(
        jnp.stack([core[0], me]), s_half, swap_core(s_half), inverse, p_trans, matrices, shard
    )
    return (input_grad, error_out, q_out.reshape(q_init.shape))


def solution(mesh):
    in_specs = (
        P("dp", "tensor"),
        P("dp", "tensor"),
        P("tensor", None),
        P("tensor", None),
        P("tensor", None),
        P("dp", None, "tensor", None),
        P(None, None, "tensor"),
    )
    out_specs = (P("dp", "tensor"), P("dp", None, "tensor", None), P(None, None, "tensor"))
    return jax.shard_map(
        per_device, mesh=mesh, in_specs=in_specs, out_specs=out_specs, check_vma=False
    )
```

```python
import jax
import jax.numpy as jnp
from jax import lax
from jax.experimental import pallas as pl
from jax.experimental.pallas import tpu as pltpu
from jax.sharding import PartitionSpec as P

BF = jnp.bfloat16
F32 = jnp.float32
SIDE = 4
DEPTH = 8
RANK = 32
ROWS = 3 * RANK
HALF = ROWS // 2
LANES = 128
TILES = HALF * 1024 // (8 * LANES)
MIB = 1 << 20
STORE = 112

X_GROUPS = [[y * SIDE + x for x in range(SIDE)] for y in range(SIDE)]
Y_GROUPS = [[y * SIDE + x for y in range(SIDE)] for x in range(SIDE)]
CORE_PAIR = [(i, i ^ 1) for i in range(2 * DEPTH)]
Z_GROUPS = [[z * 2 + c for z in range(DEPTH)] for c in range(2)]


def x_ring(k):
    return [(y * SIDE + x, y * SIDE + (x + k) % SIDE) for y in range(SIDE) for x in range(SIDE)]


def y_ring(k):
    return [(y * SIDE + x, ((y + k) % SIDE) * SIDE + x) for y in range(SIDE) for x in range(SIDE)]


def spread(value, axis, groups, size):
    return lax.all_to_all(
        jnp.broadcast_to(value[None], (size,) + value.shape), axis, 0, 0, tiled=True, axis_index_groups=groups
    )


def ring_pieces(value, ring):
    near = [value] + [None] * 3
    for k in (1, 3, 2):
        near[k] = lax.ppermute(value, "tensor", ring(SIDE - k))
    return near


def pack_kernel(x_hbm, dy_hbm, q_hbm, x_ref, dy_ref, q_ref, sems):
    tokens = x_hbm.shape[1]
    copies = [pltpu.make_async_copy(x_hbm, x_ref.at[:, pl.ds(0, tokens)], sems.at[0])]
    for i in range(SIDE):
        copies.append(pltpu.make_async_copy(dy_hbm, dy_ref.at[i, :, pl.ds(0, tokens)], sems.at[1 + i]))
    q_load = pltpu.make_async_copy(q_hbm, q_ref, sems.at[1 + SIDE])
    for copy in [q_load] + copies:
        copy.start()
    q_load.wait()
    high, low = split(q_ref[...].T)
    both = [[half[:, k * RANK : (k + 1) * RANK] for half in (high, low)] for k in range(3)]
    x_ref[:, tokens:] = jnp.concatenate(both[0] + both[1], axis=1)
    tail = jnp.concatenate(both[2] + [jnp.zeros((high.shape[0], LANES - 2 * RANK), BF)], axis=1)
    for i in range(SIDE):
        dy_ref[i, :, tokens:] = tail
    for copy in copies:
        copy.wait()


def pack(x_part, dy_part, q_rows):
    vmem = pl.BlockSpec(memory_space=pltpu.VMEM)
    anywhere = pl.BlockSpec(memory_space=pl.ANY)
    rows, tokens = x_part.shape
    return pl.pallas_call(
        pack_kernel,
        out_shape=(
            jax.ShapeDtypeStruct((rows, tokens + LANES), BF),
            jax.ShapeDtypeStruct((SIDE, rows, tokens + LANES), BF),
        ),
        in_specs=[anywhere] * 3,
        out_specs=(vmem, vmem),
        scratch_shapes=[pltpu.VMEM(q_rows.shape, F32), pltpu.SemaphoreType.DMA((2 + SIDE,))],
        compiler_params=pltpu.CompilerParams(vmem_limit_bytes=58 * MIB),
    )(x_part, dy_part, q_rows)


def order_kernel(place_ref, p0_ref, p1_ref, p2_ref, p3_ref, out_ref, sems):
    copies = [
        pltpu.make_async_copy(ref, out_ref.at[lax.rem(place_ref[0] + i, SIDE)], sems.at[i])
        for i, ref in enumerate((p0_ref, p1_ref, p2_ref, p3_ref))
    ]
    for copy in copies:
        copy.start()
    for copy in copies:
        copy.wait()


def order(position, pieces):
    anywhere = pl.BlockSpec(memory_space=pl.ANY)
    return pl.pallas_call(
        order_kernel,
        out_shape=jax.ShapeDtypeStruct((SIDE,) + pieces[0].shape, pieces[0].dtype),
        in_specs=[pl.BlockSpec(memory_space=pltpu.SMEM)] + [anywhere] * SIDE,
        out_specs=pl.BlockSpec(memory_space=pltpu.VMEM),
        scratch_shapes=[pltpu.SemaphoreType.DMA((SIDE,))],
        compiler_params=pltpu.CompilerParams(vmem_limit_bytes=20 * MIB),
    )(position.reshape(1), *pieces)


def gather_all(x_part, dy_parts, me):
    rows = SIDE * x_part.shape[0]
    dy_col = lax.all_to_all(dy_parts, "tensor", 0, 0, tiled=True, axis_index_groups=Y_GROUPS)
    near, dy_col = lax.optimization_barrier((ring_pieces(x_part, x_ring), dy_col))
    x_row, dy_col = lax.optimization_barrier((order(me % SIDE, near), dy_col))
    dy_all = spread(dy_col, "tensor", X_GROUPS, SIDE)
    far, dy_all = lax.optimization_barrier((ring_pieces(x_row, y_ring), dy_all))
    return [p.reshape(rows, -1) for p in far], dy_all.reshape(SIDE * rows, -1)


def swap_order(value):
    blocks = value.reshape((SIDE, SIDE, -1) + value.shape[1:])
    return jnp.swapaxes(blocks, 0, 1).reshape(value.shape)


def send_blocks(blocks):
    return [blocks[0]] + [lax.ppermute(blocks[k], "tensor", y_ring(k)) for k in (1, 3, 2)]


def parts_kernel(place_ref, g0_ref, g1_ref, g2_ref, g3_ref, _, o0_ref, o1_ref, o2_ref, o3_ref):
    for k, out_ref in enumerate((o0_ref, o1_ref, o2_ref, o3_ref)):
        at = lax.rem(place_ref[0] + k, SIDE)
        total = sum(ref[at].astype(F32) for ref in (g0_ref, g1_ref, g2_ref, g3_ref))
        out_ref[...] = total.astype(out_ref.dtype)


def send_parts(got, position, token):
    vmem = pl.BlockSpec(memory_space=pltpu.VMEM)
    rows, tokens = got[0].shape
    parts = pl.pallas_call(
        parts_kernel,
        out_shape=(jax.ShapeDtypeStruct((rows // SIDE, tokens), BF),) * SIDE,
        in_specs=[pl.BlockSpec(memory_space=pltpu.SMEM)] + [vmem] * (SIDE + 1),
        out_specs=(vmem,) * SIDE,
        compiler_params=pltpu.CompilerParams(vmem_limit_bytes=20 * MIB),
    )(position.reshape(1), *[v.reshape(SIDE, -1, tokens) for v in got], token)
    return [parts[0]] + [lax.ppermute(parts[k], "tensor", x_ring(k)) for k in (1, 3, 2)]


def split(value):
    high = value.astype(BF)
    return high, (value - high.astype(F32)).astype(BF)


def dot(a, b, ca, cb):
    return lax.dot_general(a, b, (((ca,), (cb,)), ((), ())), preferred_element_type=F32)


def dot3(a, b, ca, cb):
    a_high, a_low = split(a)
    b_high, b_low = split(b)
    return dot(
        jnp.concatenate([a_high, a_high, a_low], axis=ca), jnp.concatenate([b_high, b_low, b_high], axis=cb), ca, cb
    )


def own_half(core, value):
    low, high = value[:HALF], value[HALF:]
    first = core == 0
    return jnp.where(first, low, high), jnp.where(first, high, low)


def whole(core, mine, other):
    first = core == 0
    return jnp.concatenate([jnp.where(first, mine, other), jnp.where(first, other, mine)])


def prepare_kernel(gate_ref, up_ref, down_ref, err_ref, left_hbm, both_ref, token_ref, left_ref, sem):
    hid, width = gate_ref.shape
    gate, up, down = gate_ref[...], up_ref[...], down_ref[...].astype(F32)
    block = width // (SIDE * SIDE)
    left_ref[0] = gate
    left_ref[1] = up
    left_ref[2] = jnp.concatenate(
        [down[:, (y * SIDE + x) * block : (y * SIDE + x + 1) * block] for x in range(SIDE) for y in range(SIDE)],
        axis=1,
    ).astype(BF)
    for k in range(3):
        left_ref[3 + k] = err_ref[0, k]
    copy = pltpu.make_async_copy(left_ref, left_hbm.at[pl.ds(0, 6)], sem)
    copy.start()
    both_ref[:, :hid] = gate.astype(F32).T.astype(BF)
    both_ref[:, hid:] = up.astype(F32).T.astype(BF)
    token_ref[...] = jnp.zeros_like(token_ref)
    copy.wait()


def prepare(w_gate, w_up, w_down, error_in):
    vmem = pl.BlockSpec(memory_space=pltpu.VMEM)
    hid, width = w_gate.shape
    return pl.pallas_call(
        prepare_kernel,
        out_shape=(
            jax.ShapeDtypeStruct((STORE, hid, width), BF),
            jax.ShapeDtypeStruct((width, 2 * hid), BF),
            jax.ShapeDtypeStruct((8, LANES), F32),
        ),
        in_specs=[vmem] * 4,
        out_specs=(pl.BlockSpec(memory_space=pltpu.HBM), vmem, vmem),
        scratch_shapes=[pltpu.VMEM((6, hid, width), BF), pltpu.SemaphoreType.DMA],
        compiler_params=pltpu.CompilerParams(vmem_limit_bytes=20 * MIB),
    )(w_gate, w_up, w_down, error_in)


def backward_kernel(place_ref, p0_ref, p1_ref, p2_ref, p3_ref, dy_ref, w_hbm,
                    gate_grad_ref, up_grad_ref, hidden_ref, p_out_ref, x_ref, w_ref, hidden_grad_ref, sems):
    rows = p0_ref.shape[0]
    hid, tokens = hidden_ref.shape
    chunk = 256
    loads = [pltpu.make_async_copy(w_hbm.at[k], w_ref.at[k], sems.at[k]) for k in range(6)]
    pieces = []
    for i, ref in enumerate((p0_ref, p1_ref, p2_ref, p3_ref)):
        at = pl.multiple_of(lax.rem(place_ref[0] + i, SIDE) * rows, 16)
        pieces.append(pltpu.make_async_copy(ref, x_ref.at[pl.ds(at, rows), :], sems.at[6 + i]))
    for copy in [loads[2]] + pieces + loads[:2] + loads[3:]:
        copy.start()
    q_dy = dy_ref[:, tokens : tokens + 2 * RANK]
    q_dy_rows = q_dy.astype(F32).T.astype(BF)
    loads[2].wait()
    for start in range(0, tokens, chunk):
        span = slice(start, start + chunk)
        hidden_grad_ref[:, span] = dot(w_ref[2], dy_ref[:, span], 1, 0)
    for copy in pieces + loads[:2]:
        copy.wait()
    q_x = x_ref[:, tokens:]
    q_rows = q_x.astype(F32).T.astype(BF)
    q_both = [q_rows[: 2 * RANK], q_rows[2 * RANK :], q_dy_rows]
    sums = [jnp.zeros((2 * RANK, hid), F32)] * 3
    for start in range(0, tokens, chunk):
        span = slice(start, start + chunk)
        x, dy = x_ref[:, span], dy_ref[:, span]
        gate_pre = dot(w_ref[0], x, 1, 0)
        up_pre = dot(w_ref[1], x, 1, 0)
        hidden_grad = hidden_grad_ref[:, span]
        gate_sig = jax.nn.sigmoid(gate_pre)
        gate_act = gate_pre * gate_sig
        hidden = (gate_act * up_pre).astype(BF)
        gate_grad = (hidden_grad * up_pre * gate_sig * (1.0 + gate_pre * (1.0 - gate_sig))).astype(BF)
        up_grad = (hidden_grad * gate_act).astype(BF)
        gate_grad_ref[:, span] = gate_grad
        up_grad_ref[:, span] = up_grad
        hidden_ref[:, span] = hidden
        for k, (left, right) in enumerate(((gate_grad, x), (up_grad, x), (hidden, dy))):
            both = dot(q_both[k], right, 1, 0)
            halves = jnp.concatenate(split(both[:RANK] + both[RANK:]))
            sums[k] = sums[k] + dot(halves, left, 1, 1)
    block = rows // SIDE
    q_plain = q_dy.astype(F32)
    q_plain = jnp.concatenate(
        [q_plain[(x * SIDE + y) * block : (x * SIDE + y + 1) * block] for y in range(SIDE) for x in range(SIDE)]
    ).astype(BF)
    for copy in loads[3:]:
        copy.wait()
    errors = [
        dot(w_ref[3 + k], q, 1, 0) for k, q in enumerate((q_x[:, : 2 * RANK], q_x[:, 2 * RANK :], q_plain))
    ]
    error_p = jnp.concatenate([both[:, :RANK] + both[:, RANK:] for both in errors], axis=1).T
    p = jnp.concatenate([both[:RANK] + both[RANK:] for both in sums]) + error_p
    p_out_ref[...] = p.astype(BF)


def backward(place, pieces, dy_all, weights):
    hid, width = weights.shape[1:]
    wide = dy_all.shape[1]
    tokens = wide - LANES
    vmem = pl.BlockSpec(memory_space=pltpu.VMEM)
    hbm = pl.BlockSpec(memory_space=pltpu.HBM)
    grads = jax.ShapeDtypeStruct((hid, tokens), BF)
    return pl.pallas_call(
        backward_kernel,
        out_shape=(
            grads,
            grads,
            grads,
            jax.ShapeDtypeStruct((ROWS, hid), BF),
            jax.ShapeDtypeStruct((width, wide), BF),
        ),
        in_specs=[pl.BlockSpec(memory_space=pltpu.SMEM)] + [hbm] * SIDE + [vmem, hbm],
        out_specs=(vmem,) * 5,
        scratch_shapes=[
            pltpu.VMEM((6, hid, width), BF),
            pltpu.VMEM((hid, tokens), F32),
            pltpu.SemaphoreType.DMA((6 + SIDE,)),
        ],
        compiler_params=pltpu.CompilerParams(vmem_limit_bytes=20 * MIB),
        cost_estimate=pl.CostEstimate(flops=6 * hid * width * tokens, bytes_accessed=8 * MIB, transcendentals=0),
    )(place, *pieces, dy_all, weights)


def term_kernel(place_ref, w_ref, gate_grad_ref, up_grad_ref, _, t0_ref, t1_ref, t2_ref, t3_ref, token_ref):
    grads = jnp.concatenate([gate_grad_ref[...], up_grad_ref[...]])
    rows = t0_ref.shape[0]
    for i, ref in enumerate((t0_ref, t1_ref, t2_ref, t3_ref)):
        at = pl.multiple_of(lax.rem(place_ref[0] + i, SIDE) * rows, 16)
        ref[...] = dot(w_ref[pl.ds(at, rows), :], grads, 1, 0).astype(BF)
    token_ref[...] = jnp.zeros_like(token_ref)


def terms(place, w_both, gate_grad, up_grad, other):
    vmem = pl.BlockSpec(memory_space=pltpu.VMEM)
    tokens = gate_grad.shape[1]
    width, both = w_both.shape
    out = pl.pallas_call(
        term_kernel,
        out_shape=(jax.ShapeDtypeStruct((width // SIDE, tokens), BF),) * SIDE
        + (jax.ShapeDtypeStruct((8, LANES), F32),),
        in_specs=[pl.BlockSpec(memory_space=pltpu.SMEM)] + [vmem] * 4,
        out_specs=(vmem,) * (SIDE + 1),
        compiler_params=pltpu.CompilerParams(vmem_limit_bytes=20 * MIB),
        cost_estimate=pl.CostEstimate(flops=2 * width * both * tokens, bytes_accessed=4 * MIB, transcendentals=0),
    )(place, w_both, gate_grad, up_grad, other)
    return out[:SIDE], out[SIDE]


def matrices_kernel(gate_grad_ref, up_grad_ref, hidden_ref, x_ref, dy_ref, left_hbm, _,
                    m0_ref, m1_ref, m2_ref, token_ref, left_ref, sems):
    loads = [pltpu.make_async_copy(left_hbm.at[3 + k], left_ref.at[k], sems.at[k]) for k in range(3)]
    for copy in loads:
        copy.start()
    tokens = hidden_ref.shape[1]
    x = x_ref[:, :tokens]
    m0_ref[...] = dot(gate_grad_ref[...], x, 1, 1)
    m1_ref[...] = dot(up_grad_ref[...], x, 1, 1)
    swapped = dot(hidden_ref[...], dy_ref[:, :tokens], 1, 1)
    block = swapped.shape[1] // (SIDE * SIDE)
    parts = [
        swapped[:, (x * SIDE + y) * block : (x * SIDE + y + 1) * block] for y in range(SIDE) for x in range(SIDE)
    ]
    m2_ref[...] = jnp.concatenate(parts, axis=1)
    for k, m_ref in enumerate((m0_ref, m1_ref, m2_ref)):
        loads[k].wait()
        m_ref[...] += left_ref[k].astype(F32)
    token_ref[...] = jnp.zeros_like(token_ref)


def grad_matrices(grads, x_all, dy_all, weights, other):
    vmem = pl.BlockSpec(memory_space=pltpu.VMEM)
    hid, tokens = grads[0].shape
    width = dy_all.shape[0]
    out = pl.pallas_call(
        matrices_kernel,
        out_shape=(jax.ShapeDtypeStruct((hid, width), F32),) * 3 + (jax.ShapeDtypeStruct((8, LANES), F32),),
        in_specs=[vmem] * 5 + [pl.BlockSpec(memory_space=pltpu.HBM), vmem],
        out_specs=(vmem,) * 4,
        scratch_shapes=[pltpu.VMEM((3, hid, width), BF), pltpu.SemaphoreType.DMA((3,))],
        compiler_params=pltpu.CompilerParams(vmem_limit_bytes=20 * MIB),
        cost_estimate=pl.CostEstimate(flops=6 * hid * width * tokens, bytes_accessed=9 * MIB, transcendentals=0),
    )(*grads, x_all, dy_all, weights, other)
    return out[:3], out[3]


def mean_kernel(value_ref, _, out_ref):
    total = value_ref[0].astype(F32)
    for i in range(1, value_ref.shape[0]):
        total = total + value_ref[i].astype(F32)
    out_ref[...] = total * (0.5 / value_ref.shape[0])


def mean(value, token):
    vmem = pl.BlockSpec(memory_space=pltpu.VMEM)
    return pl.pallas_call(
        mean_kernel,
        out_shape=jax.ShapeDtypeStruct(value.shape[1:], F32),
        in_specs=[vmem, pl.BlockSpec(memory_space=pl.ANY)],
        out_specs=vmem,
        compiler_params=pltpu.CompilerParams(vmem_limit_bytes=20 * MIB),
    )(value, token)


def sketch_kernel(core_ref, p_ref, m0_ref, m1_ref, m2_ref, mine_ref, theirs_ref, gram_ref):
    core = core_ref[0]
    p = p_ref[...]
    rows, grams = [], []
    for k, m_ref in enumerate((m0_ref, m1_ref, m2_ref)):
        p_k = p[k * RANK : (k + 1) * RANK]
        p_high, p_low = split(p_k)
        m_high, m_low = split(m_ref[...])
        both = dot(jnp.concatenate([p_high, p_low]), m_high, 1, 0)
        term = both[:RANK] + both[RANK:] + dot(p_high, m_low, 1, 0)
        grams.append(dot3(p_k, p_k, 1, 1))
        rows.append(jnp.concatenate([term, jnp.zeros((RANK, LANES), F32)], axis=1))
    gram = jnp.concatenate(grams)
    gram_ref[...] = jnp.concatenate([gram[i * 24 : (i + 1) * 24] for i in range(4)], axis=1)
    mine, theirs = own_half(core, jnp.concatenate(rows))
    for i in range(HALF // 8):
        for j in range(8):
            tile = (i * 8 + j) * 8
            rows, cols = slice(i * 8, i * 8 + 8), slice(j * LANES, (j + 1) * LANES)
            mine_ref[tile : tile + 8, :] = mine[rows, cols]
            theirs_ref[tile : tile + 8, :] = theirs[rows, cols]


def sketch(core, p_trans, matrices):
    vmem = pl.BlockSpec(memory_space=pltpu.VMEM)
    out = jax.ShapeDtypeStruct((TILES * 8, LANES), F32)
    return pl.pallas_call(
        sketch_kernel,
        out_shape=(out, out, jax.ShapeDtypeStruct((24, LANES), F32)),
        in_specs=[pl.BlockSpec(memory_space=pltpu.SMEM)] + [vmem] * 4,
        out_specs=(vmem,) * 3,
        compiler_params=pltpu.CompilerParams(vmem_limit_bytes=20 * MIB),
    )(core, p_trans, *matrices)


def ortho_kernel(gram_ref, inverse_ref, token_ref):
    gram = gram_ref[...]
    gram = jnp.concatenate([gram[:, i * RANK : (i + 1) * RANK] for i in range(4)])
    gram = jnp.stack([gram[k * RANK : (k + 1) * RANK] for k in range(3)])
    rows = lax.broadcasted_iota(jnp.int32, (1, RANK, RANK), 1)
    cols = lax.broadcasted_iota(jnp.int32, (1, RANK, RANK), 2)
    eye = jnp.broadcast_to(jnp.where(rows == cols, 1.0, 0.0), gram.shape)
    work = jnp.concatenate([gram, eye], axis=2)
    below = lax.broadcasted_iota(jnp.int32, (1, RANK, 1), 1)
    for k in range(RANK):
        pivot = work[:, k : k + 1, :]
        scale = 1.0 / pivot[:, :, k : k + 1]
        factor = jnp.where(below > k, work[:, :, k : k + 1] * scale, 0.0)
        work = work - factor * pivot
    diag = jnp.sum(jnp.where(rows == cols, work[:, :, :RANK], 0.0), axis=2, keepdims=True)
    inverse = work[:, :, RANK:] * lax.rsqrt(diag)
    inverse_ref[...] = inverse
    token_ref[...] = jnp.zeros_like(token_ref)


def ortho(gram):
    vmem = pl.BlockSpec(memory_space=pltpu.VMEM)
    return pl.pallas_call(
        ortho_kernel,
        out_shape=(
            jax.ShapeDtypeStruct((3, RANK, RANK), F32),
            jax.ShapeDtypeStruct((8, LANES), F32),
        ),
        in_specs=[vmem],
        out_specs=(vmem, vmem),
        cost_estimate=pl.CostEstimate(flops=MIB * 4096, bytes_accessed=MIB, transcendentals=0),
    )(gram)


def finish_kernel(place_ref, s_mine_ref, s_other_ref, inverse_ref, p_ref, m0_ref, m1_ref, m2_ref,
                  error_hbm, q_ref, error_ref, sems):
    m_refs = (m0_ref, m1_ref, m2_ref)
    width = m0_ref.shape[1]

    def rows_of(ref):
        return jnp.concatenate(
            [
                jnp.concatenate([ref[(i * 8 + j) * 8 : (i * 8 + j) * 8 + 8, :] for j in range(7)], axis=1)
                for i in range(HALF // 8)
            ]
        )

    s = whole(place_ref[0], rows_of(s_mine_ref), rows_of(s_other_ref))
    stores, q_rows = [], []
    for k in range(3):
        part = slice(k * RANK, (k + 1) * RANK)
        q_new = dot3(inverse_ref[k], s[part], 1, 0)
        q_rows.append(q_new)
        p_ortho = dot3(inverse_ref[k], p_ref[part, :], 1, 0)
        error_ref[k] = (m_refs[k][...] - dot3(p_ortho, q_new, 0, 0)).astype(BF)
        stores.append(pltpu.make_async_copy(error_ref.at[k], error_hbm.at[0, k], sems.at[k]))
        stores[k].start()
    shard = q_ref.shape[1]
    at = place_ref[1] * shard
    q_ref[...] = pltpu.roll(jnp.concatenate(q_rows), lax.rem(width - at, width), 1)[:, :shard]
    for copy in stores:
        copy.wait()


def finish(place, s_mine, s_other, inverse, p_trans, matrices, shard):
    vmem = pl.BlockSpec(memory_space=pltpu.VMEM)
    hbm = pl.BlockSpec(memory_space=pltpu.HBM)
    hid, width = matrices[0].shape
    return pl.pallas_call(
        finish_kernel,
        out_shape=(jax.ShapeDtypeStruct((1, 3, hid, width), BF), jax.ShapeDtypeStruct((ROWS, shard), F32)),
        in_specs=[pl.BlockSpec(memory_space=pltpu.SMEM)] + [vmem] * 7,
        out_specs=(hbm, vmem),
        scratch_shapes=[
            pltpu.VMEM((3, hid, width), BF),
            pltpu.SemaphoreType.DMA((3,)),
        ],
        compiler_params=pltpu.CompilerParams(vmem_limit_bytes=20 * MIB),
    )(place, s_mine, s_other, inverse, p_trans, *matrices)


def after(values, other):
    return lax.optimization_barrier((values, other))[0]


def swap_core(value):
    return lax.ppermute(value, "dp", CORE_PAIR)


def dp_swap(bits):
    return [(i, i ^ bits) for i in range(2 * DEPTH)]


def take_kernel(value_ref, _, out_ref):
    out_ref[...] = value_ref[...]


def take(value, token):
    vmem = pl.BlockSpec(memory_space=pltpu.VMEM)
    return pl.pallas_call(
        take_kernel,
        out_shape=jax.ShapeDtypeStruct(value.shape, value.dtype),
        in_specs=[vmem, vmem],
        out_specs=vmem,
        compiler_params=pltpu.CompilerParams(vmem_limit_bytes=20 * MIB),
    )(value, token)


def add(values, token, scale, kind=F32):
    vmem = pl.BlockSpec(memory_space=pltpu.VMEM)

    def kernel(*refs):
        terms = [ref[...].astype(F32) for ref in refs[:-2]]
        while len(terms) > 1:
            terms = [terms[i] + terms[i + 1] for i in range(0, len(terms), 2)]
        refs[-1][...] = (terms[0] * scale).astype(kind)

    return pl.pallas_call(
        kernel,
        out_shape=jax.ShapeDtypeStruct(values[0].shape, kind),
        in_specs=[vmem] * (len(values) + 1),
        out_specs=vmem,
        compiler_params=pltpu.CompilerParams(vmem_limit_bytes=20 * MIB),
    )(*values, token)


def close_kernel(*refs):
    refs[-2][...] = sum(ref[...].astype(F32) for ref in refs[:-2]).astype(BF)
    refs[-1][...] = jnp.zeros_like(refs[-1])


def close(values):
    vmem = pl.BlockSpec(memory_space=pltpu.VMEM)
    return pl.pallas_call(
        close_kernel,
        out_shape=(jax.ShapeDtypeStruct(values[0].shape, BF), jax.ShapeDtypeStruct((8, LANES), F32)),
        in_specs=[vmem] * len(values),
        out_specs=(vmem, vmem),
        compiler_params=pltpu.CompilerParams(vmem_limit_bytes=20 * MIB),
    )(*values)


def per_device(hidden_in, out_grad, w_gate, w_up, w_down, error_in, q_init):
    n_workers = lax.axis_size("dp")
    n_tensor = lax.axis_size("tensor")
    me = lax.axis_index("tensor")
    y, x = me // SIDE, me % SIDE
    core = lax.axis_index("dp") % 2
    shard = hidden_in.shape[1]

    weights, w_both, _ = prepare(w_gate, w_up, w_down, error_in)
    x_part, dy_parts = pack(hidden_in.T, out_grad.T, q_init.reshape(ROWS, shard))
    pieces, dy_all = gather_all(x_part, dy_parts, me)
    spot = jnp.stack([y, core])
    gate_grad, up_grad, hidden, p_part, x_all = backward(spot, pieces, dy_all, weights)
    core = core.reshape(1)
    near = [p_part] + [lax.ppermute(p_part, "dp", dp_swap(bits)) for bits in (1, 2, 3)]
    matrices, token = grad_matrices((gate_grad, up_grad, hidden), x_all, dy_all, weights, p_part)
    p_pair = add(near, token, 1.0, BF)
    blocks, token = terms(spot, w_both, gate_grad, up_grad, p_pair)
    others = [lax.ppermute(p_pair, "dp", dp_swap(bits)) for bits in (4, 12, 10)]
    p_trans = add([p_pair] + others, token, 1.0 / n_workers)
    got = send_blocks(blocks)
    s_mine, s_theirs, gram = sketch(core, p_trans, matrices)
    s_pair = (s_mine + swap_core(s_theirs)).reshape(n_tensor, -1, LANES)
    gram = jnp.broadcast_to(gram[None], (n_tensor,) + gram.shape)
    sums = jnp.sum(lax.all_to_all(jnp.concatenate([s_pair, gram], axis=1), "tensor", 0, 0, tiled=True), axis=0)
    s_part, gram = sums[: s_pair.shape[1]], sums[s_pair.shape[1] :]
    s_all = spread(s_part, "dp", Z_GROUPS, DEPTH)
    inverse, token = ortho(gram)
    s_part = mean(s_all, token)
    got = send_parts(got, x, gram)
    input_grad, token = close(got)
    input_grad = input_grad.T
    s_half = take(spread(s_part, "tensor", None, n_tensor).reshape(-1, LANES), token)
    error_out, q_out = finish(
        jnp.stack([core[0], me]), s_half, swap_core(s_half), inverse, p_trans, matrices, shard
    )
    return (input_grad, error_out, q_out.reshape(q_init.shape))


def solution(mesh):
    in_specs = (
        P("dp", "tensor"),
        P("dp", "tensor"),
        P("tensor", None),
        P("tensor", None),
        P("tensor", None),
        P("dp", None, "tensor", None),
        P(None, None, "tensor"),
    )
    out_specs = (P("dp", "tensor"), P("dp", None, "tensor", None), P(None, None, "tensor"))
    return jax.shard_map(
        per_device, mesh=mesh, in_specs=in_specs, out_specs=out_specs, check_vma=False
    )
```

```python
import jax
import jax.numpy as jnp
from jax import lax
from jax.experimental import pallas as pl
from jax.experimental.pallas import tpu as pltpu
from jax.sharding import PartitionSpec as P

BF = jnp.bfloat16
F32 = jnp.float32
SIDE = 4
DEPTH = 8
RANK = 32
ROWS = 3 * RANK
HALF = ROWS // 2
LANES = 128
TILES = HALF * 1024 // (8 * LANES)
MIB = 1 << 20
STORE = 112

X_GROUPS = [[y * SIDE + x for x in range(SIDE)] for y in range(SIDE)]
Y_GROUPS = [[y * SIDE + x for y in range(SIDE)] for x in range(SIDE)]
CORE_PAIR = [(i, i ^ 1) for i in range(2 * DEPTH)]
Z_GROUPS = [[z * 2 + c for z in range(DEPTH)] for c in range(2)]


def x_ring(k):
    return [(y * SIDE + x, y * SIDE + (x + k) % SIDE) for y in range(SIDE) for x in range(SIDE)]


def y_ring(k):
    return [(y * SIDE + x, ((y + k) % SIDE) * SIDE + x) for y in range(SIDE) for x in range(SIDE)]


def spread(value, axis, groups, size):
    return lax.all_to_all(
        jnp.broadcast_to(value[None], (size,) + value.shape), axis, 0, 0, tiled=True, axis_index_groups=groups
    )


def ring_pieces(value, ring):
    near = [value] + [None] * 3
    for k in (1, 3, 2):
        near[k] = lax.ppermute(value, "tensor", ring(SIDE - k))
    return near


def pack_kernel(x_hbm, dy_hbm, q_hbm, x_ref, dy_ref, q_ref, sems):
    tokens = x_hbm.shape[1]
    copies = [pltpu.make_async_copy(x_hbm, x_ref.at[:, pl.ds(0, tokens)], sems.at[0])]
    for i in range(SIDE):
        copies.append(pltpu.make_async_copy(dy_hbm, dy_ref.at[i, :, pl.ds(0, tokens)], sems.at[1 + i]))
    q_load = pltpu.make_async_copy(q_hbm, q_ref, sems.at[1 + SIDE])
    for copy in [q_load] + copies:
        copy.start()
    q_load.wait()
    high, low = split(q_ref[...].T)
    both = [[half[:, k * RANK : (k + 1) * RANK] for half in (high, low)] for k in range(3)]
    x_ref[:, tokens:] = jnp.concatenate(both[0] + both[1], axis=1)
    tail = jnp.concatenate(both[2] + [jnp.zeros((high.shape[0], LANES - 2 * RANK), BF)], axis=1)
    for i in range(SIDE):
        dy_ref[i, :, tokens:] = tail
    for copy in copies:
        copy.wait()


def pack(x_part, dy_part, q_rows):
    vmem = pl.BlockSpec(memory_space=pltpu.VMEM)
    anywhere = pl.BlockSpec(memory_space=pl.ANY)
    rows, tokens = x_part.shape
    return pl.pallas_call(
        pack_kernel,
        out_shape=(
            jax.ShapeDtypeStruct((rows, tokens + LANES), BF),
            jax.ShapeDtypeStruct((SIDE, rows, tokens + LANES), BF),
        ),
        in_specs=[anywhere] * 3,
        out_specs=(vmem, vmem),
        scratch_shapes=[pltpu.VMEM(q_rows.shape, F32), pltpu.SemaphoreType.DMA((2 + SIDE,))],
        compiler_params=pltpu.CompilerParams(vmem_limit_bytes=58 * MIB),
    )(x_part, dy_part, q_rows)


def order_kernel(place_ref, p0_ref, p1_ref, p2_ref, p3_ref, out_ref, sems):
    copies = [
        pltpu.make_async_copy(ref, out_ref.at[lax.rem(place_ref[0] + i, SIDE)], sems.at[i])
        for i, ref in enumerate((p0_ref, p1_ref, p2_ref, p3_ref))
    ]
    for copy in copies:
        copy.start()
    for copy in copies:
        copy.wait()


def order(position, pieces):
    anywhere = pl.BlockSpec(memory_space=pl.ANY)
    return pl.pallas_call(
        order_kernel,
        out_shape=jax.ShapeDtypeStruct((SIDE,) + pieces[0].shape, pieces[0].dtype),
        in_specs=[pl.BlockSpec(memory_space=pltpu.SMEM)] + [anywhere] * SIDE,
        out_specs=pl.BlockSpec(memory_space=pltpu.VMEM),
        scratch_shapes=[pltpu.SemaphoreType.DMA((SIDE,))],
        compiler_params=pltpu.CompilerParams(vmem_limit_bytes=20 * MIB),
    )(position.reshape(1), *pieces)


def gather_all(x_part, dy_parts, me):
    rows = SIDE * x_part.shape[0]
    dy_col = lax.all_to_all(dy_parts, "tensor", 0, 0, tiled=True, axis_index_groups=Y_GROUPS)
    near, dy_col = lax.optimization_barrier((ring_pieces(x_part, x_ring), dy_col))
    x_row, dy_col = lax.optimization_barrier((order(me % SIDE, near), dy_col))
    dy_all = spread(dy_col, "tensor", X_GROUPS, SIDE)
    far, dy_all = lax.optimization_barrier((ring_pieces(x_row, y_ring), dy_all))
    return [p.reshape(rows, -1) for p in far], dy_all.reshape(SIDE * rows, -1)


def swap_order(value):
    blocks = value.reshape((SIDE, SIDE, -1) + value.shape[1:])
    return jnp.swapaxes(blocks, 0, 1).reshape(value.shape)


def send_blocks(blocks):
    return [blocks[0]] + [lax.ppermute(blocks[k], "tensor", y_ring(k)) for k in (1, 3, 2)]


def parts_kernel(place_ref, g0_ref, g1_ref, g2_ref, g3_ref, _, o0_ref, o1_ref, o2_ref, o3_ref):
    for k, out_ref in enumerate((o0_ref, o1_ref, o2_ref, o3_ref)):
        at = lax.rem(place_ref[0] + k, SIDE)
        total = sum(ref[at].astype(F32) for ref in (g0_ref, g1_ref, g2_ref, g3_ref))
        out_ref[...] = total.astype(out_ref.dtype)


def send_parts(got, position, token):
    vmem = pl.BlockSpec(memory_space=pltpu.VMEM)
    rows, tokens = got[0].shape
    parts = pl.pallas_call(
        parts_kernel,
        out_shape=(jax.ShapeDtypeStruct((rows // SIDE, tokens), BF),) * SIDE,
        in_specs=[pl.BlockSpec(memory_space=pltpu.SMEM)] + [vmem] * (SIDE + 1),
        out_specs=(vmem,) * SIDE,
        compiler_params=pltpu.CompilerParams(vmem_limit_bytes=20 * MIB),
    )(position.reshape(1), *[v.reshape(SIDE, -1, tokens) for v in got], token)
    return [parts[0]] + [lax.ppermute(parts[k], "tensor", x_ring(k)) for k in (1, 3, 2)]


def split(value):
    high = value.astype(BF)
    return high, (value - high.astype(F32)).astype(BF)


def dot(a, b, ca, cb):
    return lax.dot_general(a, b, (((ca,), (cb,)), ((), ())), preferred_element_type=F32)


def dot3(a, b, ca, cb):
    a_high, a_low = split(a)
    b_high, b_low = split(b)
    return dot(
        jnp.concatenate([a_high, a_high, a_low], axis=ca), jnp.concatenate([b_high, b_low, b_high], axis=cb), ca, cb
    )


def own_half(core, value):
    low, high = value[:HALF], value[HALF:]
    first = core == 0
    return jnp.where(first, low, high), jnp.where(first, high, low)


def whole(core, mine, other):
    first = core == 0
    return jnp.concatenate([jnp.where(first, mine, other), jnp.where(first, other, mine)])


def prepare_kernel(gate_ref, up_ref, down_ref, err_ref, left_hbm, both_ref, token_ref, left_ref, sem):
    hid, width = gate_ref.shape
    gate, up, down = gate_ref[...], up_ref[...], down_ref[...].astype(F32)
    block = width // (SIDE * SIDE)
    left_ref[0] = gate
    left_ref[1] = up
    left_ref[2] = jnp.concatenate(
        [down[:, (y * SIDE + x) * block : (y * SIDE + x + 1) * block] for x in range(SIDE) for y in range(SIDE)],
        axis=1,
    ).astype(BF)
    for k in range(3):
        left_ref[3 + k] = err_ref[0, k]
    copy = pltpu.make_async_copy(left_ref, left_hbm.at[pl.ds(0, 6)], sem)
    copy.start()
    both_ref[:, :hid] = gate.astype(F32).T.astype(BF)
    both_ref[:, hid:] = up.astype(F32).T.astype(BF)
    token_ref[...] = jnp.zeros_like(token_ref)
    copy.wait()


def prepare(w_gate, w_up, w_down, error_in):
    vmem = pl.BlockSpec(memory_space=pltpu.VMEM)
    hid, width = w_gate.shape
    return pl.pallas_call(
        prepare_kernel,
        out_shape=(
            jax.ShapeDtypeStruct((STORE, hid, width), BF),
            jax.ShapeDtypeStruct((width, 2 * hid), BF),
            jax.ShapeDtypeStruct((8, LANES), F32),
        ),
        in_specs=[vmem] * 4,
        out_specs=(pl.BlockSpec(memory_space=pltpu.HBM), vmem, vmem),
        scratch_shapes=[pltpu.VMEM((6, hid, width), BF), pltpu.SemaphoreType.DMA],
        compiler_params=pltpu.CompilerParams(vmem_limit_bytes=20 * MIB),
    )(w_gate, w_up, w_down, error_in)


def backward_kernel(place_ref, p0_ref, p1_ref, p2_ref, p3_ref, dy_ref, w_hbm,
                    gate_grad_ref, up_grad_ref, hidden_ref, p_out_ref, x_ref, w_ref, hidden_grad_ref, sems):
    rows = p0_ref.shape[0]
    hid, tokens = hidden_ref.shape
    chunk = 256
    loads = [pltpu.make_async_copy(w_hbm.at[k], w_ref.at[k], sems.at[k]) for k in range(6)]
    pieces = []
    for i, ref in enumerate((p0_ref, p1_ref, p2_ref, p3_ref)):
        at = pl.multiple_of(lax.rem(place_ref[0] + i, SIDE) * rows, 16)
        pieces.append(pltpu.make_async_copy(ref, x_ref.at[pl.ds(at, rows), :], sems.at[6 + i]))
    for copy in [loads[2], loads[5]] + pieces + loads[:2] + loads[3:5]:
        copy.start()
    q_dy = dy_ref[:, tokens : tokens + 2 * RANK]
    q_dy_rows = q_dy.astype(F32).T.astype(BF)
    loads[2].wait()
    for start in range(0, tokens, chunk):
        span = slice(start, start + chunk)
        hidden_grad_ref[:, span] = dot(w_ref[2], dy_ref[:, span], 1, 0)
    block = rows // SIDE
    q_plain = q_dy.astype(F32)
    q_plain = jnp.concatenate(
        [q_plain[(x * SIDE + y) * block : (x * SIDE + y + 1) * block] for y in range(SIDE) for x in range(SIDE)]
    ).astype(BF)
    loads[5].wait()
    last_error = dot(w_ref[5], q_plain, 1, 0)
    for copy in pieces + loads[:2]:
        copy.wait()
    q_x = x_ref[:, tokens:]
    q_rows = q_x.astype(F32).T.astype(BF)
    q_both = [q_rows[: 2 * RANK], q_rows[2 * RANK :], q_dy_rows]
    sums = [jnp.zeros((2 * RANK, hid), F32)] * 3
    for start in range(0, tokens, chunk):
        span = slice(start, start + chunk)
        x, dy = x_ref[:, span], dy_ref[:, span]
        gate_pre = dot(w_ref[0], x, 1, 0)
        up_pre = dot(w_ref[1], x, 1, 0)
        hidden_grad = hidden_grad_ref[:, span]
        gate_sig = jax.nn.sigmoid(gate_pre)
        gate_act = gate_pre * gate_sig
        hidden = (gate_act * up_pre).astype(BF)
        gate_grad = (hidden_grad * up_pre * gate_sig * (1.0 + gate_pre * (1.0 - gate_sig))).astype(BF)
        up_grad = (hidden_grad * gate_act).astype(BF)
        gate_grad_ref[:, span] = gate_grad
        up_grad_ref[:, span] = up_grad
        hidden_ref[:, span] = hidden
        for k, (left, right) in enumerate(((gate_grad, x), (up_grad, x), (hidden, dy))):
            both = dot(q_both[k], right, 1, 0)
            halves = jnp.concatenate(split(both[:RANK] + both[RANK:]))
            sums[k] = sums[k] + dot(halves, left, 1, 1)
    for copy in loads[3:5]:
        copy.wait()
    errors = [dot(w_ref[3 + k], q_x[:, 2 * k * RANK : 2 * (k + 1) * RANK], 1, 0) for k in range(2)] + [last_error]
    error_p = jnp.concatenate([both[:, :RANK] + both[:, RANK:] for both in errors], axis=1).T
    p = jnp.concatenate([both[:RANK] + both[RANK:] for both in sums]) + error_p
    p_out_ref[...] = p.astype(BF)


def backward(place, pieces, dy_all, weights):
    hid, width = weights.shape[1:]
    wide = dy_all.shape[1]
    tokens = wide - LANES
    vmem = pl.BlockSpec(memory_space=pltpu.VMEM)
    hbm = pl.BlockSpec(memory_space=pltpu.HBM)
    grads = jax.ShapeDtypeStruct((hid, tokens), BF)
    return pl.pallas_call(
        backward_kernel,
        out_shape=(
            grads,
            grads,
            grads,
            jax.ShapeDtypeStruct((ROWS, hid), BF),
            jax.ShapeDtypeStruct((width, wide), BF),
        ),
        in_specs=[pl.BlockSpec(memory_space=pltpu.SMEM)] + [hbm] * SIDE + [vmem, hbm],
        out_specs=(vmem,) * 5,
        scratch_shapes=[
            pltpu.VMEM((6, hid, width), BF),
            pltpu.VMEM((hid, tokens), F32),
            pltpu.SemaphoreType.DMA((6 + SIDE,)),
        ],
        compiler_params=pltpu.CompilerParams(vmem_limit_bytes=20 * MIB),
        cost_estimate=pl.CostEstimate(flops=6 * hid * width * tokens, bytes_accessed=8 * MIB, transcendentals=0),
    )(place, *pieces, dy_all, weights)


def term_kernel(place_ref, w_ref, gate_grad_ref, up_grad_ref, _, t0_ref, t1_ref, t2_ref, t3_ref, token_ref):
    grads = jnp.concatenate([gate_grad_ref[...], up_grad_ref[...]])
    rows = t0_ref.shape[0]
    for i, ref in enumerate((t0_ref, t1_ref, t2_ref, t3_ref)):
        at = pl.multiple_of(lax.rem(place_ref[0] + i, SIDE) * rows, 16)
        ref[...] = dot(w_ref[pl.ds(at, rows), :], grads, 1, 0).astype(BF)
    token_ref[...] = jnp.zeros_like(token_ref)


def terms(place, w_both, gate_grad, up_grad, other):
    vmem = pl.BlockSpec(memory_space=pltpu.VMEM)
    tokens = gate_grad.shape[1]
    width, both = w_both.shape
    out = pl.pallas_call(
        term_kernel,
        out_shape=(jax.ShapeDtypeStruct((width // SIDE, tokens), BF),) * SIDE
        + (jax.ShapeDtypeStruct((8, LANES), F32),),
        in_specs=[pl.BlockSpec(memory_space=pltpu.SMEM)] + [vmem] * 4,
        out_specs=(vmem,) * (SIDE + 1),
        compiler_params=pltpu.CompilerParams(vmem_limit_bytes=20 * MIB),
        cost_estimate=pl.CostEstimate(flops=2 * width * both * tokens, bytes_accessed=4 * MIB, transcendentals=0),
    )(place, w_both, gate_grad, up_grad, other)
    return out[:SIDE], out[SIDE]


def matrices_kernel(gate_grad_ref, up_grad_ref, hidden_ref, x_ref, dy_ref, left_hbm, _,
                    m0_ref, m1_ref, m2_ref, token_ref, left_ref, sems):
    loads = [pltpu.make_async_copy(left_hbm.at[3 + k], left_ref.at[k], sems.at[k]) for k in range(3)]
    for copy in loads:
        copy.start()
    tokens = hidden_ref.shape[1]
    x = x_ref[:, :tokens]
    m0_ref[...] = dot(gate_grad_ref[...], x, 1, 1)
    m1_ref[...] = dot(up_grad_ref[...], x, 1, 1)
    swapped = dot(hidden_ref[...], dy_ref[:, :tokens], 1, 1)
    block = swapped.shape[1] // (SIDE * SIDE)
    parts = [
        swapped[:, (x * SIDE + y) * block : (x * SIDE + y + 1) * block] for y in range(SIDE) for x in range(SIDE)
    ]
    m2_ref[...] = jnp.concatenate(parts, axis=1)
    for k, m_ref in enumerate((m0_ref, m1_ref, m2_ref)):
        loads[k].wait()
        m_ref[...] += left_ref[k].astype(F32)
    token_ref[...] = jnp.zeros_like(token_ref)


def grad_matrices(grads, x_all, dy_all, weights, other):
    vmem = pl.BlockSpec(memory_space=pltpu.VMEM)
    hid, tokens = grads[0].shape
    width = dy_all.shape[0]
    out = pl.pallas_call(
        matrices_kernel,
        out_shape=(jax.ShapeDtypeStruct((hid, width), F32),) * 3 + (jax.ShapeDtypeStruct((8, LANES), F32),),
        in_specs=[vmem] * 5 + [pl.BlockSpec(memory_space=pltpu.HBM), vmem],
        out_specs=(vmem,) * 4,
        scratch_shapes=[pltpu.VMEM((3, hid, width), BF), pltpu.SemaphoreType.DMA((3,))],
        compiler_params=pltpu.CompilerParams(vmem_limit_bytes=20 * MIB),
        cost_estimate=pl.CostEstimate(flops=6 * hid * width * tokens, bytes_accessed=9 * MIB, transcendentals=0),
    )(*grads, x_all, dy_all, weights, other)
    return out[:3], out[3]


def mean_kernel(value_ref, _, out_ref):
    total = value_ref[0].astype(F32)
    for i in range(1, value_ref.shape[0]):
        total = total + value_ref[i].astype(F32)
    out_ref[...] = total * (0.5 / value_ref.shape[0])


def mean(value, token):
    vmem = pl.BlockSpec(memory_space=pltpu.VMEM)
    return pl.pallas_call(
        mean_kernel,
        out_shape=jax.ShapeDtypeStruct(value.shape[1:], F32),
        in_specs=[vmem, pl.BlockSpec(memory_space=pl.ANY)],
        out_specs=vmem,
        compiler_params=pltpu.CompilerParams(vmem_limit_bytes=20 * MIB),
    )(value, token)


def sketch_kernel(core_ref, p_ref, m0_ref, m1_ref, m2_ref, mine_ref, theirs_ref, gram_ref):
    core = core_ref[0]
    p = p_ref[...]
    rows, grams = [], []
    for k, m_ref in enumerate((m0_ref, m1_ref, m2_ref)):
        p_k = p[k * RANK : (k + 1) * RANK]
        p_high, p_low = split(p_k)
        m_high, m_low = split(m_ref[...])
        both = dot(jnp.concatenate([p_high, p_low]), m_high, 1, 0)
        term = both[:RANK] + both[RANK:] + dot(p_high, m_low, 1, 0)
        grams.append(
            lax.dot_general(
                p_k, p_k, (((1,), (1,)), ((), ())), precision=lax.Precision.HIGHEST, preferred_element_type=F32
            )
        )
        rows.append(jnp.concatenate([term, jnp.zeros((RANK, LANES), F32)], axis=1))
    gram = jnp.concatenate(grams)
    gram_ref[...] = jnp.concatenate([gram[i * 24 : (i + 1) * 24] for i in range(4)], axis=1)
    mine, theirs = own_half(core, jnp.concatenate(rows))
    for i in range(HALF // 8):
        for j in range(8):
            tile = (i * 8 + j) * 8
            rows, cols = slice(i * 8, i * 8 + 8), slice(j * LANES, (j + 1) * LANES)
            mine_ref[tile : tile + 8, :] = mine[rows, cols]
            theirs_ref[tile : tile + 8, :] = theirs[rows, cols]


def sketch(core, p_trans, matrices):
    vmem = pl.BlockSpec(memory_space=pltpu.VMEM)
    out = jax.ShapeDtypeStruct((TILES * 8, LANES), F32)
    return pl.pallas_call(
        sketch_kernel,
        out_shape=(out, out, jax.ShapeDtypeStruct((24, LANES), F32)),
        in_specs=[pl.BlockSpec(memory_space=pltpu.SMEM)] + [vmem] * 4,
        out_specs=(vmem,) * 3,
        compiler_params=pltpu.CompilerParams(vmem_limit_bytes=20 * MIB),
    )(core, p_trans, *matrices)


def ortho_kernel(gram_ref, inverse_ref, token_ref):
    gram = gram_ref[...]
    gram = jnp.concatenate([gram[:, i * RANK : (i + 1) * RANK] for i in range(4)])
    gram = jnp.stack([gram[k * RANK : (k + 1) * RANK] for k in range(3)])
    rows = lax.broadcasted_iota(jnp.int32, (1, RANK, RANK), 1)
    cols = lax.broadcasted_iota(jnp.int32, (1, RANK, RANK), 2)
    eye = jnp.broadcast_to(jnp.where(rows == cols, 1.0, 0.0), gram.shape)
    work = jnp.concatenate([gram, eye], axis=2)
    below = lax.broadcasted_iota(jnp.int32, (1, RANK, 1), 1)
    for k in range(RANK):
        pivot = work[:, k : k + 1, :]
        scale = 1.0 / pivot[:, :, k : k + 1]
        factor = jnp.where(below > k, work[:, :, k : k + 1] * scale, 0.0)
        work = work - factor * pivot
    diag = jnp.sum(jnp.where(rows == cols, work[:, :, :RANK], 0.0), axis=2, keepdims=True)
    inverse = work[:, :, RANK:] * lax.rsqrt(diag)
    inverse_ref[...] = inverse
    token_ref[...] = jnp.zeros_like(token_ref)


def ortho(gram):
    vmem = pl.BlockSpec(memory_space=pltpu.VMEM)
    return pl.pallas_call(
        ortho_kernel,
        out_shape=(
            jax.ShapeDtypeStruct((3, RANK, RANK), F32),
            jax.ShapeDtypeStruct((8, LANES), F32),
        ),
        in_specs=[vmem],
        out_specs=(vmem, vmem),
        cost_estimate=pl.CostEstimate(flops=MIB * 4096, bytes_accessed=MIB, transcendentals=0),
    )(gram)


def finish_kernel(place_ref, s_mine_ref, s_other_ref, inverse_ref, p_ref, m0_ref, m1_ref, m2_ref,
                  error_hbm, q_ref, error_ref, sems):
    m_refs = (m0_ref, m1_ref, m2_ref)
    width = m0_ref.shape[1]

    def rows_of(ref):
        return jnp.concatenate(
            [
                jnp.concatenate([ref[(i * 8 + j) * 8 : (i * 8 + j) * 8 + 8, :] for j in range(7)], axis=1)
                for i in range(HALF // 8)
            ]
        )

    s = whole(place_ref[0], rows_of(s_mine_ref), rows_of(s_other_ref))
    stores, q_rows = [], []
    for k in range(3):
        part = slice(k * RANK, (k + 1) * RANK)
        q_new = dot3(inverse_ref[k], s[part], 1, 0)
        q_rows.append(q_new)
        p_ortho = dot3(inverse_ref[k], p_ref[part, :], 1, 0)
        error_ref[k] = (m_refs[k][...] - dot3(p_ortho, q_new, 0, 0)).astype(BF)
        stores.append(pltpu.make_async_copy(error_ref.at[k], error_hbm.at[0, k], sems.at[k]))
        stores[k].start()
    shard = q_ref.shape[1]
    at = place_ref[1] * shard
    q_ref[...] = pltpu.roll(jnp.concatenate(q_rows), lax.rem(width - at, width), 1)[:, :shard]
    for copy in stores:
        copy.wait()


def finish(place, s_mine, s_other, inverse, p_trans, matrices, shard):
    vmem = pl.BlockSpec(memory_space=pltpu.VMEM)
    hbm = pl.BlockSpec(memory_space=pltpu.HBM)
    hid, width = matrices[0].shape
    return pl.pallas_call(
        finish_kernel,
        out_shape=(jax.ShapeDtypeStruct((1, 3, hid, width), BF), jax.ShapeDtypeStruct((ROWS, shard), F32)),
        in_specs=[pl.BlockSpec(memory_space=pltpu.SMEM)] + [vmem] * 7,
        out_specs=(hbm, vmem),
        scratch_shapes=[
            pltpu.VMEM((3, hid, width), BF),
            pltpu.SemaphoreType.DMA((3,)),
        ],
        compiler_params=pltpu.CompilerParams(vmem_limit_bytes=20 * MIB),
    )(place, s_mine, s_other, inverse, p_trans, *matrices)


def after(values, other):
    return lax.optimization_barrier((values, other))[0]


def swap_core(value):
    return lax.ppermute(value, "dp", CORE_PAIR)


def dp_swap(bits):
    return [(i, i ^ bits) for i in range(2 * DEPTH)]


def take_kernel(value_ref, _, out_ref):
    out_ref[...] = value_ref[...]


def take(value, token):
    vmem = pl.BlockSpec(memory_space=pltpu.VMEM)
    return pl.pallas_call(
        take_kernel,
        out_shape=jax.ShapeDtypeStruct(value.shape, value.dtype),
        in_specs=[vmem, vmem],
        out_specs=vmem,
        compiler_params=pltpu.CompilerParams(vmem_limit_bytes=20 * MIB),
    )(value, token)


def add(values, token, scale, kind=F32):
    vmem = pl.BlockSpec(memory_space=pltpu.VMEM)

    def kernel(*refs):
        terms = [ref[...].astype(F32) for ref in refs[:-2]]
        while len(terms) > 1:
            terms = [terms[i] + terms[i + 1] for i in range(0, len(terms), 2)]
        refs[-1][...] = (terms[0] * scale).astype(kind)

    return pl.pallas_call(
        kernel,
        out_shape=jax.ShapeDtypeStruct(values[0].shape, kind),
        in_specs=[vmem] * (len(values) + 1),
        out_specs=vmem,
        compiler_params=pltpu.CompilerParams(vmem_limit_bytes=20 * MIB),
    )(*values, token)


def close_kernel(*refs):
    refs[-2][...] = sum(ref[...].astype(F32) for ref in refs[:-2]).astype(BF)
    refs[-1][...] = jnp.zeros_like(refs[-1])


def close(values):
    vmem = pl.BlockSpec(memory_space=pltpu.VMEM)
    return pl.pallas_call(
        close_kernel,
        out_shape=(jax.ShapeDtypeStruct(values[0].shape, BF), jax.ShapeDtypeStruct((8, LANES), F32)),
        in_specs=[vmem] * len(values),
        out_specs=(vmem, vmem),
        compiler_params=pltpu.CompilerParams(vmem_limit_bytes=20 * MIB),
    )(*values)


def per_device(hidden_in, out_grad, w_gate, w_up, w_down, error_in, q_init):
    n_workers = lax.axis_size("dp")
    n_tensor = lax.axis_size("tensor")
    me = lax.axis_index("tensor")
    y, x = me // SIDE, me % SIDE
    core = lax.axis_index("dp") % 2
    shard = hidden_in.shape[1]

    weights, w_both, _ = prepare(w_gate, w_up, w_down, error_in)
    x_part, dy_parts = pack(hidden_in.T, out_grad.T, q_init.reshape(ROWS, shard))
    pieces, dy_all = gather_all(x_part, dy_parts, me)
    spot = jnp.stack([y, core])
    gate_grad, up_grad, hidden, p_part, x_all = backward(spot, pieces, dy_all, weights)
    core = core.reshape(1)
    near = [p_part] + [lax.ppermute(p_part, "dp", dp_swap(bits)) for bits in (1, 2, 3)]
    matrices, token = grad_matrices((gate_grad, up_grad, hidden), x_all, dy_all, weights, p_part)
    p_pair = add(near, token, 1.0, BF)
    blocks, token = terms(spot, w_both, gate_grad, up_grad, p_pair)
    others = [lax.ppermute(p_pair, "dp", dp_swap(bits)) for bits in (4, 12, 10)]
    p_trans = add([p_pair] + others, token, 1.0 / n_workers)
    got = send_blocks(blocks)
    s_mine, s_theirs, gram = sketch(core, p_trans, matrices)
    s_pair = (s_mine + swap_core(s_theirs)).reshape(n_tensor, -1, LANES)
    gram = jnp.broadcast_to(gram[None], (n_tensor,) + gram.shape)
    sums = jnp.sum(lax.all_to_all(jnp.concatenate([s_pair, gram], axis=1), "tensor", 0, 0, tiled=True), axis=0)
    s_part, gram = sums[: s_pair.shape[1]], sums[s_pair.shape[1] :]
    s_all = spread(s_part, "dp", Z_GROUPS, DEPTH)
    inverse, token = ortho(gram)
    s_part = mean(s_all, token)
    got = send_parts(got, x, gram)
    input_grad, token = close(got)
    input_grad = input_grad.T
    s_half = take(spread(s_part, "tensor", None, n_tensor).reshape(-1, LANES), token)
    error_out, q_out = finish(
        jnp.stack([core[0], me]), s_half, swap_core(s_half), inverse, p_trans, matrices, shard
    )
    return (input_grad, error_out, q_out.reshape(q_init.shape))


def solution(mesh):
    in_specs = (
        P("dp", "tensor"),
        P("dp", "tensor"),
        P("tensor", None),
        P("tensor", None),
        P("tensor", None),
        P("dp", None, "tensor", None),
        P(None, None, "tensor"),
    )
    out_specs = (P("dp", "tensor"), P("dp", None, "tensor", None), P(None, None, "tensor"))
    return jax.shard_map(
        per_device, mesh=mesh, in_specs=in_specs, out_specs=out_specs, check_vma=False
    )
```

```python
import jax
import jax.numpy as jnp
from jax import lax
from jax.experimental import pallas as pl
from jax.experimental.pallas import tpu as pltpu
from jax.sharding import PartitionSpec as P

BF = jnp.bfloat16
F32 = jnp.float32
SIDE = 4
DEPTH = 8
RANK = 32
ROWS = 3 * RANK
HALF = ROWS // 2
LANES = 128
TILES = HALF * 1024 // (8 * LANES)
MIB = 1 << 20
STORE = 112

X_GROUPS = [[y * SIDE + x for x in range(SIDE)] for y in range(SIDE)]
Y_GROUPS = [[y * SIDE + x for y in range(SIDE)] for x in range(SIDE)]
CORE_PAIR = [(i, i ^ 1) for i in range(2 * DEPTH)]
Z_GROUPS = [[z * 2 + c for z in range(DEPTH)] for c in range(2)]


def x_ring(k):
    return [(y * SIDE + x, y * SIDE + (x + k) % SIDE) for y in range(SIDE) for x in range(SIDE)]


def y_ring(k):
    return [(y * SIDE + x, ((y + k) % SIDE) * SIDE + x) for y in range(SIDE) for x in range(SIDE)]


def spread(value, axis, groups, size):
    return lax.all_to_all(
        jnp.broadcast_to(value[None], (size,) + value.shape), axis, 0, 0, tiled=True, axis_index_groups=groups
    )


def ring_pieces(value, ring):
    near = [value] + [None] * 3
    for k in (1, 3, 2):
        near[k] = lax.ppermute(value, "tensor", ring(SIDE - k))
    return near


def pack_kernel(x_hbm, dy_hbm, q_hbm, x_ref, dy_ref, q_ref, sems):
    tokens = x_hbm.shape[1]
    copies = [pltpu.make_async_copy(x_hbm, x_ref.at[:, pl.ds(0, tokens)], sems.at[0])]
    for i in range(SIDE):
        copies.append(pltpu.make_async_copy(dy_hbm, dy_ref.at[i, :, pl.ds(0, tokens)], sems.at[1 + i]))
    q_load = pltpu.make_async_copy(q_hbm, q_ref, sems.at[1 + SIDE])
    for copy in [q_load] + copies:
        copy.start()
    q_load.wait()
    high, low = split(q_ref[...].T)
    both = [[half[:, k * RANK : (k + 1) * RANK] for half in (high, low)] for k in range(3)]
    x_ref[:, tokens:] = jnp.concatenate(both[0] + both[1], axis=1)
    tail = jnp.concatenate(both[2] + [jnp.zeros((high.shape[0], LANES - 2 * RANK), BF)], axis=1)
    for i in range(SIDE):
        dy_ref[i, :, tokens:] = tail
    for copy in copies:
        copy.wait()


def pack(x_part, dy_part, q_rows):
    vmem = pl.BlockSpec(memory_space=pltpu.VMEM)
    anywhere = pl.BlockSpec(memory_space=pl.ANY)
    rows, tokens = x_part.shape
    return pl.pallas_call(
        pack_kernel,
        out_shape=(
            jax.ShapeDtypeStruct((rows, tokens + LANES), BF),
            jax.ShapeDtypeStruct((SIDE, rows, tokens + LANES), BF),
        ),
        in_specs=[anywhere] * 3,
        out_specs=(vmem, vmem),
        scratch_shapes=[pltpu.VMEM(q_rows.shape, F32), pltpu.SemaphoreType.DMA((2 + SIDE,))],
        compiler_params=pltpu.CompilerParams(vmem_limit_bytes=58 * MIB),
    )(x_part, dy_part, q_rows)


def order_kernel(place_ref, p0_ref, p1_ref, p2_ref, p3_ref, out_ref, sems):
    copies = [
        pltpu.make_async_copy(ref, out_ref.at[lax.rem(place_ref[0] + i, SIDE)], sems.at[i])
        for i, ref in enumerate((p0_ref, p1_ref, p2_ref, p3_ref))
    ]
    for copy in copies:
        copy.start()
    for copy in copies:
        copy.wait()


def order(position, pieces):
    anywhere = pl.BlockSpec(memory_space=pl.ANY)
    return pl.pallas_call(
        order_kernel,
        out_shape=jax.ShapeDtypeStruct((SIDE,) + pieces[0].shape, pieces[0].dtype),
        in_specs=[pl.BlockSpec(memory_space=pltpu.SMEM)] + [anywhere] * SIDE,
        out_specs=pl.BlockSpec(memory_space=pltpu.VMEM),
        scratch_shapes=[pltpu.SemaphoreType.DMA((SIDE,))],
        compiler_params=pltpu.CompilerParams(vmem_limit_bytes=20 * MIB),
    )(position.reshape(1), *pieces)


def gather_all(x_part, dy_parts, me):
    rows = SIDE * x_part.shape[0]
    dy_col = lax.all_to_all(dy_parts, "tensor", 0, 0, tiled=True, axis_index_groups=Y_GROUPS)
    near, dy_col = lax.optimization_barrier((ring_pieces(x_part, x_ring), dy_col))
    x_row, dy_col = lax.optimization_barrier((order(me % SIDE, near), dy_col))
    dy_all = spread(dy_col, "tensor", X_GROUPS, SIDE)
    far, dy_all = lax.optimization_barrier((ring_pieces(x_row, y_ring), dy_all))
    return [p.reshape(rows, -1) for p in far], dy_all.reshape(SIDE * rows, -1)


def send_blocks(blocks):
    return [blocks[0]] + [lax.ppermute(blocks[k], "tensor", y_ring(k)) for k in (1, 3, 2)]


def parts_kernel(place_ref, g0_ref, g1_ref, g2_ref, g3_ref, _, o0_ref, o1_ref, o2_ref, o3_ref):
    for k, out_ref in enumerate((o0_ref, o1_ref, o2_ref, o3_ref)):
        at = lax.rem(place_ref[0] + k, SIDE)
        total = sum(ref[at].astype(F32) for ref in (g0_ref, g1_ref, g2_ref, g3_ref))
        out_ref[...] = total.astype(out_ref.dtype)


def send_parts(got, position, token):
    vmem = pl.BlockSpec(memory_space=pltpu.VMEM)
    rows, tokens = got[0].shape
    parts = pl.pallas_call(
        parts_kernel,
        out_shape=(jax.ShapeDtypeStruct((rows // SIDE, tokens), BF),) * SIDE,
        in_specs=[pl.BlockSpec(memory_space=pltpu.SMEM)] + [vmem] * (SIDE + 1),
        out_specs=(vmem,) * SIDE,
        compiler_params=pltpu.CompilerParams(vmem_limit_bytes=20 * MIB),
    )(position.reshape(1), *[v.reshape(SIDE, -1, tokens) for v in got], token)
    return [parts[0]] + [lax.ppermute(parts[k], "tensor", x_ring(k)) for k in (1, 3, 2)]


def split(value):
    high = value.astype(BF)
    return high, (value - high.astype(F32)).astype(BF)


def dot(a, b, ca, cb):
    return lax.dot_general(a, b, (((ca,), (cb,)), ((), ())), preferred_element_type=F32)


def dot3(a, b, ca, cb):
    a_high, a_low = split(a)
    b_high, b_low = split(b)
    return dot(
        jnp.concatenate([a_high, a_high, a_low], axis=ca), jnp.concatenate([b_high, b_low, b_high], axis=cb), ca, cb
    )


def own_half(core, value):
    low, high = value[:HALF], value[HALF:]
    first = core == 0
    return jnp.where(first, low, high), jnp.where(first, high, low)


def whole(core, mine, other):
    first = core == 0
    return jnp.concatenate([jnp.where(first, mine, other), jnp.where(first, other, mine)])


def prepare_kernel(gate_ref, up_ref, down_ref, err_ref, left_hbm, both_ref, token_ref, left_ref, sem):
    hid, width = gate_ref.shape
    gate, up, down = gate_ref[...], up_ref[...], down_ref[...].astype(F32)
    block = width // (SIDE * SIDE)
    left_ref[0] = gate
    left_ref[1] = up
    left_ref[2] = jnp.concatenate(
        [down[:, (y * SIDE + x) * block : (y * SIDE + x + 1) * block] for x in range(SIDE) for y in range(SIDE)],
        axis=1,
    ).astype(BF)
    for k in range(3):
        left_ref[3 + k] = err_ref[0, k]
    copy = pltpu.make_async_copy(left_ref, left_hbm.at[pl.ds(0, 6)], sem)
    copy.start()
    both_ref[:, :hid] = gate.astype(F32).T.astype(BF)
    both_ref[:, hid:] = up.astype(F32).T.astype(BF)
    token_ref[...] = jnp.zeros_like(token_ref)
    copy.wait()


def prepare(w_gate, w_up, w_down, error_in):
    vmem = pl.BlockSpec(memory_space=pltpu.VMEM)
    hid, width = w_gate.shape
    return pl.pallas_call(
        prepare_kernel,
        out_shape=(
            jax.ShapeDtypeStruct((STORE, hid, width), BF),
            jax.ShapeDtypeStruct((width, 2 * hid), BF),
            jax.ShapeDtypeStruct((8, LANES), F32),
        ),
        in_specs=[vmem] * 4,
        out_specs=(pl.BlockSpec(memory_space=pltpu.HBM), vmem, vmem),
        scratch_shapes=[pltpu.VMEM((6, hid, width), BF), pltpu.SemaphoreType.DMA],
        compiler_params=pltpu.CompilerParams(vmem_limit_bytes=20 * MIB),
    )(w_gate, w_up, w_down, error_in)


def backward_kernel(place_ref, p0_ref, p1_ref, p2_ref, p3_ref, dy_ref, w_hbm,
                    gate_grad_ref, up_grad_ref, hidden_ref, p_out_ref, x_ref, w_ref, hidden_grad_ref, sems):
    rows = p0_ref.shape[0]
    hid, tokens = hidden_ref.shape
    chunk = 256
    loads = [pltpu.make_async_copy(w_hbm.at[k], w_ref.at[k], sems.at[k]) for k in range(6)]
    pieces = []
    for i, ref in enumerate((p0_ref, p1_ref, p2_ref, p3_ref)):
        at = pl.multiple_of(lax.rem(place_ref[0] + i, SIDE) * rows, 16)
        pieces.append(pltpu.make_async_copy(ref, x_ref.at[pl.ds(at, rows), :], sems.at[6 + i]))
    for copy in [loads[2], loads[5]] + pieces + loads[:2] + loads[3:5]:
        copy.start()
    q_dy = dy_ref[:, tokens : tokens + 2 * RANK]
    q_dy_rows = q_dy.astype(F32).T.astype(BF)
    loads[2].wait()
    for start in range(0, tokens, chunk):
        span = slice(start, start + chunk)
        hidden_grad_ref[:, span] = dot(w_ref[2], dy_ref[:, span], 1, 0)
    block = rows // SIDE
    q_plain = q_dy.astype(F32)
    q_plain = jnp.concatenate(
        [q_plain[(x * SIDE + y) * block : (x * SIDE + y + 1) * block] for y in range(SIDE) for x in range(SIDE)]
    ).astype(BF)
    loads[5].wait()
    last_error = dot(w_ref[5], q_plain, 1, 0)
    for copy in pieces + loads[:2]:
        copy.wait()
    q_x = x_ref[:, tokens:]
    q_rows = q_x.astype(F32).T.astype(BF)
    q_both = [q_rows[: 2 * RANK], q_rows[2 * RANK :], q_dy_rows]
    sums = [jnp.zeros((2 * RANK, hid), F32)] * 3
    for start in range(0, tokens, chunk):
        span = slice(start, start + chunk)
        x, dy = x_ref[:, span], dy_ref[:, span]
        gate_pre = dot(w_ref[0], x, 1, 0)
        up_pre = dot(w_ref[1], x, 1, 0)
        hidden_grad = hidden_grad_ref[:, span]
        gate_sig = jax.nn.sigmoid(gate_pre)
        gate_act = gate_pre * gate_sig
        hidden = (gate_act * up_pre).astype(BF)
        gate_grad = (hidden_grad * up_pre * gate_sig * (1.0 + gate_pre * (1.0 - gate_sig))).astype(BF)
        up_grad = (hidden_grad * gate_act).astype(BF)
        gate_grad_ref[:, span] = gate_grad
        up_grad_ref[:, span] = up_grad
        hidden_ref[:, span] = hidden
        for k, (left, right) in enumerate(((gate_grad, x), (up_grad, x), (hidden, dy))):
            both = dot(q_both[k], right, 1, 0)
            halves = jnp.concatenate(split(both[:RANK] + both[RANK:]))
            sums[k] = sums[k] + dot(halves, left, 1, 1)
    for copy in loads[3:5]:
        copy.wait()
    errors = [dot(w_ref[3 + k], q_x[:, 2 * k * RANK : 2 * (k + 1) * RANK], 1, 0) for k in range(2)] + [last_error]
    error_p = jnp.concatenate([both[:, :RANK] + both[:, RANK:] for both in errors], axis=1).T
    p = jnp.concatenate([both[:RANK] + both[RANK:] for both in sums]) + error_p
    p_out_ref[...] = p.astype(BF)


def backward(place, pieces, dy_all, weights):
    hid, width = weights.shape[1:]
    wide = dy_all.shape[1]
    tokens = wide - LANES
    vmem = pl.BlockSpec(memory_space=pltpu.VMEM)
    hbm = pl.BlockSpec(memory_space=pltpu.HBM)
    grads = jax.ShapeDtypeStruct((hid, tokens), BF)
    return pl.pallas_call(
        backward_kernel,
        out_shape=(
            grads,
            grads,
            grads,
            jax.ShapeDtypeStruct((ROWS, hid), BF),
            jax.ShapeDtypeStruct((width, wide), BF),
        ),
        in_specs=[pl.BlockSpec(memory_space=pltpu.SMEM)] + [hbm] * SIDE + [vmem, hbm],
        out_specs=(vmem,) * 5,
        scratch_shapes=[
            pltpu.VMEM((6, hid, width), BF),
            pltpu.VMEM((hid, tokens), F32),
            pltpu.SemaphoreType.DMA((6 + SIDE,)),
        ],
        compiler_params=pltpu.CompilerParams(vmem_limit_bytes=20 * MIB),
        cost_estimate=pl.CostEstimate(flops=6 * hid * width * tokens, bytes_accessed=8 * MIB, transcendentals=0),
    )(place, *pieces, dy_all, weights)


def term_kernel(place_ref, w_ref, gate_grad_ref, up_grad_ref, _, t0_ref, t1_ref, t2_ref, t3_ref, token_ref):
    grads = jnp.concatenate([gate_grad_ref[...], up_grad_ref[...]])
    rows = t0_ref.shape[0]
    for i, ref in enumerate((t0_ref, t1_ref, t2_ref, t3_ref)):
        at = pl.multiple_of(lax.rem(place_ref[0] + i, SIDE) * rows, 16)
        ref[...] = dot(w_ref[pl.ds(at, rows), :], grads, 1, 0).astype(BF)
    token_ref[...] = jnp.zeros_like(token_ref)


def terms(place, w_both, gate_grad, up_grad, other):
    vmem = pl.BlockSpec(memory_space=pltpu.VMEM)
    tokens = gate_grad.shape[1]
    width, both = w_both.shape
    out = pl.pallas_call(
        term_kernel,
        out_shape=(jax.ShapeDtypeStruct((width // SIDE, tokens), BF),) * SIDE
        + (jax.ShapeDtypeStruct((8, LANES), F32),),
        in_specs=[pl.BlockSpec(memory_space=pltpu.SMEM)] + [vmem] * 4,
        out_specs=(vmem,) * (SIDE + 1),
        compiler_params=pltpu.CompilerParams(vmem_limit_bytes=20 * MIB),
        cost_estimate=pl.CostEstimate(flops=2 * width * both * tokens, bytes_accessed=4 * MIB, transcendentals=0),
    )(place, w_both, gate_grad, up_grad, other)
    return out[:SIDE], out[SIDE]


def matrices_kernel(gate_grad_ref, up_grad_ref, hidden_ref, x_ref, dy_ref, left_hbm, _,
                    m0_ref, m1_ref, m2_ref, token_ref, left_ref, sems):
    loads = [pltpu.make_async_copy(left_hbm.at[3 + k], left_ref.at[k], sems.at[k]) for k in range(3)]
    for copy in loads:
        copy.start()
    tokens = hidden_ref.shape[1]
    x = x_ref[:, :tokens]
    swapped = dot(hidden_ref[...], dy_ref[:, :tokens], 1, 1)
    block = swapped.shape[1] // (SIDE * SIDE)
    parts = [
        swapped[:, (x * SIDE + y) * block : (x * SIDE + y + 1) * block] for y in range(SIDE) for x in range(SIDE)
    ]
    for copy in loads:
        copy.wait()
    m2_ref[...] = jnp.concatenate(parts, axis=1) + left_ref[2].astype(F32)
    m0_ref[...] = dot(gate_grad_ref[...], x, 1, 1) + left_ref[0].astype(F32)
    m1_ref[...] = dot(up_grad_ref[...], x, 1, 1) + left_ref[1].astype(F32)
    token_ref[...] = jnp.zeros_like(token_ref)


def grad_matrices(grads, x_all, dy_all, weights, other):
    vmem = pl.BlockSpec(memory_space=pltpu.VMEM)
    hid, tokens = grads[0].shape
    width = dy_all.shape[0]
    out = pl.pallas_call(
        matrices_kernel,
        out_shape=(jax.ShapeDtypeStruct((hid, width), F32),) * 3 + (jax.ShapeDtypeStruct((8, LANES), F32),),
        in_specs=[vmem] * 5 + [pl.BlockSpec(memory_space=pltpu.HBM), vmem],
        out_specs=(vmem,) * 4,
        scratch_shapes=[pltpu.VMEM((3, hid, width), BF), pltpu.SemaphoreType.DMA((3,))],
        compiler_params=pltpu.CompilerParams(vmem_limit_bytes=20 * MIB),
        cost_estimate=pl.CostEstimate(flops=6 * hid * width * tokens, bytes_accessed=9 * MIB, transcendentals=0),
    )(*grads, x_all, dy_all, weights, other)
    return out[:3], out[3]


def mean_kernel(value_ref, _, out_ref):
    total = value_ref[0].astype(F32)
    for i in range(1, value_ref.shape[0]):
        total = total + value_ref[i].astype(F32)
    out_ref[...] = total * (0.5 / value_ref.shape[0])


def mean(value, token):
    vmem = pl.BlockSpec(memory_space=pltpu.VMEM)
    return pl.pallas_call(
        mean_kernel,
        out_shape=jax.ShapeDtypeStruct(value.shape[1:], F32),
        in_specs=[vmem, pl.BlockSpec(memory_space=pl.ANY)],
        out_specs=vmem,
        compiler_params=pltpu.CompilerParams(vmem_limit_bytes=20 * MIB),
    )(value, token)


def sketch_kernel(core_ref, p_ref, m0_ref, m1_ref, m2_ref, mine_ref, theirs_ref, gram_ref):
    core = core_ref[0]
    p = p_ref[...]
    rows, grams = [], []
    for k, m_ref in enumerate((m0_ref, m1_ref, m2_ref)):
        p_k = p[k * RANK : (k + 1) * RANK]
        p_high, p_low = split(p_k)
        m_high, m_low = split(m_ref[...])
        both = dot(jnp.concatenate([p_high, p_low]), m_high, 1, 0)
        term = both[:RANK] + both[RANK:] + dot(p_high, m_low, 1, 0)
        grams.append(
            lax.dot_general(
                p_k, p_k, (((1,), (1,)), ((), ())), precision=lax.Precision.HIGHEST, preferred_element_type=F32
            )
        )
        rows.append(jnp.concatenate([term, jnp.zeros((RANK, LANES), F32)], axis=1))
    gram = jnp.concatenate(grams)
    gram_ref[...] = jnp.concatenate([gram[i * 24 : (i + 1) * 24] for i in range(4)], axis=1)
    mine, theirs = own_half(core, jnp.concatenate(rows))
    for i in range(HALF // 8):
        for j in range(8):
            tile = (i * 8 + j) * 8
            rows, cols = slice(i * 8, i * 8 + 8), slice(j * LANES, (j + 1) * LANES)
            mine_ref[tile : tile + 8, :] = mine[rows, cols]
            theirs_ref[tile : tile + 8, :] = theirs[rows, cols]


def sketch(core, p_trans, matrices):
    vmem = pl.BlockSpec(memory_space=pltpu.VMEM)
    out = jax.ShapeDtypeStruct((TILES * 8, LANES), F32)
    return pl.pallas_call(
        sketch_kernel,
        out_shape=(out, out, jax.ShapeDtypeStruct((24, LANES), F32)),
        in_specs=[pl.BlockSpec(memory_space=pltpu.SMEM)] + [vmem] * 4,
        out_specs=(vmem,) * 3,
        compiler_params=pltpu.CompilerParams(vmem_limit_bytes=20 * MIB),
    )(core, p_trans, *matrices)


def ortho_kernel(gram_ref, inverse_ref, token_ref):
    gram = gram_ref[...]
    gram = jnp.concatenate([gram[:, i * RANK : (i + 1) * RANK] for i in range(4)])
    gram = jnp.stack([gram[k * RANK : (k + 1) * RANK] for k in range(3)])
    rows = lax.broadcasted_iota(jnp.int32, (1, RANK, RANK), 1)
    cols = lax.broadcasted_iota(jnp.int32, (1, RANK, RANK), 2)
    eye = jnp.broadcast_to(jnp.where(rows == cols, 1.0, 0.0), gram.shape)
    work = jnp.concatenate([gram, eye], axis=2)
    below = lax.broadcasted_iota(jnp.int32, (1, RANK, 1), 1)
    for k in range(RANK):
        pivot = work[:, k : k + 1, :]
        scale = 1.0 / pivot[:, :, k : k + 1]
        factor = jnp.where(below > k, work[:, :, k : k + 1] * scale, 0.0)
        work = work - factor * pivot
    diag = jnp.sum(jnp.where(rows == cols, work[:, :, :RANK], 0.0), axis=2, keepdims=True)
    inverse = work[:, :, RANK:] * lax.rsqrt(diag)
    inverse_ref[...] = inverse
    token_ref[...] = jnp.zeros_like(token_ref)


def ortho(gram):
    vmem = pl.BlockSpec(memory_space=pltpu.VMEM)
    return pl.pallas_call(
        ortho_kernel,
        out_shape=(
            jax.ShapeDtypeStruct((3, RANK, RANK), F32),
            jax.ShapeDtypeStruct((8, LANES), F32),
        ),
        in_specs=[vmem],
        out_specs=(vmem, vmem),
        cost_estimate=pl.CostEstimate(flops=MIB * 4096, bytes_accessed=MIB, transcendentals=0),
    )(gram)


def finish_kernel(place_ref, s_mine_ref, s_other_ref, inverse_ref, p_ref, m0_ref, m1_ref, m2_ref,
                  error_hbm, q_ref, error_ref, sems):
    m_refs = (m0_ref, m1_ref, m2_ref)
    width = m0_ref.shape[1]

    def rows_of(ref):
        return jnp.concatenate(
            [
                jnp.concatenate([ref[(i * 8 + j) * 8 : (i * 8 + j) * 8 + 8, :] for j in range(7)], axis=1)
                for i in range(HALF // 8)
            ]
        )

    s = whole(place_ref[0], rows_of(s_mine_ref), rows_of(s_other_ref))
    stores, q_rows = [], []
    for k in range(3):
        part = slice(k * RANK, (k + 1) * RANK)
        q_new = dot3(inverse_ref[k], s[part], 1, 0)
        q_rows.append(q_new)
        p_ortho = dot3(inverse_ref[k], p_ref[part, :], 1, 0)
        error_ref[k] = (m_refs[k][...] - dot3(p_ortho, q_new, 0, 0)).astype(BF)
        stores.append(pltpu.make_async_copy(error_ref.at[k], error_hbm.at[0, k], sems.at[k]))
        stores[k].start()
    shard = q_ref.shape[1]
    at = place_ref[1] * shard
    q_ref[...] = pltpu.roll(jnp.concatenate(q_rows), lax.rem(width - at, width), 1)[:, :shard]
    for copy in stores:
        copy.wait()


def finish(place, s_mine, s_other, inverse, p_trans, matrices, shard):
    vmem = pl.BlockSpec(memory_space=pltpu.VMEM)
    hbm = pl.BlockSpec(memory_space=pltpu.HBM)
    hid, width = matrices[0].shape
    return pl.pallas_call(
        finish_kernel,
        out_shape=(jax.ShapeDtypeStruct((1, 3, hid, width), BF), jax.ShapeDtypeStruct((ROWS, shard), F32)),
        in_specs=[pl.BlockSpec(memory_space=pltpu.SMEM)] + [vmem] * 7,
        out_specs=(hbm, vmem),
        scratch_shapes=[
            pltpu.VMEM((3, hid, width), BF),
            pltpu.SemaphoreType.DMA((3,)),
        ],
        compiler_params=pltpu.CompilerParams(vmem_limit_bytes=20 * MIB),
    )(place, s_mine, s_other, inverse, p_trans, *matrices)


def swap_core(value):
    return lax.ppermute(value, "dp", CORE_PAIR)


def dp_swap(bits):
    return [(i, i ^ bits) for i in range(2 * DEPTH)]


def take_kernel(value_ref, _, out_ref):
    out_ref[...] = value_ref[...]


def take(value, token):
    vmem = pl.BlockSpec(memory_space=pltpu.VMEM)
    return pl.pallas_call(
        take_kernel,
        out_shape=jax.ShapeDtypeStruct(value.shape, value.dtype),
        in_specs=[vmem, vmem],
        out_specs=vmem,
        compiler_params=pltpu.CompilerParams(vmem_limit_bytes=20 * MIB),
    )(value, token)


def add(values, token, scale, kind=F32):
    vmem = pl.BlockSpec(memory_space=pltpu.VMEM)

    def kernel(*refs):
        terms = [ref[...].astype(F32) for ref in refs[:-2]]
        while len(terms) > 1:
            terms = [terms[i] + terms[i + 1] for i in range(0, len(terms), 2)]
        refs[-1][...] = (terms[0] * scale).astype(kind)

    return pl.pallas_call(
        kernel,
        out_shape=jax.ShapeDtypeStruct(values[0].shape, kind),
        in_specs=[vmem] * (len(values) + 1),
        out_specs=vmem,
        compiler_params=pltpu.CompilerParams(vmem_limit_bytes=20 * MIB),
    )(*values, token)


def close_kernel(*refs):
    refs[-2][...] = sum(ref[...].astype(F32) for ref in refs[:-2]).astype(BF)
    refs[-1][...] = jnp.zeros_like(refs[-1])


def close(values):
    vmem = pl.BlockSpec(memory_space=pltpu.VMEM)
    return pl.pallas_call(
        close_kernel,
        out_shape=(jax.ShapeDtypeStruct(values[0].shape, BF), jax.ShapeDtypeStruct((8, LANES), F32)),
        in_specs=[vmem] * len(values),
        out_specs=(vmem, vmem),
        compiler_params=pltpu.CompilerParams(vmem_limit_bytes=20 * MIB),
    )(*values)


def per_device(hidden_in, out_grad, w_gate, w_up, w_down, error_in, q_init):
    n_workers = lax.axis_size("dp")
    n_tensor = lax.axis_size("tensor")
    me = lax.axis_index("tensor")
    y, x = me // SIDE, me % SIDE
    core = lax.axis_index("dp") % 2
    shard = hidden_in.shape[1]

    weights, w_both, _ = prepare(w_gate, w_up, w_down, error_in)
    x_part, dy_parts = pack(hidden_in.T, out_grad.T, q_init.reshape(ROWS, shard))
    pieces, dy_all = gather_all(x_part, dy_parts, me)
    spot = jnp.stack([y, core])
    gate_grad, up_grad, hidden, p_part, x_all = backward(spot, pieces, dy_all, weights)
    core = core.reshape(1)
    near = [p_part] + [lax.ppermute(p_part, "dp", dp_swap(bits)) for bits in (1, 2, 3)]
    matrices, token = grad_matrices((gate_grad, up_grad, hidden), x_all, dy_all, weights, p_part)
    p_pair = add(near, token, 1.0, BF)
    blocks, token = terms(spot, w_both, gate_grad, up_grad, p_pair)
    others = [lax.ppermute(p_pair, "dp", dp_swap(bits)) for bits in (4, 12, 10)]
    p_trans = add([p_pair] + others, token, 1.0 / n_workers)
    got = send_blocks(blocks)
    s_mine, s_theirs, gram = sketch(core, p_trans, matrices)
    s_pair = (s_mine + swap_core(s_theirs)).reshape(n_tensor, -1, LANES)
    gram = jnp.broadcast_to(gram[None], (n_tensor,) + gram.shape)
    sums = jnp.sum(lax.all_to_all(jnp.concatenate([s_pair, gram], axis=1), "tensor", 0, 0, tiled=True), axis=0)
    s_part, gram = sums[: s_pair.shape[1]], sums[s_pair.shape[1] :]
    s_all = spread(s_part, "dp", Z_GROUPS, DEPTH)
    inverse, token = ortho(gram)
    s_part = mean(s_all, token)
    got = send_parts(got, x, gram)
    input_grad, token = close(got)
    input_grad = input_grad.T
    s_half = take(spread(s_part, "tensor", None, n_tensor).reshape(-1, LANES), token)
    error_out, q_out = finish(
        jnp.stack([core[0], me]), s_half, swap_core(s_half), inverse, p_trans, matrices, shard
    )
    return (input_grad, error_out, q_out.reshape(q_init.shape))


def solution(mesh):
    in_specs = (
        P("dp", "tensor"),
        P("dp", "tensor"),
        P("tensor", None),
        P("tensor", None),
        P("tensor", None),
        P("dp", None, "tensor", None),
        P(None, None, "tensor"),
    )
    out_specs = (P("dp", "tensor"), P("dp", None, "tensor", None), P(None, None, "tensor"))
    return jax.shard_map(
        per_device, mesh=mesh, in_specs=in_specs, out_specs=out_specs, check_vma=False
    )
```

```python
import jax
import jax.numpy as jnp
from jax import lax
from jax.experimental import pallas as pl
from jax.experimental.pallas import tpu as pltpu
from jax.sharding import PartitionSpec as P

BF = jnp.bfloat16
F32 = jnp.float32
SIDE = 4
DEPTH = 8
RANK = 32
ROWS = 3 * RANK
HALF = ROWS // 2
LANES = 128
TILES = HALF * 1024 // (8 * LANES)
MIB = 1 << 20
STORE = 112

X_GROUPS = [[y * SIDE + x for x in range(SIDE)] for y in range(SIDE)]
Y_GROUPS = [[y * SIDE + x for y in range(SIDE)] for x in range(SIDE)]
CORE_PAIR = [(i, i ^ 1) for i in range(2 * DEPTH)]
Z_GROUPS = [[z * 2 + c for z in range(DEPTH)] for c in range(2)]


def x_ring(k):
    return [(y * SIDE + x, y * SIDE + (x + k) % SIDE) for y in range(SIDE) for x in range(SIDE)]


def y_ring(k):
    return [(y * SIDE + x, ((y + k) % SIDE) * SIDE + x) for y in range(SIDE) for x in range(SIDE)]


def spread(value, axis, groups, size):
    return lax.all_to_all(
        jnp.broadcast_to(value[None], (size,) + value.shape), axis, 0, 0, tiled=True, axis_index_groups=groups
    )


def ring_pieces(value, ring):
    near = [value] + [None] * 3
    for k in (1, 3, 2):
        near[k] = lax.ppermute(value, "tensor", ring(SIDE - k))
    return near


def pack_kernel(x_hbm, dy_hbm, q_hbm, x_ref, dy_ref, q_ref, sems):
    tokens = x_hbm.shape[1]
    copies = [pltpu.make_async_copy(x_hbm, x_ref.at[:, pl.ds(0, tokens)], sems.at[0])]
    for i in range(SIDE):
        copies.append(pltpu.make_async_copy(dy_hbm, dy_ref.at[i, :, pl.ds(0, tokens)], sems.at[1 + i]))
    q_load = pltpu.make_async_copy(q_hbm, q_ref, sems.at[1 + SIDE])
    for copy in [q_load] + copies:
        copy.start()
    q_load.wait()
    high, low = split(q_ref[...].T)
    both = [[half[:, k * RANK : (k + 1) * RANK] for half in (high, low)] for k in range(3)]
    x_ref[:, tokens:] = jnp.concatenate(both[0] + both[1], axis=1)
    tail = jnp.concatenate(both[2] + [jnp.zeros((high.shape[0], LANES - 2 * RANK), BF)], axis=1)
    for i in range(SIDE):
        dy_ref[i, :, tokens:] = tail
    for copy in copies:
        copy.wait()


def pack(x_part, dy_part, q_rows):
    vmem = pl.BlockSpec(memory_space=pltpu.VMEM)
    anywhere = pl.BlockSpec(memory_space=pl.ANY)
    rows, tokens = x_part.shape
    return pl.pallas_call(
        pack_kernel,
        out_shape=(
            jax.ShapeDtypeStruct((rows, tokens + LANES), BF),
            jax.ShapeDtypeStruct((SIDE, rows, tokens + LANES), BF),
        ),
        in_specs=[anywhere] * 3,
        out_specs=(vmem, vmem),
        scratch_shapes=[pltpu.VMEM(q_rows.shape, F32), pltpu.SemaphoreType.DMA((2 + SIDE,))],
        compiler_params=pltpu.CompilerParams(vmem_limit_bytes=58 * MIB),
    )(x_part, dy_part, q_rows)


def order_kernel(place_ref, p0_ref, p1_ref, p2_ref, p3_ref, out_ref, sems):
    copies = [
        pltpu.make_async_copy(ref, out_ref.at[lax.rem(place_ref[0] + i, SIDE)], sems.at[i])
        for i, ref in enumerate((p0_ref, p1_ref, p2_ref, p3_ref))
    ]
    for copy in copies:
        copy.start()
    for copy in copies:
        copy.wait()


def order(position, pieces):
    anywhere = pl.BlockSpec(memory_space=pl.ANY)
    return pl.pallas_call(
        order_kernel,
        out_shape=jax.ShapeDtypeStruct((SIDE,) + pieces[0].shape, pieces[0].dtype),
        in_specs=[pl.BlockSpec(memory_space=pltpu.SMEM)] + [anywhere] * SIDE,
        out_specs=pl.BlockSpec(memory_space=pltpu.VMEM),
        scratch_shapes=[pltpu.SemaphoreType.DMA((SIDE,))],
        compiler_params=pltpu.CompilerParams(vmem_limit_bytes=20 * MIB),
    )(position.reshape(1), *pieces)


def gather_all(x_part, dy_parts, me):
    rows = SIDE * x_part.shape[0]
    dy_col = lax.all_to_all(dy_parts, "tensor", 0, 0, tiled=True, axis_index_groups=Y_GROUPS)
    near, dy_col = lax.optimization_barrier((ring_pieces(x_part, x_ring), dy_col))
    x_row, dy_col = lax.optimization_barrier((order(me % SIDE, near), dy_col))
    dy_all = spread(dy_col, "tensor", X_GROUPS, SIDE)
    far, dy_all = lax.optimization_barrier((ring_pieces(x_row, y_ring), dy_all))
    return [p.reshape(rows, -1) for p in far], dy_all.reshape(SIDE * rows, -1)


def send_blocks(blocks):
    return [blocks[0]] + [lax.ppermute(blocks[k], "tensor", y_ring(k)) for k in (1, 3, 2)]


def parts_kernel(place_ref, g0_ref, g1_ref, g2_ref, g3_ref, _, o0_ref, o1_ref, o2_ref, o3_ref):
    for k, out_ref in enumerate((o0_ref, o1_ref, o2_ref, o3_ref)):
        at = lax.rem(place_ref[0] + k, SIDE)
        total = sum(ref[at].astype(F32) for ref in (g0_ref, g1_ref, g2_ref, g3_ref))
        out_ref[...] = total.astype(out_ref.dtype)


def send_parts(got, position, token):
    vmem = pl.BlockSpec(memory_space=pltpu.VMEM)
    rows, tokens = got[0].shape
    parts = pl.pallas_call(
        parts_kernel,
        out_shape=(jax.ShapeDtypeStruct((rows // SIDE, tokens), BF),) * SIDE,
        in_specs=[pl.BlockSpec(memory_space=pltpu.SMEM)] + [vmem] * (SIDE + 1),
        out_specs=(vmem,) * SIDE,
        compiler_params=pltpu.CompilerParams(vmem_limit_bytes=20 * MIB),
    )(position.reshape(1), *[v.reshape(SIDE, -1, tokens) for v in got], token)
    return [parts[0]] + [lax.ppermute(parts[k], "tensor", x_ring(k)) for k in (1, 3, 2)]


def split(value):
    high = value.astype(BF)
    return high, (value - high.astype(F32)).astype(BF)


def dot(a, b, ca, cb):
    return lax.dot_general(a, b, (((ca,), (cb,)), ((), ())), preferred_element_type=F32)


def dot3(a, b, ca, cb):
    a_high, a_low = split(a)
    b_high, b_low = split(b)
    return dot(
        jnp.concatenate([a_high, a_high, a_low], axis=ca), jnp.concatenate([b_high, b_low, b_high], axis=cb), ca, cb
    )


def own_half(core, value):
    low, high = value[:HALF], value[HALF:]
    first = core == 0
    return jnp.where(first, low, high), jnp.where(first, high, low)


def whole(core, mine, other):
    first = core == 0
    return jnp.concatenate([jnp.where(first, mine, other), jnp.where(first, other, mine)])


def prepare_kernel(gate_ref, up_ref, down_ref, err_ref, left_hbm, both_ref, token_ref, left_ref, sem):
    hid, width = gate_ref.shape
    gate, up, down = gate_ref[...], up_ref[...], down_ref[...].astype(F32)
    block = width // (SIDE * SIDE)
    left_ref[0] = gate
    left_ref[1] = up
    left_ref[2] = jnp.concatenate(
        [down[:, (y * SIDE + x) * block : (y * SIDE + x + 1) * block] for x in range(SIDE) for y in range(SIDE)],
        axis=1,
    ).astype(BF)
    for k in range(3):
        left_ref[3 + k] = err_ref[0, k]
    copy = pltpu.make_async_copy(left_ref, left_hbm.at[pl.ds(0, 6)], sem)
    copy.start()
    both_ref[:, :hid] = gate.astype(F32).T.astype(BF)
    both_ref[:, hid:] = up.astype(F32).T.astype(BF)
    token_ref[...] = jnp.zeros_like(token_ref)
    copy.wait()


def prepare(w_gate, w_up, w_down, error_in):
    vmem = pl.BlockSpec(memory_space=pltpu.VMEM)
    hid, width = w_gate.shape
    return pl.pallas_call(
        prepare_kernel,
        out_shape=(
            jax.ShapeDtypeStruct((STORE, hid, width), BF),
            jax.ShapeDtypeStruct((width, 2 * hid), BF),
            jax.ShapeDtypeStruct((8, LANES), F32),
        ),
        in_specs=[vmem] * 4,
        out_specs=(pl.BlockSpec(memory_space=pltpu.HBM), vmem, vmem),
        scratch_shapes=[pltpu.VMEM((6, hid, width), BF), pltpu.SemaphoreType.DMA],
        compiler_params=pltpu.CompilerParams(vmem_limit_bytes=20 * MIB),
    )(w_gate, w_up, w_down, error_in)


def backward_kernel(place_ref, p0_ref, p1_ref, p2_ref, p3_ref, dy_ref, w_hbm,
                    gate_grad_ref, up_grad_ref, hidden_ref, p_out_ref, x_ref, w_ref, hidden_grad_ref, sems):
    rows = p0_ref.shape[0]
    hid, tokens = hidden_ref.shape
    chunk = 256
    loads = [pltpu.make_async_copy(w_hbm.at[k], w_ref.at[k], sems.at[k]) for k in range(6)]
    pieces = []
    for i, ref in enumerate((p0_ref, p1_ref, p2_ref, p3_ref)):
        at = pl.multiple_of(lax.rem(place_ref[0] + i, SIDE) * rows, 16)
        pieces.append(pltpu.make_async_copy(ref, x_ref.at[pl.ds(at, rows), :], sems.at[6 + i]))
    for copy in [loads[2], loads[5]] + pieces + loads[:2] + loads[3:5]:
        copy.start()
    q_dy = dy_ref[:, tokens : tokens + 2 * RANK]
    q_dy_rows = q_dy.astype(F32).T.astype(BF)
    loads[2].wait()
    for start in range(0, tokens, chunk):
        span = slice(start, start + chunk)
        hidden_grad_ref[:, span] = dot(w_ref[2], dy_ref[:, span], 1, 0)
    block = rows // SIDE
    q_plain = q_dy.astype(F32)
    q_plain = jnp.concatenate(
        [q_plain[(x * SIDE + y) * block : (x * SIDE + y + 1) * block] for y in range(SIDE) for x in range(SIDE)]
    ).astype(BF)
    loads[5].wait()
    last_error = dot(w_ref[5], q_plain, 1, 0)
    for copy in pieces + loads[:2]:
        copy.wait()
    q_x = x_ref[:, tokens:]
    q_rows = q_x.astype(F32).T.astype(BF)
    q_both = [q_rows[: 2 * RANK], q_rows[2 * RANK :], q_dy_rows]
    sums = [jnp.zeros((2 * RANK, hid), F32)] * 3
    for start in range(0, tokens, chunk):
        span = slice(start, start + chunk)
        x, dy = x_ref[:, span], dy_ref[:, span]
        gate_pre = dot(w_ref[0], x, 1, 0)
        up_pre = dot(w_ref[1], x, 1, 0)
        hidden_grad = hidden_grad_ref[:, span]
        gate_sig = jax.nn.sigmoid(gate_pre)
        gate_act = gate_pre * gate_sig
        hidden = (gate_act * up_pre).astype(BF)
        gate_grad = (hidden_grad * up_pre * gate_sig * (1.0 + gate_pre - gate_act)).astype(BF)
        up_grad = (hidden_grad * gate_act).astype(BF)
        gate_grad_ref[:, span] = gate_grad
        up_grad_ref[:, span] = up_grad
        hidden_ref[:, span] = hidden
        for k, (left, right) in enumerate(((gate_grad, x), (up_grad, x), (hidden, dy))):
            both = dot(q_both[k], right, 1, 0)
            halves = jnp.concatenate(split(both[:RANK] + both[RANK:]))
            sums[k] = sums[k] + dot(halves, left, 1, 1)
    for copy in loads[3:5]:
        copy.wait()
    errors = [dot(w_ref[3 + k], q_x[:, 2 * k * RANK : 2 * (k + 1) * RANK], 1, 0) for k in range(2)] + [last_error]
    error_p = jnp.concatenate([both[:, :RANK] + both[:, RANK:] for both in errors], axis=1).T
    p = jnp.concatenate([both[:RANK] + both[RANK:] for both in sums]) + error_p
    p_out_ref[...] = p.astype(BF)


def backward(place, pieces, dy_all, weights):
    hid, width = weights.shape[1:]
    wide = dy_all.shape[1]
    tokens = wide - LANES
    vmem = pl.BlockSpec(memory_space=pltpu.VMEM)
    hbm = pl.BlockSpec(memory_space=pltpu.HBM)
    grads = jax.ShapeDtypeStruct((hid, tokens), BF)
    return pl.pallas_call(
        backward_kernel,
        out_shape=(
            grads,
            grads,
            grads,
            jax.ShapeDtypeStruct((ROWS, hid), BF),
            jax.ShapeDtypeStruct((width, wide), BF),
        ),
        in_specs=[pl.BlockSpec(memory_space=pltpu.SMEM)] + [hbm] * SIDE + [vmem, hbm],
        out_specs=(vmem,) * 5,
        scratch_shapes=[
            pltpu.VMEM((6, hid, width), BF),
            pltpu.VMEM((hid, tokens), F32),
            pltpu.SemaphoreType.DMA((6 + SIDE,)),
        ],
        compiler_params=pltpu.CompilerParams(vmem_limit_bytes=20 * MIB),
        cost_estimate=pl.CostEstimate(flops=6 * hid * width * tokens, bytes_accessed=8 * MIB, transcendentals=0),
    )(place, *pieces, dy_all, weights)


def term_kernel(place_ref, w_ref, gate_grad_ref, up_grad_ref, _, t0_ref, t1_ref, t2_ref, t3_ref, token_ref):
    grads = jnp.concatenate([gate_grad_ref[...], up_grad_ref[...]])
    rows = t0_ref.shape[0]
    for i, ref in enumerate((t0_ref, t1_ref, t2_ref, t3_ref)):
        at = pl.multiple_of(lax.rem(place_ref[0] + i, SIDE) * rows, 16)
        ref[...] = dot(w_ref[pl.ds(at, rows), :], grads, 1, 0).astype(BF)
    token_ref[...] = jnp.zeros_like(token_ref)


def terms(place, w_both, gate_grad, up_grad, other):
    vmem = pl.BlockSpec(memory_space=pltpu.VMEM)
    tokens = gate_grad.shape[1]
    width, both = w_both.shape
    out = pl.pallas_call(
        term_kernel,
        out_shape=(jax.ShapeDtypeStruct((width // SIDE, tokens), BF),) * SIDE
        + (jax.ShapeDtypeStruct((8, LANES), F32),),
        in_specs=[pl.BlockSpec(memory_space=pltpu.SMEM)] + [vmem] * 4,
        out_specs=(vmem,) * (SIDE + 1),
        compiler_params=pltpu.CompilerParams(vmem_limit_bytes=20 * MIB),
        cost_estimate=pl.CostEstimate(flops=2 * width * both * tokens, bytes_accessed=4 * MIB, transcendentals=0),
    )(place, w_both, gate_grad, up_grad, other)
    return out[:SIDE], out[SIDE]


def matrices_kernel(gate_grad_ref, up_grad_ref, hidden_ref, x_ref, dy_ref, left_hbm, _,
                    m0_ref, m1_ref, m2_ref, token_ref, left_ref, sems):
    loads = [pltpu.make_async_copy(left_hbm.at[3 + k], left_ref.at[k], sems.at[k]) for k in range(3)]
    for copy in loads:
        copy.start()
    tokens = hidden_ref.shape[1]
    x = x_ref[:, :tokens]
    swapped = dot(hidden_ref[...], dy_ref[:, :tokens], 1, 1)
    block = swapped.shape[1] // (SIDE * SIDE)
    parts = [
        swapped[:, (x * SIDE + y) * block : (x * SIDE + y + 1) * block] for y in range(SIDE) for x in range(SIDE)
    ]
    for copy in loads:
        copy.wait()
    m2_ref[...] = jnp.concatenate(parts, axis=1) + left_ref[2].astype(F32)
    m0_ref[...] = dot(gate_grad_ref[...], x, 1, 1) + left_ref[0].astype(F32)
    m1_ref[...] = dot(up_grad_ref[...], x, 1, 1) + left_ref[1].astype(F32)
    token_ref[...] = jnp.zeros_like(token_ref)


def grad_matrices(grads, x_all, dy_all, weights, other):
    vmem = pl.BlockSpec(memory_space=pltpu.VMEM)
    hid, tokens = grads[0].shape
    width = dy_all.shape[0]
    out = pl.pallas_call(
        matrices_kernel,
        out_shape=(jax.ShapeDtypeStruct((hid, width), F32),) * 3 + (jax.ShapeDtypeStruct((8, LANES), F32),),
        in_specs=[vmem] * 5 + [pl.BlockSpec(memory_space=pltpu.HBM), vmem],
        out_specs=(vmem,) * 4,
        scratch_shapes=[pltpu.VMEM((3, hid, width), BF), pltpu.SemaphoreType.DMA((3,))],
        compiler_params=pltpu.CompilerParams(vmem_limit_bytes=20 * MIB),
        cost_estimate=pl.CostEstimate(flops=6 * hid * width * tokens, bytes_accessed=9 * MIB, transcendentals=0),
    )(*grads, x_all, dy_all, weights, other)
    return out[:3], out[3]


def mean_kernel(value_ref, _, out_ref):
    total = value_ref[0].astype(F32)
    for i in range(1, value_ref.shape[0]):
        total = total + value_ref[i].astype(F32)
    out_ref[...] = total * (0.5 / value_ref.shape[0])


def mean(value, token):
    vmem = pl.BlockSpec(memory_space=pltpu.VMEM)
    return pl.pallas_call(
        mean_kernel,
        out_shape=jax.ShapeDtypeStruct(value.shape[1:], F32),
        in_specs=[vmem, pl.BlockSpec(memory_space=pl.ANY)],
        out_specs=vmem,
        compiler_params=pltpu.CompilerParams(vmem_limit_bytes=20 * MIB),
    )(value, token)


def sketch_kernel(core_ref, p_ref, m0_ref, m1_ref, m2_ref, mine_ref, theirs_ref, gram_ref):
    core = core_ref[0]
    p = p_ref[...]
    rows, grams = [], []
    for k, m_ref in enumerate((m0_ref, m1_ref, m2_ref)):
        p_k = p[k * RANK : (k + 1) * RANK]
        p_high, p_low = split(p_k)
        m_high, m_low = split(m_ref[...])
        both = dot(jnp.concatenate([p_high, p_low]), m_high, 1, 0)
        term = both[:RANK] + both[RANK:] + dot(p_high, m_low, 1, 0)
        grams.append(
            lax.dot_general(
                p_k, p_k, (((1,), (1,)), ((), ())), precision=lax.Precision.HIGHEST, preferred_element_type=F32
            )
        )
        rows.append(jnp.concatenate([term, jnp.zeros((RANK, LANES), F32)], axis=1))
    gram = jnp.concatenate(grams)
    gram_ref[...] = jnp.concatenate([gram[i * 24 : (i + 1) * 24] for i in range(4)], axis=1)
    mine, theirs = own_half(core, jnp.concatenate(rows))
    for i in range(HALF // 8):
        for j in range(8):
            tile = (i * 8 + j) * 8
            rows, cols = slice(i * 8, i * 8 + 8), slice(j * LANES, (j + 1) * LANES)
            mine_ref[tile : tile + 8, :] = mine[rows, cols]
            theirs_ref[tile : tile + 8, :] = theirs[rows, cols]


def sketch(core, p_trans, matrices):
    vmem = pl.BlockSpec(memory_space=pltpu.VMEM)
    out = jax.ShapeDtypeStruct((TILES * 8, LANES), F32)
    return pl.pallas_call(
        sketch_kernel,
        out_shape=(out, out, jax.ShapeDtypeStruct((24, LANES), F32)),
        in_specs=[pl.BlockSpec(memory_space=pltpu.SMEM)] + [vmem] * 4,
        out_specs=(vmem,) * 3,
        compiler_params=pltpu.CompilerParams(vmem_limit_bytes=20 * MIB),
    )(core, p_trans, *matrices)


def ortho_kernel(gram_ref, inverse_ref, token_ref):
    gram = gram_ref[...]
    gram = jnp.concatenate([gram[:, i * RANK : (i + 1) * RANK] for i in range(4)])
    gram = jnp.stack([gram[k * RANK : (k + 1) * RANK] for k in range(3)])
    rows = lax.broadcasted_iota(jnp.int32, (1, RANK, RANK), 1)
    cols = lax.broadcasted_iota(jnp.int32, (1, RANK, RANK), 2)
    eye = jnp.broadcast_to(jnp.where(rows == cols, 1.0, 0.0), gram.shape)
    work = jnp.concatenate([gram, eye], axis=2)
    below = lax.broadcasted_iota(jnp.int32, (1, RANK, 1), 1)
    for k in range(RANK):
        pivot = work[:, k : k + 1, :]
        scale = 1.0 / pivot[:, :, k : k + 1]
        factor = jnp.where(below > k, work[:, :, k : k + 1] * scale, 0.0)
        work = work - factor * pivot
    diag = jnp.sum(jnp.where(rows == cols, work[:, :, :RANK], 0.0), axis=2, keepdims=True)
    inverse = work[:, :, RANK:] * lax.rsqrt(diag)
    inverse_ref[...] = inverse
    token_ref[...] = jnp.zeros_like(token_ref)


def ortho(gram):
    vmem = pl.BlockSpec(memory_space=pltpu.VMEM)
    return pl.pallas_call(
        ortho_kernel,
        out_shape=(
            jax.ShapeDtypeStruct((3, RANK, RANK), F32),
            jax.ShapeDtypeStruct((8, LANES), F32),
        ),
        in_specs=[vmem],
        out_specs=(vmem, vmem),
        cost_estimate=pl.CostEstimate(flops=MIB * 4096, bytes_accessed=MIB, transcendentals=0),
    )(gram)


def finish_kernel(place_ref, s_mine_ref, s_other_ref, inverse_ref, p_ref, m0_ref, m1_ref, m2_ref,
                  error_hbm, q_ref, error_ref, sems):
    m_refs = (m0_ref, m1_ref, m2_ref)
    width = m0_ref.shape[1]

    def rows_of(ref):
        return jnp.concatenate(
            [
                jnp.concatenate([ref[(i * 8 + j) * 8 : (i * 8 + j) * 8 + 8, :] for j in range(7)], axis=1)
                for i in range(HALF // 8)
            ]
        )

    s = whole(place_ref[0], rows_of(s_mine_ref), rows_of(s_other_ref))
    stores, q_rows = [], []
    for k in range(3):
        part = slice(k * RANK, (k + 1) * RANK)
        q_new = dot3(inverse_ref[k], s[part], 1, 0)
        q_rows.append(q_new)
        p_ortho = dot3(inverse_ref[k], p_ref[part, :], 1, 0)
        error_ref[k] = (m_refs[k][...] - dot3(p_ortho, q_new, 0, 0)).astype(BF)
        stores.append(pltpu.make_async_copy(error_ref.at[k], error_hbm.at[0, k], sems.at[k]))
        stores[k].start()
    shard = q_ref.shape[1]
    at = place_ref[1] * shard
    q_ref[...] = pltpu.roll(jnp.concatenate(q_rows), lax.rem(width - at, width), 1)[:, :shard]
    for copy in stores:
        copy.wait()


def finish(place, s_mine, s_other, inverse, p_trans, matrices, shard):
    vmem = pl.BlockSpec(memory_space=pltpu.VMEM)
    hbm = pl.BlockSpec(memory_space=pltpu.HBM)
    hid, width = matrices[0].shape
    return pl.pallas_call(
        finish_kernel,
        out_shape=(jax.ShapeDtypeStruct((1, 3, hid, width), BF), jax.ShapeDtypeStruct((ROWS, shard), F32)),
        in_specs=[pl.BlockSpec(memory_space=pltpu.SMEM)] + [vmem] * 7,
        out_specs=(hbm, vmem),
        scratch_shapes=[
            pltpu.VMEM((3, hid, width), BF),
            pltpu.SemaphoreType.DMA((3,)),
        ],
        compiler_params=pltpu.CompilerParams(vmem_limit_bytes=20 * MIB),
    )(place, s_mine, s_other, inverse, p_trans, *matrices)


def swap_core(value):
    return lax.ppermute(value, "dp", CORE_PAIR)


def dp_swap(bits):
    return [(i, i ^ bits) for i in range(2 * DEPTH)]


def take_kernel(value_ref, _, out_ref):
    out_ref[...] = value_ref[...]


def take(value, token):
    vmem = pl.BlockSpec(memory_space=pltpu.VMEM)
    return pl.pallas_call(
        take_kernel,
        out_shape=jax.ShapeDtypeStruct(value.shape, value.dtype),
        in_specs=[vmem, vmem],
        out_specs=vmem,
        compiler_params=pltpu.CompilerParams(vmem_limit_bytes=20 * MIB),
    )(value, token)


def add(values, token, scale, kind=F32):
    vmem = pl.BlockSpec(memory_space=pltpu.VMEM)

    def kernel(*refs):
        terms = [ref[...].astype(F32) for ref in refs[:-2]]
        while len(terms) > 1:
            terms = [terms[i] + terms[i + 1] for i in range(0, len(terms), 2)]
        refs[-1][...] = (terms[0] * scale).astype(kind)

    return pl.pallas_call(
        kernel,
        out_shape=jax.ShapeDtypeStruct(values[0].shape, kind),
        in_specs=[vmem] * (len(values) + 1),
        out_specs=vmem,
        compiler_params=pltpu.CompilerParams(vmem_limit_bytes=20 * MIB),
    )(*values, token)


def close_kernel(*refs):
    refs[-2][...] = sum(ref[...].astype(F32) for ref in refs[:-2]).astype(BF)
    refs[-1][...] = jnp.zeros_like(refs[-1])


def close(values):
    vmem = pl.BlockSpec(memory_space=pltpu.VMEM)
    return pl.pallas_call(
        close_kernel,
        out_shape=(jax.ShapeDtypeStruct(values[0].shape, BF), jax.ShapeDtypeStruct((8, LANES), F32)),
        in_specs=[vmem] * len(values),
        out_specs=(vmem, vmem),
        compiler_params=pltpu.CompilerParams(vmem_limit_bytes=20 * MIB),
    )(*values)


def per_device(hidden_in, out_grad, w_gate, w_up, w_down, error_in, q_init):
    n_workers = lax.axis_size("dp")
    n_tensor = lax.axis_size("tensor")
    me = lax.axis_index("tensor")
    y, x = me // SIDE, me % SIDE
    core = lax.axis_index("dp") % 2
    shard = hidden_in.shape[1]

    weights, w_both, _ = prepare(w_gate, w_up, w_down, error_in)
    x_part, dy_parts = pack(hidden_in.T, out_grad.T, q_init.reshape(ROWS, shard))
    pieces, dy_all = gather_all(x_part, dy_parts, me)
    spot = jnp.stack([y, core])
    gate_grad, up_grad, hidden, p_part, x_all = backward(spot, pieces, dy_all, weights)
    core = core.reshape(1)
    near = [p_part] + [lax.ppermute(p_part, "dp", dp_swap(bits)) for bits in (1, 2, 3)]
    matrices, token = grad_matrices((gate_grad, up_grad, hidden), x_all, dy_all, weights, p_part)
    p_pair = add(near, token, 1.0, BF)
    blocks, token = terms(spot, w_both, gate_grad, up_grad, p_pair)
    others = [lax.ppermute(p_pair, "dp", dp_swap(bits)) for bits in (4, 12, 10)]
    p_trans = add([p_pair] + others, token, 1.0 / n_workers)
    got = send_blocks(blocks)
    s_mine, s_theirs, gram = sketch(core, p_trans, matrices)
    s_pair = (s_mine + swap_core(s_theirs)).reshape(n_tensor, -1, LANES)
    gram = jnp.broadcast_to(gram[None], (n_tensor,) + gram.shape)
    sums = jnp.sum(lax.all_to_all(jnp.concatenate([s_pair, gram], axis=1), "tensor", 0, 0, tiled=True), axis=0)
    s_part, gram = sums[: s_pair.shape[1]], sums[s_pair.shape[1] :]
    s_all = spread(s_part, "dp", Z_GROUPS, DEPTH)
    inverse, token = ortho(gram)
    s_part = mean(s_all, token)
    got = send_parts(got, x, gram)
    input_grad, token = close(got)
    input_grad = input_grad.T
    s_half = take(spread(s_part, "tensor", None, n_tensor).reshape(-1, LANES), token)
    error_out, q_out = finish(
        jnp.stack([core[0], me]), s_half, swap_core(s_half), inverse, p_trans, matrices, shard
    )
    return (input_grad, error_out, q_out.reshape(q_init.shape))


def solution(mesh):
    in_specs = (
        P("dp", "tensor"),
        P("dp", "tensor"),
        P("tensor", None),
        P("tensor", None),
        P("tensor", None),
        P("dp", None, "tensor", None),
        P(None, None, "tensor"),
    )
    out_specs = (P("dp", "tensor"), P("dp", None, "tensor", None), P(None, None, "tensor"))
    return jax.shard_map(
        per_device, mesh=mesh, in_specs=in_specs, out_specs=out_specs, check_vma=False
    )
```
